32 devices in a mesh: section: 2 (over y), dp: 16 (over z, x, core).
Axes of the slice: x: 2, y: 2, z: 4, core: 2. Of those that a mesh axis runs over, the one named last changes fastest.
Arguments:
- tokens: bfloat16 [4160, 768], P('dp'), may hold values from -6 to 6
- patch_order: int32 [64, 256], P('dp'), may hold values from 0 to 255, each once within a row
- sensor_tag: int32 [64], P('dp'), may hold values from 0 to 7
- class_token: bfloat16 [768], replicated, may hold values from -6 to 6
- sensor_table: bfloat16 [8, 768], replicated, may hold values from -3 to 3
- enc_gain_one: bfloat16 [768], replicated, may hold values from 0.25 to 1.75
- enc_qkv: bfloat16 [768, 2304], P(('section', 'dp')), may hold values from -0.21875 to 0.21875
- enc_out: bfloat16 [768, 768], P(('section', 'dp')), may hold values from -0.875 to 0.875
- enc_gain_two: bfloat16 [768], replicated, may hold values from 0.25 to 1.75
- enc_up: bfloat16 [768, 3072], P(('section', 'dp')), may hold values from -0.21875 to 0.21875
- enc_down: bfloat16 [3072, 768], P(('section', 'dp')), may hold values from -0.109375 to 0.109375
- dec_proj: bfloat16 [768, 512], P(('section', 'dp')), may hold values from -0.21875 to 0.21875
- mask_token: bfloat16 [512], replicated, may hold values from -6 to 6
- dec_gain_one: bfloat16 [512], replicated, may hold values from 0.25 to 1.75
- dec_qkv: bfloat16 [512, 1536], P(('section', 'dp')), may hold values from -0.25 to 0.25
- dec_out: bfloat16 [512, 512], P(('section', 'dp')), may hold values from -1.5 to 1.5
- dec_gain_two: bfloat16 [512], replicated, may hold values from 0.25 to 1.75
- dec_up: bfloat16 [512, 2048], P(('section', 'dp')), may hold values from -0.25 to 0.25
- dec_down: bfloat16 [2048, 512], P(('section', 'dp')), may hold values from -0.125 to 0.125
- out_grad: bfloat16 [16384, 512], P('dp'), may hold values from -6 to 6
Outputs:
- block_out: bfloat16 [16384, 512], P('dp', 'section')
- tokens_grad: float32 [4160, 768], P('dp', 'section')
- enc_qkv_grad: float32 [768, 2304], P(('section', 'dp'))
- enc_out_grad: float32 [768, 768], P(('section', 'dp'))
- enc_up_grad: float32 [768, 3072], P(('section', 'dp'))
- enc_down_grad: float32 [3072, 768], P(('section', 'dp'))
- dec_proj_grad: float32 [768, 512], P(('section', 'dp'))
- dec_qkv_grad: float32 [512, 1536], P(('section', 'dp'))
- dec_out_grad: float32 [512, 512], P(('section', 'dp'))
- dec_up_grad: float32 [512, 2048], P(('section', 'dp'))
- dec_down_grad: float32 [2048, 512], P(('section', 'dp'))
- class_token_grad: float32 [768], replicated
- sensor_table_grad: float32 [8, 768], replicated
- enc_gain_one_grad: float32 [768], replicated
- enc_gain_two_grad: float32 [768], replicated
- mask_token_grad: float32 [512], replicated
- dec_gain_one_grad: float32 [512], replicated
- dec_gain_two_grad: float32 [512], replicated
The draws below stay inside these ranges and needn't reach their ends.
Inputs may be any that keep to these rules, and one draw needn't show every extreme that they name: `patch_order`: each row holds every patch number once; its first 64 entries are the patches of the rows 1 to 64 of that chip in tokens, in order.
All inputs are finite; a program needn't handle non-finite values.
Results may differ from the reference program's by a relative error of at most 0.018.
Values may be sent and summed in bfloat16 or wider, within the bound.
No kernel may reach another device: no remote copies, remote signals or barrier semaphores. Data moves between devices by JAX's collectives and lax.ppermute only.
A program may use at most 448 MiB of HBM per device.

```python
import math
import jax
import jax.numpy as jnp
import numpy as np
from jax import lax

D_E = 768
HEADS_E = 12
MLP_E = 3072
D_D = 512
HEADS_D = 8
MLP_D = 2048
HEAD_DIM = 64
PATCHES = 256
VIS = 64
SENSORS = 8
CHIPS = 64


def with_ends(array, rng, low, high):
    spot = [jax.random.randint(jax.random.fold_in(rng, axis), (), 0, length) for axis, length in enumerate(array.shape)]
    widest = array.shape.index(max(array.shape))
    neighbour = spot[:widest] + [(spot[widest] + 1) % array.shape[widest]] + spot[widest + 1:]
    return array.at[tuple(spot)].set(low).at[tuple(neighbour)].set(high)


def steps_of(own_key, shape, shards, low, top_value):
    level, own = 1.0, jax.random.fold_in(own_key, 6)
    for position, shards_of in shards:
        steps = jnp.exp(jax.random.uniform(jax.random.fold_in(own, position), (shards_of,), jnp.float32, low / len(shards), top_value / len(shards)))
        level = level * jnp.repeat(steps, shape[position] // shards_of).reshape([-1 if axis == position else 1 for axis in range(len(shape))])
    return level


def cumulative_ranks(amount, slope):
    portions = [(1 << 20) // math.isqrt(grade ** slope) + 1 for grade in range(1, amount + 1)]
    scale = 1 + sum(portions) // (1 << 30)
    return np.cumsum(np.array([max(1, weight // scale) for weight in portions]))


def skewed_ids(key, shape, count, slope):
    grid = cumulative_ranks(count, slope)
    lot = jax.random.randint(jax.random.fold_in(key, 1), shape, 0, int(grid[count - 1]))
    grade = jnp.searchsorted(jnp.asarray(grid, jnp.int32), lot, side="right")
    return jax.random.permutation(jax.random.fold_in(key, 2), count)[grade].astype(jnp.int32)


def bell_draw(own_key, extent, deviation, reach, shards=(), held_as=jnp.bfloat16):
    values = deviation * jax.random.normal(own_key, extent, jnp.float32)
    if shards:
        values = values * steps_of(own_key, extent, shards, -0.22, 0.18)
    return jnp.clip(values, -reach, reach).astype(held_as)


def setup_inputs(seed: int = 0) -> dict:
    keys = jax.random.split(jax.random.key(seed), 21)
    return {
        "tokens": bell_draw(keys[0], (CHIPS * (VIS + 1), D_E), 1.0, 6.0, ((0, 16),)),
        "patch_order": jax.vmap(lambda own: jax.random.permutation(own, PATCHES))(jax.random.split(keys[1], CHIPS)).reshape((CHIPS, PATCHES)).astype(jnp.int32),
        "sensor_tag": with_ends(skewed_ids(keys[2], (CHIPS,), SENSORS, 2), jax.random.fold_in(keys[2], 3), 0, SENSORS - 1).astype(jnp.int32),
        "class_token": bell_draw(keys[3], (D_E,), 1.0, 6.0),
        "sensor_table": bell_draw(keys[4], (SENSORS, D_E), 0.5, 3.0),
        "enc_gain_one": jnp.clip(1.0 + 0.15 * jax.random.normal(keys[5], (D_E,), jnp.float32), 0.25, 1.75).astype(jnp.bfloat16),
        "enc_qkv": bell_draw(keys[6], (D_E, 3 * D_E), D_E ** -0.5, 0.21875, ((0, 32),)),
        "enc_out": bell_draw(keys[7], (D_E, D_E), (D_E // 16) ** -0.5, 0.875, ((0, 32),)),
        "enc_gain_two": jnp.clip(1.0 + 0.15 * jax.random.normal(keys[8], (D_E,), jnp.float32), 0.25, 1.75).astype(jnp.bfloat16),
        "enc_up": bell_draw(keys[9], (D_E, MLP_E), D_E ** -0.5, 0.21875, ((0, 32),)),
        "enc_down": bell_draw(keys[10], (MLP_E, D_E), MLP_E ** -0.5, 0.109375, ((0, 32),)),
        "dec_proj": bell_draw(keys[11], (D_E, D_D), D_E ** -0.5, 0.21875, ((0, 32),)),
        "mask_token": bell_draw(keys[12], (D_D,), 1.0, 6.0),
        "dec_gain_one": jnp.clip(1.0 + 0.15 * jax.random.normal(keys[13], (D_D,), jnp.float32), 0.25, 1.75).astype(jnp.bfloat16),
        "dec_qkv": bell_draw(keys[14], (D_D, 3 * D_D), D_D ** -0.5, 0.25, ((0, 32),)),
        "dec_out": bell_draw(keys[15], (D_D, D_D), (D_D // 32) ** -0.5, 1.5, ((0, 32),)),
        "dec_gain_two": jnp.clip(1.0 + 0.15 * jax.random.normal(keys[16], (D_D,), jnp.float32), 0.25, 1.75).astype(jnp.bfloat16),
        "dec_up": bell_draw(keys[17], (D_D, MLP_D), D_D ** -0.5, 0.25, ((0, 32),)),
        "dec_down": bell_draw(keys[18], (MLP_D, D_D), MLP_D ** -0.5, 0.125, ((0, 32),)),
        "out_grad": bell_draw(keys[19], (CHIPS * PATCHES, D_D), 1.0, 6.0, ((0, 16),)),
    }


@jax.custom_vjp
def low(v):
    return lax.optimization_barrier(v.astype(jnp.bfloat16)).astype(jnp.float32)

@jax.custom_vjp
def low_back(v):
    return v

def low_keep(v):
    return (low(v), None)

def low_pass(kept, grad):
    return (grad,)

def back_keep(v):
    return (v, None)

def back_low(kept, grad):
    return (low(grad),)
low.defvjp(low_keep, low_pass)
low_back.defvjp(back_keep, back_low)

def layer_norm(rows, gain):
    mean = lax.optimization_barrier(jnp.mean(rows, axis=-1, keepdims=True))
    centred = rows - mean
    spread = lax.optimization_barrier(jnp.mean(centred * centred, axis=-1, keepdims=True))
    return centred * lax.rsqrt(spread + 1e-05) * gain

def gelu_tanh(value):
    return 0.5 * value * (1.0 + jnp.tanh(0.7978845608028654 * (value + 0.044715 * value * value * value)))

def product(left, right):
    return jnp.einsum('gld,de->gle', left, right, precision=lax.Precision.HIGHEST)

def position_table():
    half = D_D // 2
    place = jnp.arange(PATCHES, dtype=jnp.float32)[:, None]
    rate = jnp.exp(jnp.arange(half, dtype=jnp.float32) * (-math.log(10000.0) / half))
    angle = place * rate[None, :]
    return jnp.concatenate([jnp.sin(angle), jnp.cos(angle)], axis=1)

def block(rows, weights, heads):
    gain_one, w_triple, w_mixing, gain_two, w_expand, w_reduce = weights
    groups, length, width = rows.shape
    normed = low(layer_norm(rows, gain_one))
    triple = low(low_back(product(normed, w_triple)))
    parts = triple.reshape(groups, length, 3, heads, HEAD_DIM)
    scores = jnp.einsum('gqhe,gkhe->ghqk', parts[:, :, 0], parts[:, :, 1], precision=lax.Precision.HIGHEST) * HEAD_DIM ** (-0.5)
    scores = low_back(scores)
    top = lax.optimization_barrier(jnp.max(scores, axis=-1, keepdims=True))
    raised = jnp.exp(scores - top)
    shares = low(raised / lax.optimization_barrier(jnp.sum(raised, axis=-1, keepdims=True)))
    mixed = jnp.einsum('ghqk,gkhe->gqhe', shares, parts[:, :, 2], precision=lax.Precision.HIGHEST)
    mixed = low(low_back(mixed.reshape(groups, length, width)))
    rows = rows + low_back(product(mixed, w_mixing))
    normed = low(layer_norm(rows, gain_two))
    hidden = low(gelu_tanh(low_back(product(normed, w_expand))))
    return rows + low_back(product(hidden, w_reduce))

def chip_group(pack, params):
    tokens, order, tags = pack
    class_token, sensor_table, enc_weights, dec_proj, mask_token, dec_weights = params
    chips = tags.shape[0]
    onehot = (tags[:, None] == jnp.arange(SENSORS, dtype=jnp.int32)[None, :]).astype(jnp.float32)
    sensor_rows = jnp.dot(onehot, sensor_table, precision=lax.Precision.HIGHEST)
    lead = jnp.broadcast_to(class_token[None, None, :], (chips, 1, D_E))
    sequence = jnp.concatenate([lead, tokens], axis=1) + sensor_rows[:, None, :]
    encoded = block(sequence, enc_weights, HEADS_E)
    visible = low(low_back(encoded[:, 2:, :]))
    projected = low_back(product(visible, dec_proj))
    places = jnp.arange(PATCHES, dtype=jnp.int32)
    rank = lax.optimization_barrier(jnp.sum(jnp.where(order[:, :, None] == places[None, None, :], places[None, :, None], 0), axis=1)).astype(jnp.int32)
    picked = jnp.take_along_axis(projected, jnp.minimum(rank, VIS - 1)[:, :, None], axis=1)
    decoder_in = jnp.where((rank < VIS)[:, :, None], picked, mask_token[None, None, :]) + position_table()[None, :, :]
    return block(decoder_in, dec_weights, HEADS_D)

def reference(tokens, patch_order, sensor_tag, class_token, sensor_table, enc_gain_one, enc_qkv, enc_out, enc_gain_two, enc_up, enc_down, dec_proj, mask_token, dec_gain_one, dec_qkv, dec_out, dec_gain_two, dec_up, dec_down, out_grad):

    def wide(value):
        return value.astype(jnp.float32)
    enc_weights = (wide(enc_gain_one), wide(enc_qkv), wide(enc_out), wide(enc_gain_two), wide(enc_up), wide(enc_down))
    dec_weights = (wide(dec_gain_one), wide(dec_qkv), wide(dec_out), wide(dec_gain_two), wide(dec_up), wide(dec_down))
    params = (wide(class_token), wide(sensor_table), enc_weights, wide(dec_proj), wide(mask_token), dec_weights)
    group = max(1, 4096 // PATCHES)
    while CHIPS % group != 0:
        group = group - 1
    count = CHIPS // group
    order = patch_order.reshape(count, group, PATCHES)
    tags = sensor_tag.reshape(count, group)
    step = jax.checkpoint(chip_group)

    def forward(token_rows, weights):
        packed = token_rows.reshape(count, group, VIS + 1, D_E)
        result = lax.map(lambda pack: step(pack, weights), (packed, order, tags))
        return result.reshape(CHIPS * PATCHES, D_D)
    decoded, pullback = jax.vjp(forward, wide(tokens), params)
    tokens_grad, grads = pullback(wide(out_grad))
    class_grad, sensor_grad, enc_grads, proj_grad, mask_grad, dec_grads = grads
    return (decoded.astype(jnp.bfloat16), tokens_grad, enc_grads[1], enc_grads[2], enc_grads[4], enc_grads[5], proj_grad, dec_grads[1], dec_grads[2], dec_grads[4], dec_grads[5], class_grad, sensor_grad, enc_grads[0], enc_grads[3], mask_grad, dec_grads[0], dec_grads[3])
```

```python
import math

import jax
import jax.numpy as jnp
from jax import lax
from jax.sharding import PartitionSpec as P

HEADS_E = 12
HEADS_D = 8
HEAD_DIM = 64
BF = jnp.bfloat16
F32 = jnp.float32


def matmul(left, right):
    return jnp.dot(left, right, preferred_element_type=F32)


def against_rows(left, right):
    return lax.dot_general(left, right, (((1,), (1,)), ((), ())), preferred_element_type=F32)


def over_rows(left, right):
    return lax.dot_general(left, right, (((0,), (0,)), ((), ())), preferred_element_type=F32)


def layer_norm(rows, gain):
    mean = jnp.mean(rows, axis=-1, keepdims=True)
    centred = rows - mean
    spread = jnp.mean(centred * centred, axis=-1, keepdims=True)
    return centred * lax.rsqrt(spread + 1e-05) * gain


def gelu_tanh(value):
    return (
        0.5
        * value
        * (1.0 + jnp.tanh(0.7978845608028654 * (value + 0.044715 * value * value * value)))
    )


def position_table(count, width):
    half = width // 2
    place = jnp.arange(count, dtype=F32)[:, None]
    rate = jnp.exp(jnp.arange(half, dtype=F32) * (-math.log(10000.0) / half))
    angle = place * rate[None, :]
    return jnp.concatenate([jnp.sin(angle), jnp.cos(angle)], axis=1)


def attend(triple, chips, heads):
    rows = triple.shape[0]
    width = triple.shape[1] // 3
    length = rows // chips
    parts = triple.reshape(chips, length, 3, heads, HEAD_DIM)
    scores = jnp.einsum(
        "cqhe,ckhe->chqk", parts[:, :, 0], parts[:, :, 1], preferred_element_type=F32
    ) * HEAD_DIM ** (-0.5)
    top = jnp.max(scores, axis=-1, keepdims=True)
    raised = jnp.exp(scores - top)
    exact = raised / jnp.sum(raised, axis=-1, keepdims=True)
    shares = exact.astype(BF)
    mixed = jnp.einsum("chqk,ckhe->cqhe", shares, parts[:, :, 2], preferred_element_type=F32)
    return mixed.astype(BF).reshape(rows, width), exact


def attend_back(triple, exact, grad_mixed, chips, heads):
    rows = triple.shape[0]
    width = triple.shape[1] // 3
    length = rows // chips
    parts = triple.reshape(chips, length, 3, heads, HEAD_DIM)
    query, key, value = parts[:, :, 0], parts[:, :, 1], parts[:, :, 2]
    scale = HEAD_DIM ** (-0.5)
    grad_heads = grad_mixed.reshape(chips, length, heads, HEAD_DIM)
    grad_value = jnp.einsum(
        "chqk,cqhe->ckhe", exact.astype(BF), grad_heads, preferred_element_type=F32
    )
    grad_shares = jnp.einsum("cqhe,ckhe->chqk", grad_heads, value, preferred_element_type=F32)
    grad_scores = (
        exact * (grad_shares - jnp.sum(grad_shares * exact, axis=-1, keepdims=True))
    ).astype(BF)
    grad_query = (
        jnp.einsum("chqk,ckhe->cqhe", grad_scores, key, preferred_element_type=F32) * scale
    )
    grad_key = (
        jnp.einsum("chqk,cqhe->ckhe", grad_scores, query, preferred_element_type=F32) * scale
    )
    grad_triple = jnp.stack([grad_query, grad_key, grad_value], axis=2)
    return grad_triple.astype(BF).reshape(rows, 3 * width)


def block_forward(rows, weights, chips, heads):
    gain_one, w_triple, w_mixing, gain_two, w_expand, w_reduce = weights
    normed_one = layer_norm(rows, gain_one).astype(BF)
    triple = matmul(normed_one, w_triple).astype(BF)
    mixed, exact = attend(triple, chips, heads)
    middle = rows + matmul(mixed, w_mixing)
    normed_two = layer_norm(middle, gain_two).astype(BF)
    expanded = matmul(normed_two, w_expand)
    hidden = gelu_tanh(expanded).astype(BF)
    result = middle + matmul(hidden, w_reduce)
    return result, (rows, normed_one, triple, mixed, exact, middle, normed_two, expanded, hidden)


def block_back(kept, grad_out, weights, chips, heads):
    rows, normed_one, triple, mixed, exact, middle, normed_two, expanded, hidden = kept
    gain_one, w_triple, w_mixing, gain_two, w_expand, w_reduce = weights
    grad_branch = grad_out.astype(BF)
    grad_reduce = over_rows(hidden, grad_branch)
    grad_hidden = against_rows(grad_branch, w_reduce)
    _, gelu_back = jax.vjp(gelu_tanh, expanded)
    grad_expanded = gelu_back(grad_hidden)[0].astype(BF)
    grad_expand = over_rows(normed_two, grad_expanded)
    grad_normed = against_rows(grad_expanded, w_expand)
    _, norm_back = jax.vjp(layer_norm, middle, gain_two)
    grad_part, grad_gain_two = norm_back(grad_normed)
    grad_middle = grad_out + grad_part
    grad_branch = grad_middle.astype(BF)
    grad_mixing = over_rows(mixed, grad_branch)
    grad_mixed = against_rows(grad_branch, w_mixing).astype(BF)
    grad_triple = attend_back(triple, exact, grad_mixed, chips, heads)
    grad_weights = over_rows(normed_one, grad_triple)
    grad_normed = against_rows(grad_triple, w_triple)
    _, norm_back = jax.vjp(layer_norm, rows, gain_one)
    grad_part, grad_gain_one = norm_back(grad_normed)
    return (
        grad_middle + grad_part,
        (grad_weights, grad_mixing, grad_expand, grad_reduce),
        (grad_gain_one, grad_gain_two),
    )


class Cube:
    def __init__(self):
        self.dims = {}
        self.names = []
        for axis in ("section", "dp"):
            bits = (lax.axis_size(axis) - 1).bit_length()
            for bit in reversed(range(bits)):
                name = (axis, bit)
                self.names.append(name)
                self.dims[name] = (lax.axis_index(axis) >> bit) & 1
        z = [("dp", bit) for bit in range(2, len(self.names) - 1)]
        first, second, core = ("dp", 1), ("section", 0), ("dp", 0)
        self.orders = (z + [first, second, core], z + [second, first, core])

    def swap(self, value, name):
        axis, bit = name
        route = [(i, i ^ (1 << bit)) for i in range(lax.axis_size(axis))]
        return lax.ppermute(value, axis, route)

    def gather(self, piece, order):
        held = []
        value = piece
        lead = 0
        for name in order:
            got = self.swap(value, name)
            place = sum(1 for other in held if self.names.index(other) < self.names.index(name))
            mine = self.dims[name] == 0
            value = jnp.where(
                mine, jnp.stack([value, got], place), jnp.stack([got, value], place)
            )
            held.append(name)
            lead += 1
        return value.reshape((1 << lead,) + piece.shape)

    def scatter(self, value, order):
        held = list(self.names)
        tail = value.shape[1:]
        value = value.reshape((2,) * len(held) + tail)
        for name in reversed(order):
            place = held.index(name)
            mine = self.dims[name]
            away = lax.dynamic_index_in_dim(value, 1 - mine, place, keepdims=False)
            here = lax.dynamic_index_in_dim(value, mine, place, keepdims=False)
            got = self.swap(away, name)
            total = here.astype(F32) + got.astype(F32)
            held.remove(name)
            value = total.astype(BF) if held else total
        return value


def stacked(shard, width):
    return jnp.concatenate(
        [shard[:, i : i + width] for i in range(0, shard.shape[1], width)], axis=0
    )


def pack(shards, width):
    return jnp.concatenate([stacked(shard, width) for shard in shards], axis=0)


def unpack(full, shards, width):
    out = []
    at = 0
    for rows, columns in shards:
        parts = columns // width
        blocks = [full[:, at + i * rows : at + (i + 1) * rows] for i in range(parts)]
        at += parts * rows
        whole = blocks[0] if parts == 1 else jnp.concatenate(blocks, axis=2)
        out.append(whole.reshape(full.shape[0] * rows, columns))
    return out


def pack_whole(grads, shards, width, devices):
    blocks = []
    for grad, (rows, columns) in zip(grads, shards):
        split = grad.astype(BF).reshape(devices, rows, columns)
        blocks += [split[:, :, i : i + width] for i in range(0, columns, width)]
    return jnp.concatenate(blocks, axis=1)


def unpack_shard(piece, shards, width):
    out = []
    at = 0
    for rows, columns in shards:
        blocks = []
        for _ in range(columns // width):
            blocks.append(piece[at : at + rows])
            at += rows
        out.append(blocks[0] if len(blocks) == 1 else jnp.concatenate(blocks, axis=1))
    return out


def local(
    tokens,
    patch_order,
    sensor_tag,
    class_token,
    sensor_table,
    enc_gain_one,
    enc_qkv,
    enc_out,
    enc_gain_two,
    enc_up,
    enc_down,
    dec_proj,
    mask_token,
    dec_gain_one,
    dec_qkv,
    dec_out,
    dec_gain_two,
    dec_up,
    dec_down,
    out_grad,
):
    cube = Cube()
    devices = lax.axis_size("section") * lax.axis_size("dp")
    section = lax.axis_index("section")
    sections = lax.axis_size("section")
    width_enc = tokens.shape[1]
    width_dec = out_grad.shape[1]
    groups = (
        ((enc_qkv, enc_out), width_enc, 0),
        ((enc_up,), width_enc, 1),
        ((enc_down,), width_enc, 0),
        ((dec_proj, dec_qkv, dec_out), width_dec, 1),
        ((dec_up, dec_down), width_dec, 0),
    )
    shapes = [[shard.shape for shard in group] for group, _, _ in groups]
    full = []
    for (group, width, way), shape in zip(groups, shapes):
        whole = cube.gather(pack(group, width), cube.orders[way])
        full += unpack(whole, shape, width)
    enc_weights = (
        enc_gain_one.astype(F32),
        full[0],
        full[1],
        enc_gain_two.astype(F32),
        full[2],
        full[3],
    )
    projection = full[4]
    dec_weights = (
        dec_gain_one.astype(F32),
        full[5],
        full[6],
        dec_gain_two.astype(F32),
        full[7],
        full[8],
    )
    chips_all = patch_order.shape[0]
    chips = chips_all // sections
    seq_in = tokens.shape[0] // chips_all
    seq_out = patch_order.shape[1]
    visible_count = seq_in - 1
    sensor_count = sensor_table.shape[0]

    def mine(whole):
        rows = whole.shape[0] // sections
        return lax.dynamic_slice_in_dim(whole, section * rows, rows, axis=0)

    tok_rows, tags, order, grad_rows = (
        mine(tokens),
        mine(sensor_tag),
        mine(patch_order),
        mine(out_grad),
    )
    table = position_table(seq_out, width_dec)
    places = jnp.arange(seq_out, dtype=jnp.int32)
    onehot = tags[:, None] == jnp.arange(sensor_count, dtype=jnp.int32)[None, :]
    sensor_rows = matmul(onehot.astype(BF), sensor_table)
    lead = jnp.broadcast_to(class_token.astype(F32)[None, None, :], (chips, 1, width_enc))
    sequence = (
        jnp.concatenate([lead, tok_rows.astype(F32).reshape(chips, seq_in, width_enc)], axis=1)
        + sensor_rows[:, None, :]
    ).reshape(chips * (seq_in + 1), width_enc)

    encoded, enc_kept = block_forward(sequence, enc_weights, chips, HEADS_E)
    visible = encoded.reshape(chips, seq_in + 1, width_enc)[:, 2:].astype(BF)

    projected = matmul(visible.reshape(-1, width_enc), projection).reshape(
        chips, visible_count, width_dec
    )
    chosen = places[None, :, None] == order[:, None, :visible_count]
    seen = jnp.any(chosen, axis=2)[:, :, None]
    high = projected.astype(BF)
    low = (projected - high.astype(F32)).astype(BF)
    picked = jnp.einsum(
        "cpj,cjd->cpd",
        jnp.concatenate([chosen, chosen], axis=2).astype(BF),
        jnp.concatenate([high, low], axis=1),
        preferred_element_type=F32,
    )
    decoder_in = (
        jnp.where(seen, picked, mask_token.astype(F32)[None, None, :]) + table[None, :, :]
    )
    decoded, dec_kept = block_forward(
        decoder_in.reshape(-1, width_dec), dec_weights, chips, HEADS_D
    )
    grad_in, dec_matrices, dec_gains = block_back(
        dec_kept, grad_rows.astype(F32), dec_weights, chips, HEADS_D
    )
    grad_chip = grad_in.reshape(chips, seq_out, width_dec)
    mask_grad = jnp.sum(jnp.where(seen, 0.0, grad_chip), axis=(0, 1))
    grad_projected = (
        jnp.einsum(
            "cpj,cpd->cjd", chosen.astype(BF), grad_chip.astype(BF), preferred_element_type=F32
        )
        .astype(BF)
        .reshape(chips * visible_count, width_dec)
    )
    proj_grad = over_rows(visible.reshape(-1, width_enc), grad_projected)
    grad_visible = against_rows(grad_projected, projection).astype(BF)

    grad_encoded = jnp.pad(
        grad_visible.astype(F32).reshape(chips, visible_count, width_enc),
        ((0, 0), (2, 0), (0, 0)),
    )
    grad_sequence, enc_matrices, enc_gains = block_back(
        enc_kept, grad_encoded.reshape(-1, width_enc), enc_weights, chips, HEADS_E
    )
    grad_seq = grad_sequence.reshape(chips, seq_in + 1, width_enc)
    sensor_grad = jnp.sum(
        jnp.where(onehot[:, :, None], jnp.sum(grad_seq, axis=1)[:, None, :], 0.0), axis=0
    )
    class_grad = jnp.sum(grad_seq[:, 0], axis=0)
    token_rows = grad_seq[:, 1:].reshape(chips * seq_in, width_enc)

    grads = (
        (enc_matrices[0], enc_matrices[1]),
        (enc_matrices[2],),
        (enc_matrices[3],),
        (proj_grad, dec_matrices[0], dec_matrices[1]),
        (dec_matrices[2], dec_matrices[3]),
    )
    sums = [None] * len(groups)
    for index in (4, 3, 2, 1, 0):
        _, width, way = groups[index]
        whole = pack_whole(grads[index], shapes[index], width, devices)
        piece = cube.scatter(whole, cube.orders[way])
        sums[index] = unpack_shard(piece, shapes[index], width)
    big = [value for group in sums for value in group]

    small = lax.psum(
        (class_grad, sensor_grad) + enc_gains + (mask_grad,) + dec_gains, ("section", "dp")
    )

    def halves(rows):
        half = rows.shape[1] // sections
        own = lax.dynamic_slice_in_dim(rows, section * half, half, axis=1)
        away = lax.dynamic_slice_in_dim(rows, (1 - section) * half, half, axis=1)
        got = cube.swap(away.astype(BF), ("section", 0)).astype(rows.dtype)
        return jnp.where(
            section == 0, jnp.concatenate([own, got], 0), jnp.concatenate([got, own], 0)
        )

    return (halves(decoded.astype(BF)), halves(token_rows)) + tuple(big) + tuple(small)


def solution(mesh):
    every = P(("section", "dp"), None)
    rows = P("dp", None)
    in_specs = (
        rows,
        rows,
        P("dp"),
        P(),
        P(),
        P(),
        every,
        every,
        P(),
        every,
        every,
        every,
        P(),
        P(),
        every,
        every,
        P(),
        every,
        every,
        rows,
    )
    out_specs = (P("dp", "section"),) * 2 + (every,) * 9 + (P(),) * 7
    return jax.shard_map(local, mesh=mesh, in_specs=in_specs, out_specs=out_specs, check_vma=False)
```

```python
import math

import jax
import jax.numpy as jnp
from jax import lax
from jax.experimental import pallas as pl
from jax.experimental.pallas import tpu as pltpu
from jax.sharding import PartitionSpec as P

HEAD_DIM = 64
PAIR = 2 * HEAD_DIM
BF = jnp.bfloat16
F32 = jnp.float32
SCALE = HEAD_DIM ** (-0.5)


def matmul(left, right):
    return jnp.dot(left, right, preferred_element_type=F32)


def against_rows(left, right):
    return lax.dot_general(left, right, (((1,), (1,)), ((), ())), preferred_element_type=F32)


def over_rows(left, right):
    return lax.dot_general(left, right, (((0,), (0,)), ((), ())), preferred_element_type=F32)


def normal_parts(rows):
    mean = jnp.mean(rows, axis=-1, keepdims=True)
    centred = rows - mean
    spread = jnp.mean(centred * centred, axis=-1, keepdims=True)
    inverse = lax.rsqrt(spread + 1e-05)
    return centred * inverse, inverse


def layer_norm(rows, gain):
    return (normal_parts(rows)[0] * gain).astype(BF)


def norm_back(rows, gain, grad):
    hat, inverse = normal_parts(rows)
    scaled = grad * gain
    out = inverse * (
        scaled
        - jnp.mean(scaled, axis=-1, keepdims=True)
        - hat * jnp.mean(scaled * hat, axis=-1, keepdims=True)
    )
    return out, jnp.sum(grad * hat, axis=0, keepdims=True)


def gelu_parts(value):
    square = value * value
    flat = jnp.tanh(0.7978845608028654 * (value + 0.044715 * value * square))
    side = 0.5 * (1.0 + flat)
    slope = side + 0.5 * value * (1.0 - flat * flat) * (
        0.7978845608028654 + 3.0 * 0.044715 * 0.7978845608028654 * square
    )
    return value * side, slope


def position_table(count, width):
    half = width // 2
    place = jnp.arange(count, dtype=F32)[:, None]
    rate = jnp.exp(jnp.arange(half, dtype=F32) * (-math.log(10000.0) / half))
    angle = place * rate[None, :]
    return jnp.concatenate([jnp.sin(angle), jnp.cos(angle)], axis=1)


def shares_of(key, query, bias):
    scores = against_rows(key, query) * SCALE
    if bias is not None:
        scores = scores + bias
    raised = jnp.exp(scores - jnp.max(scores, axis=0, keepdims=True))
    return raised / jnp.sum(raised, axis=0, keepdims=True)


def one_head(value, head):
    lane = lax.broadcasted_iota(jnp.int32, value.shape, 1)
    own = lane < HEAD_DIM if head == 0 else lane >= HEAD_DIM
    return jnp.where(own, value, jnp.zeros_like(value))


def two_heads(values):
    lane = lax.broadcasted_iota(jnp.int32, values[0].shape, 1)
    return jnp.where(lane < HEAD_DIM, values[0], values[1])


def bias_of(length, seq, valid):
    if length == valid:
        return None
    key = lax.broadcasted_iota(jnp.int32, (length, length), 0)
    query = lax.broadcasted_iota(jnp.int32, (length, length), 1)
    kept = jnp.zeros((length, length), jnp.bool_)
    for start in range(0, length, seq):
        kept = kept | (
            (key >= start) & (key < start + valid) & (query >= start) & (query < start + seq)
        )
    return jnp.where(kept, 0.0, -1e30)


def attend(triple, width, bias):
    out = []
    for at in range(0, width, PAIR):
        query, key, value = (triple[:, i * width + at : i * width + at + PAIR] for i in range(3))
        mixed = []
        for head in range(2):
            shares = shares_of(key, one_head(query, head), bias).astype(BF)
            mixed.append(over_rows(shares, value))
        out.append(two_heads(mixed).astype(BF))
    return jnp.concatenate(out, axis=1)


def attend_back(triple, grad_mixed, width, bias):
    out = ([], [], [])
    for at in range(0, width, PAIR):
        query, key, value = (triple[:, i * width + at : i * width + at + PAIR] for i in range(3))
        grad = grad_mixed[:, at : at + PAIR]
        parts = ([], [], [])
        for head in range(2):
            exact = shares_of(key, one_head(query, head), bias)
            grad_shares = against_rows(value, one_head(grad, head))
            parts[2].append(matmul(exact.astype(BF), grad))
            mean = jnp.sum(grad_shares * exact, axis=0, keepdims=True)
            grad_scores = (exact * (grad_shares - mean)).astype(BF)
            parts[0].append(over_rows(grad_scores, key) * SCALE)
            parts[1].append(matmul(grad_scores, query) * SCALE)
        for i in range(3):
            out[i].append(two_heads(parts[i]).astype(BF))
    return [jnp.concatenate(piece, axis=1) for piece in out]


def call(body, name, args, *outs):
    return pl.pallas_call(
        body,
        out_shape=[jax.ShapeDtypeStruct(shape, dtype) for shape, dtype in outs],
        cost_estimate=pl.CostEstimate(flops=1000, bytes_accessed=1000, transcendentals=0),
        compiler_params=pltpu.CompilerParams(vmem_limit_bytes=40 << 20),
        name=name,
    )(*args)


def after(value, *others):
    return lax.optimization_barrier((value,) + others)[0]


class Cube:
    def __init__(self):
        self.dims = {}
        self.names = []
        for axis in ("section", "dp"):
            bits = (lax.axis_size(axis) - 1).bit_length()
            for bit in reversed(range(bits)):
                name = (axis, bit)
                self.names.append(name)
                self.dims[name] = (lax.axis_index(axis) >> bit) & 1
        self.z = [("dp", bit) for bit in range(2, len(self.names) - 1)]
        self.x, self.y, self.core = ("dp", 1), ("section", 0), ("dp", 0)
        self.within = self.z + [self.x, self.core]
        self.over = self.z + [self.x, self.y, self.core]

    def swap(self, value, name):
        axis, bit = name
        route = [(i, i ^ (1 << bit)) for i in range(lax.axis_size(axis))]
        return lax.ppermute(value, axis, route)

    def both(self, own, got, name, place):
        mine = self.dims[name] == 0
        return jnp.where(mine, jnp.stack([own, got], place), jnp.stack([got, own], place))


class Gather:
    def __init__(self, cube, piece, order):
        self.cube, self.order = cube, list(order)
        self.value, self.lead, self.tail = piece, piece.shape[:-2], piece.shape[-2:]
        self.held, self.got = [], None

    def start(self, *others):
        name = self.order[len(self.held)]
        value = after(self.value, *others) if others else self.value
        self.got = self.cube.swap(value, name)
        return self

    def finish(self, *others):
        got = after(self.got, *others) if others else self.got
        name = self.order[len(self.held)]
        names = self.cube.names
        place = sum(1 for other in self.held if names.index(other) < names.index(name))
        self.value = self.cube.both(self.value, got, name, len(self.lead) + place)
        self.held.append(name)
        return self.value

    def whole(self):
        return self.value.reshape(self.lead + (-1, self.tail[-1]))


class Scatter:
    def __init__(self, cube, value, lead, rows, order):
        self.cube, self.order = cube, list(order)
        self.held = [name for name in cube.names if name in order]
        self.lead = len(lead)
        self.value = value.reshape(lead + (2,) * len(self.held) + (rows, value.shape[-1]))
        self.here = self.got = None

    def start(self, *others):
        name = self.order[0]
        place = self.lead + self.held.index(name)
        mine = self.cube.dims[name]
        away = lax.dynamic_index_in_dim(self.value, 1 - mine, place, keepdims=False)
        self.here = lax.dynamic_index_in_dim(self.value, mine, place, keepdims=False)
        if others:
            away = after(away, *others)
        self.got = self.cube.swap(away, name)
        return self

    def finish(self, *others):
        got = after(self.got, *others) if others else self.got
        name = self.order.pop(0)
        self.held.remove(name)
        total = self.here.astype(F32) + got.astype(F32)
        self.value = total.astype(BF) if self.order else total
        return self.value


def blocks_of(shard, width):
    return [shard[..., i : i + width] for i in range(0, shard.shape[-1], width)]


def local(
    tokens,
    patch_order,
    sensor_tag,
    class_token,
    sensor_table,
    enc_gain_one,
    enc_qkv,
    enc_out,
    enc_gain_two,
    enc_up,
    enc_down,
    dec_proj,
    mask_token,
    dec_gain_one,
    dec_qkv,
    dec_out,
    dec_gain_two,
    dec_up,
    dec_down,
    out_grad,
):
    cube = Cube()
    section = lax.axis_index("section")
    sections = lax.axis_size("section")
    group = lax.axis_size("dp")
    devices = sections * group
    wide = tokens.shape[1]
    thin = out_grad.shape[1]
    half = wide // sections
    mlp = enc_up.shape[1] // sections
    ups = mlp // half
    rows_e, rows_m = enc_qkv.shape[0], enc_down.shape[0]
    rows_p, rows_d, rows_n = dec_proj.shape[0], dec_qkv.shape[0], dec_down.shape[0]
    mlp_d = dec_up.shape[1]
    v_ups = mlp_d // thin
    chips_all = patch_order.shape[0]
    chips = chips_all // sections
    seq_in = tokens.shape[0] // chips_all
    seq_out = patch_order.shape[1]
    visible_count = seq_in - 1
    sensor_count = sensor_table.shape[0]
    length = -(-(seq_in + 1) // 8) * 8
    own = chips * length
    every = sections * own
    rows_all = chips * seq_out
    y = cube.y

    def part(value, which, axis):
        size = value.shape[axis] // sections
        return lax.dynamic_slice_in_dim(value, which * size, size, axis=axis)

    qkv_cut = enc_qkv.reshape(rows_e, 3, sections, half)
    qkv_mine = lax.dynamic_index_in_dim(qkv_cut, section, 2, keepdims=False)
    qkv_away = lax.dynamic_index_in_dim(qkv_cut, 1 - section, 2, keepdims=False)
    up_mine, up_away = part(enc_up, section, 1), part(enc_up, 1 - section, 1)
    away = jnp.stack([qkv_away[:, i] for i in range(3)] + blocks_of(up_away, half))
    mine = jnp.stack([qkv_mine[:, i] for i in range(3)] + blocks_of(up_mine, half))
    piece_three = jnp.stack(blocks_of(enc_down, half))
    piece_four = jnp.concatenate([dec_proj] + blocks_of(dec_qkv, thin) + [dec_out], axis=0)
    piece_five = jnp.stack(
        blocks_of(dec_up, thin) + [dec_down[i : i + rows_d] for i in range(0, rows_n, rows_d)]
    )
    d_two = Gather(cube, piece_five, cube.over).start()
    columns = cube.both(mine, cube.swap(away, y), y, 1)
    e_one = Gather(
        cube,
        jnp.concatenate([columns[:3], jnp.stack(blocks_of(enc_out, half))[None]], axis=0),
        cube.within,
    )
    e_two = Gather(cube, columns[3:], cube.within)
    e_three = Gather(cube, piece_three, cube.within)
    d_one = Gather(cube, piece_four, cube.over)

    chain = [d_two, e_one, d_one, e_two, e_three]
    flow = {name: [] for name in cube.names}
    for chunk in chain:
        for step, name in enumerate(chunk.order):
            if name == cube.core:
                continue
            if not (chunk is d_two and step == 0):
                earlier = flow[name]
                window = 2 if name == cube.z[0] else 1
                chunk.start(*([earlier[-window]] if len(earlier) >= window else []))
            chunk.finish()
            flow[name].append(chunk.got)
    for chunk in chain:
        chunk.start()
        chunk.finish()
    w_one, w_two, w_three, v_five = (
        e_one.whole().reshape(4, wide, half),
        e_two.whole().reshape(ups, wide, half),
        e_three.whole(),
        d_two.whole(),
    )
    v_four = d_one.whole().reshape(devices, -1, thin)
    w_proj = v_four[:, :rows_p].reshape(wide, thin)
    v_one = (
        v_four[:, rows_p:].reshape(devices, 4, rows_d, thin).transpose(1, 0, 2, 3)
    ).reshape(4, thin, thin)
    v_up = v_five[:v_ups]
    v_down = (
        v_five[v_ups:].reshape(-1, devices, rows_d, thin).transpose(1, 0, 2, 3)
    ).reshape(v_ups, thin, thin)

    gains = [
        gain.astype(F32)[None, :]
        for gain in (enc_gain_one, enc_gain_two, dec_gain_one, dec_gain_two)
    ]

    def mine_first(value):
        return jnp.concatenate([part(value, section, 0), part(value, 1 - section, 0)], axis=0)

    tags = mine_first(sensor_tag)
    onehot = tags[:, None] == jnp.arange(sensor_count, dtype=jnp.int32)[None, :]
    sensor_rows = matmul(onehot.astype(BF), sensor_table)
    chip_tokens = mine_first(tokens.reshape(chips_all, seq_in, wide)).astype(F32)
    lead = jnp.broadcast_to(class_token.astype(F32)[None, None, :], (chips_all, 1, wide))
    filled = (
        jnp.concatenate([chip_tokens[:, 1:], chip_tokens[:, :1], lead], axis=1)
        + sensor_rows[:, None, :]
    )
    sequence = jnp.pad(filled, ((0, 0), (0, length - seq_in - 1), (0, 0))).reshape(every, wide)
    table = position_table(seq_out, thin)
    order = part(patch_order, section, 0)[:, :visible_count]
    grad_rows = part(out_grad, section, 0)
    mask_row = mask_token.astype(F32)[None, :]

    def enc_attend(seq, gain, w, normed_out, triple_out, mixed_out, part_out, away_out):
        normed = layer_norm(seq[...], gain[...])
        normed_out[...] = normed
        for i in range(3):
            triple_out[:, i * half : (i + 1) * half] = matmul(normed, w[i]).astype(BF)
        bias = bias_of(own, length, seq_in + 1)
        triple = triple_out[...]
        mixed = jnp.concatenate(
            [attend(triple[i : i + own], half, bias) for i in range(0, every, own)], axis=0
        )
        mixed_out[...] = mixed
        for i in range(2):
            cols = slice(i * half, (i + 1) * half)
            total = matmul(mixed, w[3, i * half : (i + 1) * half])
            part_out[:, cols] = total[:own]
            away_out[:, cols] = total[own:].astype(BF)

    normed_one, triple, mixed, part_own, part_away = call(
        enc_attend,
        "enc_attend",
        (sequence, gains[0], w_one),
        ((every, wide), BF),
        ((every, 3 * half), BF),
        ((every, half), BF),
        ((own, wide), F32),
        ((own, wide), BF),
    )

    def enc_norm(seq, own_part, got, gain, middle_out, normed_out):
        middle = seq[:own] + own_part[...] + got[...].astype(F32)
        middle_out[...] = middle
        normed_out[...] = layer_norm(middle, gain[...])

    middle, normed_two = call(
        enc_norm,
        "enc_norm",
        (sequence, part_own, cube.swap(part_away, y), gains[1]),
        ((own, wide), F32),
        ((own, wide), BF),
    )
    normed_far = cube.swap(normed_two, y)

    def enc_up_body(near, far, w, hidden_out, slope_out):
        rows = jnp.concatenate([near[...], far[...]], axis=0)
        for i in range(ups):
            cols = slice(i * half, (i + 1) * half)
            value, slope = gelu_parts(matmul(rows, w[i]))
            hidden_out[:, cols] = value.astype(BF)
            slope_out[:, cols] = slope

    hidden, slope = call(
        enc_up_body,
        "enc_up",
        (normed_two, normed_far, w_two),
        ((every, mlp), BF),
        ((every, mlp), F32),
    )

    def enc_down_body(rows, w, part_out, away_out):
        for i in range(2):
            cols = slice(i * half, (i + 1) * half)
            total = matmul(rows[...], w[i])
            part_out[:, cols] = total[:own]
            away_out[:, cols] = total[own:].astype(BF)

    part_own, part_away = call(
        enc_down_body, "enc_down", (hidden, w_three), ((own, wide), F32), ((own, wide), BF)
    )

    def chosen_of(order_ref, chip):
        place = lax.broadcasted_iota(jnp.int32, (seq_out, visible_count), 0)
        return (place == order_ref[chip : chip + 1, :]).astype(F32)

    def dec_attend(
        mid, own_part, got, w_p, order_ref, mask, tab, gain, w, gain_two,
        visible_out, input_out, normed_out, triple_out, mixed_out, middle_out, normed_two_out,
    ):
        encoded = mid[...] + own_part[...] + got[...].astype(F32)
        for chip in range(chips):
            visible = encoded[chip * length : chip * length + visible_count].astype(BF)
            visible_out[chip * visible_count : (chip + 1) * visible_count, :] = visible
        projected = matmul(visible_out[...], w_p[...])
        high = projected.astype(BF)
        low = (projected - high.astype(F32)).astype(BF)
        for chip in range(chips):
            rows = slice(chip * seq_out, (chip + 1) * seq_out)
            few = slice(chip * visible_count, (chip + 1) * visible_count)
            chosen = chosen_of(order_ref, chip)
            seen = jnp.sum(chosen, axis=1, keepdims=True)
            chosen = chosen.astype(BF)
            value = matmul(chosen, high[few]) + matmul(chosen, low[few])
            value = value + (1.0 - seen) * mask[...] + tab[...]
            input_out[rows, :] = value
            normed = layer_norm(value, gain[...])
            normed_out[rows, :] = normed
            triple_d = jnp.concatenate([matmul(normed, w[i]).astype(BF) for i in range(3)], axis=1)
            triple_out[rows, :] = triple_d
            mixed_d = attend(triple_d, thin, None)
            mixed_out[rows, :] = mixed_d
            middle_d = value + matmul(mixed_d, w[3])
            middle_out[rows, :] = middle_d
            normed_two_out[rows, :] = layer_norm(middle_d, gain_two[...])

    visible, decoder_in, normed_three, triple_d, mixed_d, middle_d, normed_four = call(
        dec_attend,
        "dec_attend",
        (
            middle,
            part_own,
            cube.swap(part_away, y),
            w_proj,
            order,
            mask_row,
            table,
            gains[2],
            v_one,
            gains[3],
        ),
        ((chips * visible_count, wide), BF),
        ((rows_all, thin), F32),
        ((rows_all, thin), BF),
        ((rows_all, 3 * thin), BF),
        ((rows_all, thin), BF),
        ((rows_all, thin), F32),
        ((rows_all, thin), BF),
    )

    aligned = rows_d % 16 == 0

    def dec_mlp(mid, normed, w_u, w_d, grad_ref, out, grads, back_out):
        rows, grad = normed[...], grad_ref[...]
        total = mid[...]
        back = jnp.zeros((rows_all, thin), F32)
        for b in range(v_ups):
            value, slope_d = gelu_parts(matmul(rows, w_u[b]))
            value = value.astype(BF)
            total = total + matmul(value, w_d[b])
            down = over_rows(value, grad).astype(BF)
            if aligned:
                for i in range(0, thin, rows_n):
                    to = (b * thin + i) // rows_n * rows_d
                    for q in range(0, rows_n, rows_d):
                        grads[v_ups + q // rows_d, to : to + rows_d, :] = down[
                            i + q : i + q + rows_d
                        ]
            else:
                grads[v_ups + b] = down
            change = (slope_d * against_rows(grad, w_d[b])).astype(BF)
            grads[b] = over_rows(rows, change).astype(BF)
            back = back + against_rows(change, w_u[b])
        out[...] = total.astype(BF)
        back_out[...] = back

    decoded, grads_five, back_four = call(
        dec_mlp,
        "dec_mlp",
        (middle_d, normed_four, v_up, v_down, grad_rows),
        ((rows_all, thin), BF),
        ((2 * v_ups, thin, thin), BF),
        ((rows_all, thin), F32),
    )
    if not aligned:
        turned = grads_five[v_ups:].reshape(devices, rows_n // rows_d, rows_d, thin)
        grads_five = jnp.concatenate(
            [grads_five[:v_ups], turned.transpose(1, 0, 2, 3).reshape(-1, thin, thin)], axis=0
        )

    within = cube.within[::-1]
    s_five = Scatter(
        cube, grads_five, (2 * v_ups,), rows_d, [cube.core, y, cube.x] + cube.z[::-1]
    ).start()

    def dec_back_one(mid, gain, back, grad_ref, mix, w, middle_out, gain_out, out_out, mixed_out):
        change, gain_grad = norm_back(mid[...], gain[...], back[...])
        total = grad_ref[...].astype(F32) + change
        middle_out[...] = total
        gain_out[...] = gain_grad
        branch = total.astype(BF)
        out_out[...] = over_rows(mix[...], branch).astype(BF)
        mixed_out[...] = against_rows(branch, w[3]).astype(BF)

    grad_middle_d, gain_four_grad, grad_out_d, grad_mixed_d = call(
        dec_back_one,
        "dec_back_one",
        (middle_d, gains[3], back_four, grad_rows, mixed_d, v_one),
        ((rows_all, thin), F32),
        ((1, thin), F32),
        ((thin, thin), BF),
        ((rows_all, thin), BF),
    )
    s_five.finish()
    s_five.start()
    grad_mixed_d = after(grad_mixed_d, s_five.value)

    def dec_back_two(
        triple_ref, grad_ref, normed, w, start, gain, grad_mid, order_ref, seen_rows, w_p,
        qkv_out, gain_out, mask_out, proj_out, branch_out,
    ):
        gain_grad = jnp.zeros((1, thin), F32)
        mask_grad = jnp.zeros((1, thin), F32)
        pieces = ([], [], [])
        few = []
        for chip in range(chips):
            rows = slice(chip * seq_out, (chip + 1) * seq_out)
            parts = attend_back(triple_ref[rows, :], grad_ref[rows, :], thin, None)
            change = 0.0
            for i in range(3):
                pieces[i].append(parts[i])
                change = change + against_rows(parts[i], w[i])
            change, gain_part = norm_back(start[rows, :], gain[...], change)
            gain_grad = gain_grad + gain_part
            total = grad_mid[rows, :] + change
            chosen = chosen_of(order_ref, chip)
            seen = jnp.sum(chosen, axis=1, keepdims=True)
            mask_grad = mask_grad + jnp.sum((1.0 - seen) * total, axis=0, keepdims=True)
            few.append(over_rows(chosen.astype(BF), total.astype(BF)).astype(BF))
        for i in range(3):
            qkv_out[i] = over_rows(normed[...], jnp.concatenate(pieces[i], axis=0)).astype(BF)
        gain_out[...] = gain_grad
        mask_out[...] = mask_grad
        few = jnp.concatenate(few, axis=0)
        proj_out[...] = over_rows(seen_rows[...], few).astype(BF)
        branch = against_rows(few, w_p[...])
        gap = jnp.zeros((length - visible_count, wide), F32)
        branch_out[...] = jnp.concatenate(
            [
                piece
                for chip in range(chips)
                for piece in (branch[chip * visible_count : (chip + 1) * visible_count], gap)
            ],
            axis=0,
        ).astype(BF)

    grad_qkv_d, gain_three_grad, mask_grad, grad_proj, branch = call(
        dec_back_two,
        "dec_back_two",
        (
            triple_d,
            grad_mixed_d,
            normed_three,
            v_one,
            decoder_in,
            gains[2],
            grad_middle_d,
            order,
            visible,
            w_proj,
        ),
        ((3, thin, thin), BF),
        ((1, thin), F32),
        ((1, thin), F32),
        ((wide, thin), BF),
        ((own, wide), BF),
    )
    branch_far = cube.swap(branch, y)
    grads_four = jnp.concatenate(
        [grad_proj.reshape(devices, rows_p, thin)]
        + [grad_qkv_d[i].reshape(devices, rows_d, thin) for i in range(3)]
        + [grad_out_d.reshape(devices, rows_d, thin)],
        axis=1,
    )
    s_four = Scatter(
        cube, grads_four, (), rows_p + 4 * rows_d, [cube.core, cube.x, y] + cube.z[::-1]
    ).start()
    s_five.finish()
    s_five.start()
    branch_far = after(branch_far, s_five.value)

    def enc_mlp_back(near, far, w_d, hid, slo, norm_near, norm_far, w_u, down, up, part_out, away_out):
        grad = jnp.concatenate([near[...], far[...]], axis=0)
        rows = jnp.concatenate([norm_near[...], norm_far[...]], axis=0)
        total = 0.0
        for i in range(2):
            down[i] = over_rows(hid[...], grad[:, i * half : (i + 1) * half]).astype(BF)
        for b in range(ups):
            cols = slice(b * half, (b + 1) * half)
            change = sum(
                against_rows(grad[:, i * half : (i + 1) * half], w_d[i, cols]) for i in range(2)
            )
            change = (slo[:, cols] * change).astype(BF)
            up[b] = over_rows(rows, change).astype(BF)
            total = total + against_rows(change, w_u[b])
        part_out[...] = total[:own]
        away_out[...] = total[own:].astype(BF)

    grads_three, grads_two, part_own, part_away = call(
        enc_mlp_back,
        "enc_mlp_back",
        (branch, branch_far, w_three, hidden, slope, normed_two, normed_far, w_two),
        ((2, mlp, half), BF),
        ((ups, wide, half), BF),
        ((own, wide), F32),
        ((own, wide), BF),
    )
    part_got = cube.swap(part_away, y)
    s_three = Scatter(cube, grads_three, (2,), rows_m, within).start()
    s_four.finish()
    s_four.start()
    part_got = after(part_got, s_four.value)

    def enc_norm_back(mid, gain, own_part, got, near, middle_out, gain_out, branch_out):
        change, gain_grad = norm_back(
            mid[...], gain[...], own_part[...] + got[...].astype(F32)
        )
        total = near[...].astype(F32) + change
        middle_out[...] = total
        gain_out[...] = gain_grad
        branch_out[...] = total.astype(BF)

    grad_middle, gain_two_grad, branch = call(
        enc_norm_back,
        "enc_norm_back",
        (middle, gains[1], part_own, part_got, branch),
        ((own, wide), F32),
        ((1, wide), F32),
        ((own, wide), BF),
    )
    branch_far = cube.swap(branch, y)
    s_two = Scatter(cube, grads_two, (ups, 2), rows_e, within).start()
    s_five.finish()
    s_three.finish()
    s_three.start(s_five.got)
    s_five.start()
    branch_far = after(branch_far, s_three.value, s_five.value)

    def enc_attend_back(near, far, mix, triple_ref, normed, w, grads, part_out, away_out):
        grad = jnp.concatenate([near[...], far[...]], axis=0)
        for i in range(2):
            grads[3, i * half : (i + 1) * half, :] = over_rows(
                mix[...], grad[:, i * half : (i + 1) * half]
            ).astype(BF)
        grad_mixed = sum(
            against_rows(grad[:, i * half : (i + 1) * half], w[3, i * half : (i + 1) * half])
            for i in range(2)
        ).astype(BF)
        bias = bias_of(own, length, seq_in + 1)
        pieces = [
            attend_back(triple_ref[i : i + own, :], grad_mixed[i : i + own], half, bias)
            for i in range(0, every, own)
        ]
        total = 0.0
        for i in range(3):
            change = jnp.concatenate([piece[i] for piece in pieces], axis=0)
            grads[i] = over_rows(normed[...], change).astype(BF)
            total = total + against_rows(change, w[i])
        part_out[...] = total[:own]
        away_out[...] = total[own:].astype(BF)

    grads_one, part_own, part_away = call(
        enc_attend_back,
        "enc_attend_back",
        (branch, branch_far, mixed, triple, normed_one, w_one),
        ((4, wide, half), BF),
        ((own, wide), F32),
        ((own, wide), BF),
    )
    s_one = Scatter(cube, grads_one, (4, 2), rows_e, within).start()
    part_got = cube.swap(part_away, y)

    def enc_last(seq, gain, own_part, got, grad_mid, out, gain_out):
        change, gain_grad = norm_back(
            seq[:own], gain[...], own_part[...] + got[...].astype(F32)
        )
        out[...] = grad_mid[...] + change
        gain_out[...] = gain_grad

    s_two.finish()
    s_two.start(s_three.got)
    s_three.finish()
    s_three.start()
    part_got = after(part_got, s_two.value)
    grad_seq, gain_one_grad = call(
        enc_last,
        "enc_last",
        (sequence, gains[0], part_own, part_got, grad_middle),
        ((own, wide), F32),
        ((1, wide), F32),
    )

    grad_seq = grad_seq.reshape(chips, length, wide)[:, : seq_in + 1]
    sensor_grad = jnp.sum(
        jnp.where(onehot[:chips, :, None], jnp.sum(grad_seq, axis=1)[:, None, :], 0.0), axis=0
    )
    class_grad = jnp.sum(grad_seq[:, seq_in], axis=0, keepdims=True)
    token_rows = jnp.concatenate(
        [grad_seq[:, visible_count : visible_count + 1], grad_seq[:, :visible_count]], axis=1
    ).reshape(chips * seq_in, wide)

    def widened(row):
        return jnp.pad(row, ((0, 0), (0, wide - thin)))

    small = jnp.concatenate(
        [class_grad, sensor_grad, gain_one_grad, gain_two_grad]
        + [widened(row) for row in (mask_grad, gain_three_grad, gain_four_grad)],
        axis=0,
    )
    for name in cube.names:
        small = small + cube.swap(small, name)

    s_four.finish()
    while s_four.order:
        s_four.start()
        s_four.finish()
    s_five.finish()
    while s_five.order:
        s_five.start()
        s_five.finish()
    s_three.finish()
    s_two.finish()
    s_one.finish()
    s_one.start(s_two.got)
    s_one.finish()
    while s_one.order:
        for piece in (s_three, s_two, s_one):
            if piece.order:
                piece.start().finish()
    sum_one, sum_two, sum_three, sum_four, sum_five = (
        s.value for s in (s_one, s_two, s_three, s_four, s_five)
    )

    columns = jnp.concatenate([sum_one[:3], sum_two], axis=0)
    here = lax.dynamic_index_in_dim(columns, section, 1, keepdims=False)
    away = lax.dynamic_index_in_dim(columns, 1 - section, 1, keepdims=False).astype(BF)
    columns = cube.both(here, cube.swap(away, y).astype(F32), y, 1)
    qkv_grad = columns[:3].transpose(2, 0, 1, 3).reshape(rows_e, 3 * wide)
    up_grad = columns[3:].transpose(2, 1, 0, 3).reshape(rows_e, sections * mlp)
    out_part = jnp.concatenate([sum_one[3, i] for i in range(2)], axis=1)
    down_part = jnp.concatenate([sum_three[i] for i in range(2)], axis=1)
    proj_part = sum_four[:rows_p]
    cuts = [sum_four[rows_p + i * rows_d : rows_p + (i + 1) * rows_d] for i in range(4)]
    qkv_part, out_part_d = jnp.concatenate(cuts[:3], axis=1), cuts[3]
    up_part = jnp.concatenate([sum_five[i] for i in range(v_ups)], axis=1)
    down_part_d = sum_five[v_ups:].reshape(rows_n, thin)

    def halves(rows):
        mine, away = part(rows, section, 1), part(rows, 1 - section, 1)
        got = cube.swap(away.astype(BF), y).astype(rows.dtype)
        return cube.both(mine, got, y, 0).reshape(-1, mine.shape[1])

    count = sensor_count + 1
    return (
        halves(decoded),
        halves(token_rows),
        qkv_grad,
        out_part,
        up_grad,
        down_part,
        proj_part,
        qkv_part,
        out_part_d,
        up_part,
        down_part_d,
        small[0],
        small[1:count],
        small[count],
        small[count + 1],
        small[count + 2, :thin],
        small[count + 3, :thin],
        small[count + 4, :thin],
    )


def solution(mesh):
    every = P(("section", "dp"), None)
    rows = P("dp", None)
    in_specs = (
        rows,
        rows,
        P("dp"),
        P(),
        P(),
        P(),
        every,
        every,
        P(),
        every,
        every,
        every,
        P(),
        P(),
        every,
        every,
        P(),
        every,
        every,
        rows,
    )
    out_specs = (P("dp", "section"),) * 2 + (every,) * 9 + (P(),) * 7
    return jax.shard_map(local, mesh=mesh, in_specs=in_specs, out_specs=out_specs, check_vma=False)
```

```python
import math

import jax
import jax.numpy as jnp
from jax import lax
from jax.experimental import pallas as pl
from jax.experimental.pallas import tpu as pltpu
from jax.sharding import PartitionSpec as P

HEAD_DIM = 64
PAIR = 2 * HEAD_DIM
BF = jnp.bfloat16
F32 = jnp.float32
SCALE = HEAD_DIM ** (-0.5)


def matmul(left, right):
    return jnp.dot(left, right, preferred_element_type=F32)


def against_rows(left, right):
    return lax.dot_general(left, right, (((1,), (1,)), ((), ())), preferred_element_type=F32)


def over_rows(left, right):
    return lax.dot_general(left, right, (((0,), (0,)), ((), ())), preferred_element_type=F32)


def normal_parts(rows):
    mean = jnp.mean(rows, axis=-1, keepdims=True)
    centred = rows - mean
    spread = jnp.mean(centred * centred, axis=-1, keepdims=True)
    inverse = lax.rsqrt(spread + 1e-05)
    return centred * inverse, inverse


def layer_norm(rows, gain):
    return (normal_parts(rows)[0] * gain).astype(BF)


def norm_back(rows, gain, grad):
    hat, inverse = normal_parts(rows)
    scaled = grad * gain
    out = inverse * (
        scaled
        - jnp.mean(scaled, axis=-1, keepdims=True)
        - hat * jnp.mean(scaled * hat, axis=-1, keepdims=True)
    )
    return out, jnp.sum(grad * hat, axis=0, keepdims=True)


def gelu_parts(value):
    square = value * value
    flat = jnp.tanh(0.7978845608028654 * (value + 0.044715 * value * square))
    side = 0.5 * (1.0 + flat)
    slope = side + 0.5 * value * (1.0 - flat * flat) * (
        0.7978845608028654 + 3.0 * 0.044715 * 0.7978845608028654 * square
    )
    return value * side, slope


def position_table(count, width):
    half = width // 2
    place = jnp.arange(count, dtype=F32)[:, None]
    rate = jnp.exp(jnp.arange(half, dtype=F32) * (-math.log(10000.0) / half))
    angle = place * rate[None, :]
    return jnp.concatenate([jnp.sin(angle), jnp.cos(angle)], axis=1)


def shares_of(key, query, bias):
    scores = against_rows(key, query)
    if bias is not None:
        scores = scores + jnp.concatenate([bias, bias], axis=1)
    raised = jnp.exp(scores - jnp.max(scores, axis=0, keepdims=True))
    return raised * (1.0 / jnp.sum(raised, axis=0, keepdims=True))


def apart(value):
    first = lax.broadcasted_iota(jnp.int32, value.shape, 1) < HEAD_DIM
    none = jnp.zeros_like(value)
    return jnp.concatenate([jnp.where(first, value, none), jnp.where(first, none, value)], axis=0)


def together(value):
    rows = value.shape[0] // 2
    first = lax.broadcasted_iota(jnp.int32, (rows, value.shape[1]), 1) < HEAD_DIM
    return jnp.where(first, value[:rows], value[rows:])


def bias_of(length, seq, valid):
    if length == valid:
        return None
    key = lax.broadcasted_iota(jnp.int32, (length, length), 0)
    query = lax.broadcasted_iota(jnp.int32, (length, length), 1)
    kept = jnp.zeros((length, length), jnp.bool_)
    for start in range(0, length, seq):
        kept = kept | (
            (key >= start) & (key < start + valid) & (query >= start) & (query < start + seq)
        )
    return jnp.where(kept, 0.0, -1e30)


def attend(triple, width, bias):
    out = []
    for at in range(0, width, PAIR):
        query, key, value = (triple[:, i * width + at : i * width + at + PAIR] for i in range(3))
        shares = shares_of(key, apart(query) * SCALE, bias).astype(BF)
        out.append(together(over_rows(shares, value)).astype(BF))
    return jnp.concatenate(out, axis=1)


def attend_back(triple, grad_mixed, width, bias):
    out = ([], [], [])
    for at in range(0, width, PAIR):
        query, key, value = (triple[:, i * width + at : i * width + at + PAIR] for i in range(3))
        queries, grads = apart(query) * SCALE, apart(grad_mixed[:, at : at + PAIR])
        exact = shares_of(key, queries, bias)
        grad_shares = against_rows(value, grads)
        mean = jnp.sum(grad_shares * exact, axis=0, keepdims=True)
        grad_scores = (exact * (grad_shares - mean)).astype(BF)
        out[0].append((together(over_rows(grad_scores, key)) * SCALE).astype(BF))
        out[1].append(matmul(grad_scores, queries).astype(BF))
        out[2].append(matmul(exact.astype(BF), grads).astype(BF))
    return [jnp.concatenate(piece, axis=1) for piece in out]


HEAVY = ("attn", "up", "down", "dattn", "dmlp", "db1", "db2", "db3", "emlp", "emlpg", "eab")


def call(body, name, args, *outs, bits=0, scratch=(), space=pltpu.VMEM):
    size = sum(math.prod(shape) * jnp.dtype(dtype).itemsize for shape, dtype in outs)
    size += sum(value.size * value.dtype.itemsize for value in args[bits:])
    run = pl.pallas_call(
        body,
        out_shape=[jax.ShapeDtypeStruct(shape, dtype) for shape, dtype in outs],
        in_specs=[pl.BlockSpec(memory_space=pltpu.SMEM)] * bits
        + [pl.BlockSpec(memory_space=space)] * (len(args) - bits),
        cost_estimate=pl.CostEstimate(flops=COSTS.get(Plan.now, 10**10), bytes_accessed=1000, transcendentals=0),
        compiler_params=pltpu.CompilerParams(
            vmem_limit_bytes=size + size // 4 + ((10 << 20) if name in HEAVY else (1 << 20))
        ),
        scratch_shapes=list(scratch),
        name=name,
    )
    return list(run(*args))


def after(value, *others):
    return lax.optimization_barrier((value,) + others)[0]


def flat(value, place, split):
    rest = value.shape[place + split : -1]
    head = (math.prod(value.shape[:place]),) + (2,) * split
    return value.reshape(head + (math.prod(rest), value.shape[-1]))


def merge_kernel(bit, own, got, out):
    def step(i, _):
        out[i, bit[0]] = own[i]
        out[i, 1 - bit[0]] = got[i]
        return 0

    lax.fori_loop(0, own.shape[0], step, 0)


def merged(own, got, bit, place, aligned):
    if not aligned:
        mine = bit[0] == 0
        return jnp.where(mine, jnp.stack([own, got], place), jnp.stack([got, own], place))
    left, right = flat(own, place, False), flat(got, place, False)
    shape = left.shape[:1] + (2,) + left.shape[1:]
    (out,) = call(merge_kernel, "merge", (bit, left, right), (shape, own.dtype), bits=1)
    return out.reshape(own.shape[:place] + (2,) + own.shape[place:])


def split_kernel(bit, here, got, away_out, here_out):
    def step(i, _):
        for out, side in ((away_out, 1 - bit[0]), (here_out, bit[0])):
            out[i] = here[i, side] + got[i, side]
        return 0

    lax.fori_loop(0, here.shape[0], step, 0)


def split_sum(here, got, bit, place, aligned):
    rest = here.shape[:place] + here.shape[place + 1 :]
    if not aligned:
        return split(here + got, bit, place)
    left, right = flat(here, place, True), flat(got, place, True)
    shape = left.shape[:1] + left.shape[2:]
    parts = call(
        split_kernel, "split_sum", (bit, left, right), (shape, BF), (shape, BF), bits=1
    )
    return [value.reshape(rest) for value in parts]


def split(total, bit, place):
    return [
        lax.dynamic_index_in_dim(total, which, place, keepdims=False)
        for which in (1 - bit[0], bit[0])
    ]


class Cube:
    def __init__(self):
        self.names = [
            (axis, bit)
            for axis in ("section", "dp")
            for bit in reversed(range((lax.axis_size(axis) - 1).bit_length()))
        ]
        self.bits = {
            (axis, bit): ((lax.axis_index(axis) >> bit) & 1).reshape(1)
            for axis, bit in self.names
        }
        depth = len(self.names) - 3
        self.of = {"c": ("dp", 0), "x": ("dp", 1), "y": ("section", 0)}
        self.of.update({f"z{i}": ("dp", 2 + i) for i in range(depth)})
        self.z = [f"z{i}" for i in range(depth)]

    def swap(self, value, step):
        axis, bit = self.of[step]
        route = [(i, i ^ (1 << bit)) for i in range(lax.axis_size(axis))]
        return lax.ppermute(value, axis, route)

    def bit(self, step):
        return self.bits[self.of[step]]

    def place(self, held, step):
        at = self.names.index(self.of[step])
        return sum(1 for other in held if self.names.index(self.of[other]) < at)


class Plan:
    now = None

    def __init__(self):
        self.steps, self.value, self.token = {}, {}, None

    def add(self, name, needs, body):
        self.steps[name] = (needs, body)

    def hold(self, value):
        if self.token is None:
            return value
        if Plan.now in FLIPS:
            return lax.optimization_barrier((self.token, value))[1]
        return after(value, self.token)

    def run(self, order):
        left, names = dict(self.steps), list(self.steps)
        wanted = [names[i] for i in order] if len(order) == len(names) else names
        while left:
            name = next(
                n for n in wanted if n in left and all(d in self.value for d in left[n][0])
            )
            Plan.now = names.index(name)
            with jax.named_scope(name):
                self.value[name] = left.pop(name)[1]()

    def __getitem__(self, name):
        return self.value[name]

    def kernel(self, name, needs, body):
        def step():
            out = body()
            self.token = min((v for v in out if v is not None), key=lambda value: value.size)
            return out

        self.add(name, needs, step)

    def send(self, name, needs, cube, step, value):
        self.add(name, needs, lambda: cube.swap(self.hold(value()), step))


def gather(plan, cube, name, order, needs, piece, lead, aligned):
    held = []
    for step in order:
        before = (lambda at: lambda: plan[at][0])(f"{name}.m{held[-1]}") if held else piece
        plan.send(f"{name}.{step}", needs, cube, step, before)
        if aligned and step == "c":
            plan.value[f"{name}.own"] = before
            return f"{name}.{step}"

        def finish(step=step, before=before, place=lead + cube.place(held, step)):
            got = plan.hold(plan[f"{name}.{step}"])
            return [merged(before(), got, cube.bit(step), place, aligned)]

        needs = [f"{name}.m{step}"]
        plan.kernel(needs[0], [f"{name}.{step}"], finish)
        held.append(step)
    return needs[0]


def scatter(plan, cube, name, order, needs, cut, lead, aligned, last):
    held = sorted(order, key=lambda step: cube.names.index(cube.of[step]))
    before = cut
    for index, step in enumerate(order):
        plan.send(f"{name}.{step}", needs, cube, step, lambda before=before: before()[0])
        held = [other for other in held if other != step]
        follow = order[index + 1] if held else None

        def finish(step=step, before=before, follow=follow, held=tuple(held)):
            got = plan.hold(plan[f"{name}.{step}"])
            if follow is None:
                return last(before()[1], got)
            place = lead + cube.place(held, follow)
            return split_sum(before()[1], got, cube.bit(follow), place, aligned)

        needs = [f"{name}.a{step}"]
        plan.kernel(needs[0], [f"{name}.{step}"], finish)
        before = (lambda at: lambda: plan[at])(needs[0])
    return needs[0]


def blocks_of(shard, width):
    return [shard[..., i : i + width] for i in range(0, shard.shape[-1], width)]

def E3_ORDER(z):
    return z + ["x"] + ["c"]


def GD2_ORDER(z):
    return ["y", "x"] + z[::-1]


def GD1_ORDER(z):
    return ["x"] + ["y"] + z[::-1]


def GE1_ORDER(z):
    return ["x"] + z[::-1]


def GE3_ORDER(z):
    return z[::-1] + ["x"]


def GE2_ORDER(z):
    return ["x"] + z[::-1]


ORDER = (
    0, 24, 1, 33, 17, 42, 25, 26, 2, 3, 10, 34, 35, 27, 4, 5, 28, 36, 37, 29, 18, 11, 12, 6, 7, 30, 19,
    38, 39, 13, 14, 8, 9, 20, 31, 32, 21, 43, 44, 40, 41, 15, 16, 45, 46, 22, 23, 47, 48, 49, 50, 51,
    62, 52, 63, 64, 65, 66, 53, 54, 67, 68, 76, 77, 78, 79, 87, 80, 88, 95, 81, 96, 122, 89, 69, 70, 97,
    98, 55, 56, 90, 91, 71, 106, 99, 100, 82, 83, 107, 57, 58, 108, 123, 101, 102, 124, 109, 92, 93,
    125, 110, 84, 59, 60, 85, 94, 120, 111, 86, 112, 72, 121, 61, 103, 104, 113, 114, 115, 116, 73, 74,
    105, 118, 117, 119, 75,
)
COSTS = {
    2: 1000000000, 4: 3000000000, 8: 1000000000, 15: 3000000000, 20: 3000000000, 25: 3000000000, 27:
    1000, 29: 3000000000, 36: 1000000000, 38: 1000000000, 40: 1000, 42: 3000000000, 45: 3000000000, 48:
    1000000000, 50: 1000, 55: 3000000000, 57: 1000, 62: 1000000000, 65: 1000, 76: 1000, 78: 1000, 82:
    3000000000, 90: 1000000000, 92: 3000000000, 99: 3000000000, 101: 1000, 109: 3000000000, 121:
    3000000000, 123: 1000000000, 125: 3000000000,
}
FLIPS = (21, 28, 31, 41, 50, 57, 75, 109, 123,)


def local(
    tokens,
    patch_order,
    sensor_tag,
    class_token,
    sensor_table,
    enc_gain_one,
    enc_qkv,
    enc_out,
    enc_gain_two,
    enc_up,
    enc_down,
    dec_proj,
    mask_token,
    dec_gain_one,
    dec_qkv,
    dec_out,
    dec_gain_two,
    dec_up,
    dec_down,
    out_grad,
):
    cube, plan = Cube(), Plan()
    section = lax.axis_index("section")
    sections = lax.axis_size("section")
    group = lax.axis_size("dp")
    devices = sections * group
    wide = tokens.shape[1]
    thin = out_grad.shape[1]
    half = wide // sections
    mlp = enc_up.shape[1] // sections
    ups = mlp // half
    rows_e, rows_m = enc_qkv.shape[0], enc_down.shape[0]
    rows_p, rows_d, rows_n = dec_proj.shape[0], dec_qkv.shape[0], dec_down.shape[0]
    rows_four = 4 * rows_d + rows_p
    v_ups = dec_up.shape[1] // thin
    quarters = rows_n // rows_d
    chips_all = patch_order.shape[0]
    chips = chips_all // sections
    seq_in = tokens.shape[0] // chips_all
    seq_out = patch_order.shape[1]
    visible_count = seq_in - 1
    sensor_count = sensor_table.shape[0]
    length = -(-(seq_in + 1) // 8) * 8
    own = chips * length
    every = sections * own
    rows_all = chips * seq_out
    aligned = rows_d % 16 == 0 and rows_e % 8 == 0
    side, core = cube.bit("y"), cube.bit("c")
    lead_d, lead_e = (2,) * (len(cube.names) - 1), (2,) * (len(cube.names) - 2)

    def part(value, which, axis):
        size = value.shape[axis] // sections
        return lax.dynamic_slice_in_dim(value, which * size, size, axis=axis)

    def mine_first(value):
        return jnp.concatenate([part(value, section, 0), part(value, 1 - section, 0)], axis=0)

    gains = [
        gain.astype(F32)[None, :]
        for gain in (enc_gain_one, enc_gain_two, dec_gain_one, dec_gain_two)
    ]
    order = part(patch_order, section, 0)[:, :visible_count]
    grad_rows = part(out_grad, section, 0)
    mask_row = mask_token.astype(F32)[None, :]
    tags = mine_first(sensor_tag)
    onehot = tags[:, None] == jnp.arange(sensor_count, dtype=jnp.int32)[None, :]

    def pack_kernel(bit, *refs):
        far_refs, outs, near_refs, sems = refs[:9], refs[9:15], refs[15:24], refs[24]
        copies = [
            pltpu.make_async_copy(far, near, sems.at[i])
            for i, (far, near) in enumerate(zip(far_refs, near_refs))
        ]
        for copy in copies:
            copy.start()
        for copy in copies:
            copy.wait()
        qkv, out, up, down, proj, qkv_d, out_d, up_d, down_d = near_refs
        away, mine, outs_out, three, four, five = outs
        other = bit[0] == 1
        for i in range(3 + ups):
            from_ref, at = (qkv, i * wide) if i < 3 else (up, (i - 3) * half)
            step = half if i < 3 else mlp
            near, far = (from_ref[:, at + j * step : at + j * step + half] for j in range(2))
            mine[i] = jnp.where(other, far, near)
            away[i] = jnp.where(other, near, far)
        for i in range(2):
            outs_out[0, i] = out[:, i * half : (i + 1) * half]
            three[i] = down[:, i * half : (i + 1) * half]
        for i in range(3):
            four[i * rows_d : (i + 1) * rows_d, :] = qkv_d[:, i * thin : (i + 1) * thin]
        four[3 * rows_d : 4 * rows_d, :] = out_d[...]
        four[4 * rows_d :, :] = proj[...]
        for i in range(v_ups):
            five[i] = up_d[:, i * thin : (i + 1) * thin]
        for i in range(quarters):
            five[v_ups + i] = down_d[i * rows_d : (i + 1) * rows_d, :]

    def pack():
        if aligned:
            return call(
                pack_kernel,
                "pack",
                (side, enc_qkv, enc_out, enc_up, enc_down, dec_proj, dec_qkv, dec_out, dec_up, dec_down),
                ((3 + ups, rows_e, half), BF),
                ((3 + ups, rows_e, half), BF),
                ((1, 2, rows_e, half), BF),
                ((2, rows_m, half), BF),
                ((rows_four, thin), BF),
                ((v_ups + quarters, rows_d, thin), BF),
                bits=1,
                space=pltpu.HBM,
                scratch=[
                    pltpu.VMEM(shard.shape, BF)
                    for shard in (
                        enc_qkv, enc_out, enc_up, enc_down, dec_proj, dec_qkv, dec_out, dec_up, dec_down,
                    )
                ]
                + [pltpu.SemaphoreType.DMA((9,))],
            )
        cut = enc_qkv.reshape(rows_e, 3, sections, half)
        sides = [
            jnp.stack(
                [cut[:, i, which] for i in range(3)]
                + blocks_of(part(enc_up, which, 1), half)
            )
            for which in range(2)
        ]
        return [
            jnp.where(side[0] == 1, sides[0], sides[1]),
            jnp.where(side[0] == 1, sides[1], sides[0]),
            jnp.stack(blocks_of(enc_out, half))[None],
            jnp.stack(blocks_of(enc_down, half)),
            jnp.concatenate(blocks_of(dec_qkv, thin) + [dec_out, dec_proj], axis=0),
            jnp.stack(
                blocks_of(dec_up, thin)
                + [dec_down[i : i + rows_d] for i in range(0, rows_n, rows_d)]
            ),
        ]

    plan.kernel("pack", [], pack)
    plan.send("sw", ["pack"], cube, "y", lambda: plan["pack"][0])

    def columns_kernel(bit, mine, got, outs, one, two):
        for i in range(3 + ups):
            to, at = (one, i) if i < 3 else (two, i - 3)
            to[at, bit[0]] = mine[i]
            to[at, 1 - bit[0]] = got[i]
        one[3] = outs[0]

    def columns():
        mine, got, outs = plan["pack"][1], plan.hold(plan["sw"]), plan["pack"][2]
        if aligned:
            return call(
                columns_kernel,
                "columns",
                (side, mine, got, outs),
                ((4, 2, rows_e, half), BF),
                ((ups, 2, rows_e, half), BF),
                bits=1,
            )
        both = merged(mine, got, side, 1, False)
        return [jnp.concatenate([both[:3], outs], axis=0), both[3:]]

    plan.kernel("msw", ["sw"], columns)
    z = cube.z
    e_one = gather(plan, cube, "E1", z + ["x", "c"], ["msw"], lambda: plan["msw"][0], 2, aligned)
    e_two = gather(plan, cube, "E2", z + ["x", "c"], ["msw"], lambda: plan["msw"][1], 2, aligned)
    e_three = gather(plan, cube, "E3", E3_ORDER(z), ["pack"], lambda: plan["pack"][3], 1, aligned)
    d_one = gather(plan, cube, "D1", z + ["x", "y", "c"], ["pack"], lambda: plan["pack"][4], 0, aligned)
    d_two = gather(plan, cube, "D2", z + ["x", "y", "c"], ["pack"], lambda: plan["pack"][5], 1, aligned)

    def halves_in(name):
        return [plan.value[f"{name}.own"](), plan.hold(plan[f"{name}.c"])]

    def read_whole(bit, own_block, got_block):
        wide_rows = own_block.shape[1] % 16 != 0
        near, far = own_block, got_block
        if wide_rows:
            near, far = near.astype(F32), far.astype(F32)
        first = bit[0] == 0
        both = jnp.stack([jnp.where(first, near, far), jnp.where(first, far, near)], axis=1)
        return both.reshape(-1, both.shape[-1]).astype(BF)

    def with_whole(kernel, count, shape, at, outs_at):
        def body(bit, *refs):
            refs = list(refs)
            near, far = refs[at], refs[at + 1]
            whole = refs[outs_at]
            for i in range(count):
                whole[i] = read_whole(bit, near[i], far[i])
            kernel(*refs[:at], whole, *refs[at + 2 : outs_at], *refs[outs_at + 1 :])

        return body

    def weighted(name, kernel, args, at, chunk, natural, count, shape, *outs):
        if not aligned:
            whole = natural()
            return call(kernel, name, args[:at] + (whole,) + args[at:], *outs) + [whole]
        near, far = (value.reshape((count, -1) + value.shape[-2:]) for value in halves_in(chunk))
        body = with_whole(kernel, count, shape, at, len(args) + 2)
        out = call(
            body,
            name,
            (core,) + args[:at] + (near, far) + args[at:],
            ((count,) + shape, BF),
            *outs,
            bits=1,
        )
        return out[1:] + out[:1]

    def w_one():
        return plan["attn"][5]

    def w_two():
        return plan["up"][2]

    def w_three():
        return plan["down"][2]

    def four_natural():
        whole = plan[d_one][0].reshape(devices, rows_four, thin)
        blocks = whole[:, : 4 * rows_d].reshape(devices, 4, rows_d, thin)
        return [
            whole[:, 4 * rows_d :].reshape(wide, thin),
            blocks.transpose(1, 0, 2, 3).reshape(4, thin, thin),
        ]

    def five_natural():
        whole = plan[d_two][0].reshape(v_ups + quarters, devices, rows_d, thin)
        return [
            whole[:v_ups].reshape(v_ups, thin, thin),
            whole[v_ups:].transpose(1, 0, 2, 3).reshape(v_ups, thin, thin),
        ]

    def sequence():
        table_rows = plan.hold(sensor_table)
        sensor_rows = matmul(onehot.astype(BF), table_rows)
        chip_tokens = mine_first(tokens.reshape(chips_all, seq_in, wide)).astype(F32)
        lead = jnp.broadcast_to(class_token.astype(F32)[None, None, :], (chips_all, 1, wide))
        filled = (
            jnp.concatenate([chip_tokens[:, 1:], chip_tokens[:, :1], lead], axis=1)
            + sensor_rows[:, None, :]
        )
        rows = jnp.pad(filled, ((0, 0), (0, length - seq_in - 1), (0, 0))).reshape(every, wide)
        return [rows, position_table(seq_out, thin)]

    plan.kernel("seq", ["pack"], sequence)

    def attn_kernel(seq, gain, w, normed_out, triple_out, mixed_out, part_out, away_out):
        normed = layer_norm(seq[...], gain[...])
        normed_out[...] = normed
        for i in range(3):
            triple_out[:, i * half : (i + 1) * half] = matmul(normed, w[i]).astype(BF)
        bias = bias_of(own, length, seq_in + 1)
        triple = triple_out[...]
        mixed = jnp.concatenate(
            [attend(triple[i : i + own], half, bias) for i in range(0, every, own)], axis=0
        )
        mixed_out[...] = mixed
        for i in range(2):
            cols = slice(i * half, (i + 1) * half)
            total = matmul(mixed, w[3, i * half : (i + 1) * half])
            part_out[:, cols] = total[:own]
            away_out[:, cols] = total[own:].astype(BF)

    plan.kernel(
        "attn",
        ["seq", e_one],
        lambda: weighted(
            "attn",
            attn_kernel,
            (plan.hold(plan["seq"][0]), gains[0]),
            2,
            "E1",
            lambda: plan[e_one][0].reshape(4, wide, half),
            4,
            (wide, half),
            ((every, wide), BF),
            ((every, 3 * half), BF),
            ((every, half), BF),
            ((own, wide), F32),
            ((own, wide), BF),
        ),
    )
    plan.send("X1", ["attn"], cube, "y", lambda: plan["attn"][4])

    def norm_kernel(seq, own_part, got, gain, middle_out, normed_out):
        middle = seq[:own] + own_part[...] + got[...].astype(F32)
        middle_out[...] = middle
        normed_out[...] = layer_norm(middle, gain[...])

    plan.kernel(
        "norm",
        ["X1"],
        lambda: call(
            norm_kernel,
            "norm",
            (plan["seq"][0], plan["attn"][3], plan.hold(plan["X1"]), gains[1]),
            ((own, wide), F32),
            ((own, wide), BF),
        ),
    )
    plan.send("X2", ["norm"], cube, "y", lambda: plan["norm"][1])

    def up_kernel(near, far, w, hidden_out, slope_out):
        rows = jnp.concatenate([near[...], far[...]], axis=0)
        for i in range(ups):
            cols = slice(i * half, (i + 1) * half)
            value, slope = gelu_parts(matmul(rows, w[i]))
            hidden_out[:, cols] = value.astype(BF)
            slope_out[:, cols] = slope

    plan.kernel(
        "up",
        ["X2", e_two],
        lambda: weighted(
            "up",
            up_kernel,
            (plan["norm"][1], plan.hold(plan["X2"])),
            2,
            "E2",
            lambda: plan[e_two][0].reshape(ups, wide, half),
            ups,
            (wide, half),
            ((every, mlp), BF),
            ((every, mlp), F32),
        ),
    )

    def down_kernel(rows, w, part_out, away_out):
        for i in range(2):
            cols = slice(i * half, (i + 1) * half)
            total = matmul(rows[...], w[i])
            part_out[:, cols] = total[:own]
            away_out[:, cols] = total[own:].astype(BF)

    plan.kernel(
        "down",
        ["up", e_three],
        lambda: weighted(
            "down",
            down_kernel,
            (plan.hold(plan["up"][0]),),
            1,
            "E3",
            lambda: plan[e_three][0].reshape(2, mlp, half),
            2,
            (mlp, half),
            ((own, wide), F32),
            ((own, wide), BF),
        ),
    )
    plan.send("X3", ["down"], cube, "y", lambda: plan["down"][1])

    def chosen_of(order_ref, chip):
        place = lax.broadcasted_iota(jnp.int32, (seq_out, visible_count), 0)
        return (place == order_ref[chip : chip + 1, :]).astype(F32)

    def dattn_body(bit, mid, own_part, got, near, far, *refs):
        w_p, w = refs[5], refs[6]
        for i in range(4):
            rows = slice(i * rows_d, (i + 1) * rows_d)
            w[i] = read_whole(bit, near[:, rows, :], far[:, rows, :])
        w_p[...] = read_whole(bit, near[:, 4 * rows_d :, :], far[:, 4 * rows_d :, :])
        order_ref, mask, tab, gain, gain_two = refs[:5]
        dattn_kernel(
            mid, own_part, got, w_p, order_ref, mask, tab, gain, w, gain_two, *refs[7:]
        )

    def dattn_kernel(
        mid, own_part, got, w_p, order_ref, mask, tab, gain, w, gain_two,
        visible_out, input_out, normed_out, triple_out, mixed_out, middle_out, normed_two_out,
    ):
        encoded = mid[...] + own_part[...] + got[...].astype(F32)
        for chip in range(chips):
            visible = encoded[chip * length : chip * length + visible_count].astype(BF)
            visible_out[chip * visible_count : (chip + 1) * visible_count, :] = visible
        projected = matmul(visible_out[...], w_p[...])
        high = projected.astype(BF)
        low = (projected - high.astype(F32)).astype(BF)
        for chip in range(chips):
            rows = slice(chip * seq_out, (chip + 1) * seq_out)
            few = slice(chip * visible_count, (chip + 1) * visible_count)
            chosen = chosen_of(order_ref, chip)
            seen = jnp.sum(chosen, axis=1, keepdims=True)
            chosen = chosen.astype(BF)
            value = matmul(chosen, high[few]) + matmul(chosen, low[few])
            value = value + (1.0 - seen) * mask[...] + tab[...]
            input_out[rows, :] = value
            normed = layer_norm(value, gain[...])
            normed_out[rows, :] = normed
            triple_d = jnp.concatenate([matmul(normed, w[i]).astype(BF) for i in range(3)], axis=1)
            triple_out[rows, :] = triple_d
            mixed_d = attend(triple_d, thin, None)
            mixed_out[rows, :] = mixed_d
            middle_d = value + matmul(mixed_d, w[3])
            middle_out[rows, :] = middle_d
            normed_two_out[rows, :] = layer_norm(middle_d, gain_two[...])

    def dattn():
        outs = (
            ((chips * visible_count, wide), BF),
            ((rows_all, thin), F32),
            ((rows_all, thin), BF),
            ((rows_all, 3 * thin), BF),
            ((rows_all, thin), BF),
            ((rows_all, thin), F32),
            ((rows_all, thin), BF),
        )
        first = (plan["norm"][0], plan["down"][0], plan.hold(plan["X3"]))
        table = plan["seq"][1]
        if not aligned:
            w_p, w = four_natural()
            args = first + (w_p, order, mask_row, table, gains[2], w, gains[3])
            return call(dattn_kernel, "dattn", args, *outs) + [w_p, w]
        near, far = (value.reshape(-1, rows_four, thin) for value in halves_in("D1"))
        out = call(
            dattn_body,
            "dattn",
            (core,) + first + (near, far, order, mask_row, table, gains[2], gains[3]),
            ((wide, thin), BF),
            ((4, thin, thin), BF),
            *outs,
            bits=1,
        )
        return out[2:] + out[:2]

    plan.kernel("dattn", ["X3", d_one], dattn)

    def halves_of(value, bit, rows):
        cut = value.reshape(-1, 2, rows, value.shape[-1])
        other = bit[0] == 1
        near, far = cut[:, 0], cut[:, 1]
        return jnp.where(other, near, far), jnp.where(other, far, near)

    def dmlp_kernel(
        bit, section_bit, mid, normed, near_w, far_w, grad_ref, out, away_out, back_out, *grads
    ):
        def up_weight(b):
            return read_whole(bit, near_w[b], far_w[b]) if aligned else near_w[b]

        def down_weight(b):
            if not aligned:
                return far_w[b]
            count = thin // rows_n // 2
            some = slice(b * count, (b + 1) * count)
            near, far = (
                jnp.concatenate([ref[v_ups + q, some] for q in range(quarters)], axis=1)
                for ref in (near_w, far_w)
            )
            return read_whole(bit, near, far)

        rows, grad = normed[...], grad_ref[...]
        total = mid[...]
        back = jnp.zeros((rows_all, thin), F32)
        for b in range(v_ups):
            w_u, w_d = up_weight(b), down_weight(b)
            value, slope_d = gelu_parts(matmul(rows, w_u))
            value = value.astype(BF)
            total = total + matmul(value, w_d)
            change = (slope_d * against_rows(grad, w_d)).astype(BF)
            back = back + against_rows(change, w_u)
            down, up = over_rows(value, grad), over_rows(rows, change)
            if aligned:
                for ref, value in zip(grads, halves_of(up, bit, rows_d)):
                    ref[b] = value.astype(BF)
                count = thin // rows_n // 2
                for ref, value in zip(grads, halves_of(down, bit, rows_n)):
                    for q in range(quarters):
                        ref[v_ups + q, b * count : (b + 1) * count] = value[
                            :, q * rows_d : (q + 1) * rows_d
                        ].astype(BF)
            else:
                grads[0][b], grads[0][v_ups + b] = up.astype(BF), down.astype(BF)
        other = section_bit[0] == 1
        near, far = total[:, : thin // 2].astype(BF), total[:, thin // 2 :].astype(BF)
        out[...] = jnp.where(other, far, near)
        away_out[...] = jnp.where(other, near, far)
        back_out[...] = back

    def dmlp():
        if aligned:
            shape = (v_ups + quarters, devices // 2, rows_d, thin)
            weights = [value.reshape(shape) for value in halves_in("D2")]
        else:
            weights = five_natural()
        shape = (v_ups + quarters, devices // 2, rows_d, thin)
        natural = (v_ups + quarters, thin, thin)
        out = call(
            dmlp_kernel,
            "dmlp",
            (
                core,
                side,
                plan["dattn"][5],
                plan["dattn"][6],
                *weights,
                plan.hold(grad_rows),
            ),
            ((rows_all, thin // 2), BF),
            ((rows_all, thin // 2), BF),
            ((rows_all, thin), F32),
            *([(shape, BF)] * 2 if aligned else [(natural, BF)]),
            bits=2,
        )
        if not aligned:
            turned = out[3][v_ups:].reshape(devices, quarters, rows_d, thin).transpose(1, 0, 2, 3)
            whole = jnp.concatenate([out[3][:v_ups].reshape(turned.shape), turned], axis=0)
            whole = whole.reshape((v_ups + quarters, devices // 2, 2, rows_d, thin))
            out = out[:3] + split(whole, core, 2)
        lead = (v_ups + quarters,) + lead_d + (rows_d, thin)
        return out[:3] + [value.reshape(lead) for value in out[3:]]

    plan.kernel("dmlp", ["dattn", d_two], dmlp)

    def five_kernel(here, got, up_out, down_out):
        for i in range(v_ups):
            up_out[:, i * thin : (i + 1) * thin] = here[i].astype(F32) + got[i].astype(F32)
        for i in range(quarters):
            down_out[i * rows_d : (i + 1) * rows_d, :] = here[v_ups + i].astype(F32) + got[
                v_ups + i
            ].astype(F32)

    def five_sum(here, got):
        if aligned:
            return call(
                five_kernel,
                "five_sum",
                (here, got),
                ((rows_d, v_ups * thin), F32),
                ((rows_n, thin), F32),
            )
        total = here.astype(F32) + got.astype(F32)
        return [
            jnp.concatenate([total[i] for i in range(v_ups)], axis=1),
            total[v_ups:].reshape(rows_n, thin),
        ]

    sum_five = scatter(
        plan, cube, "gD2", ["c"] + GD2_ORDER(z), ["dmlp"], lambda: plan["dmlp"][3:], 1, aligned, five_sum
    )

    def db1_kernel(mid, gain, back, grad_ref, w, middle_out, gain_out, mixed_out):
        change, gain_grad = norm_back(mid[...], gain[...], back[...])
        total = grad_ref[...].astype(F32) + change
        middle_out[...] = total
        gain_out[...] = gain_grad
        mixed_out[...] = against_rows(total.astype(BF), w[3]).astype(BF)

    plan.kernel(
        "db1",
        ["dmlp"],
        lambda: call(
            db1_kernel,
            "db1",
            (plan["dattn"][5], gains[3], plan.hold(plan["dmlp"][2]), grad_rows, plan["dattn"][8]),
            ((rows_all, thin), F32),
            ((1, thin), F32),
            ((rows_all, thin), BF),
        ),
    )

    def db2_kernel(
        triple_ref, grad_ref, w, start, gain, grad_mid, order_ref, w_p,
        triple_out, gain_out, mask_out, few_out, branch_out,
    ):
        gain_grad = jnp.zeros((1, thin), F32)
        mask_grad = jnp.zeros((1, thin), F32)
        for chip in range(chips):
            rows = slice(chip * seq_out, (chip + 1) * seq_out)
            parts = attend_back(triple_ref[rows, :], grad_ref[rows, :], thin, None)
            change = 0.0
            for i in range(3):
                triple_out[rows, i * thin : (i + 1) * thin] = parts[i]
                change = change + against_rows(parts[i], w[i])
            change, gain_part = norm_back(start[rows, :], gain[...], change)
            gain_grad = gain_grad + gain_part
            total = grad_mid[rows, :] + change
            chosen = chosen_of(order_ref, chip)
            seen = jnp.sum(chosen, axis=1, keepdims=True)
            mask_grad = mask_grad + jnp.sum((1.0 - seen) * total, axis=0, keepdims=True)
            few = over_rows(chosen.astype(BF), total.astype(BF)).astype(BF)
            few_out[chip * visible_count : (chip + 1) * visible_count, :] = few
        gain_out[...] = gain_grad
        mask_out[...] = mask_grad
        branch = against_rows(few_out[...], w_p[...])
        gap = jnp.zeros((length - visible_count, wide), F32)
        branch_out[...] = jnp.concatenate(
            [
                piece
                for chip in range(chips)
                for piece in (branch[chip * visible_count : (chip + 1) * visible_count], gap)
            ],
            axis=0,
        ).astype(BF)

    plan.kernel(
        "db2",
        ["db1"],
        lambda: call(
            db2_kernel,
            "db2",
            (
                plan["dattn"][3],
                plan.hold(plan["db1"][2]),
                plan["dattn"][8],
                plan["dattn"][1],
                gains[2],
                plan["db1"][0],
                order,
                plan["dattn"][7],
            ),
            ((rows_all, 3 * thin), BF),
            ((1, thin), F32),
            ((1, thin), F32),
            ((chips * visible_count, thin), BF),
            ((own, wide), BF),
        ),
    )
    plan.send("Y1", ["db2"], cube, "y", lambda: plan["db2"][4])

    def db3_kernel(bit, change, normed, grad_mid, mix, few, seen_rows, *grads):
        def put(value, at, rows):
            if aligned:
                for ref, side_value in zip(grads, halves_of(value, bit, rows)):
                    ref[:, at : at + rows, :] = side_value.astype(BF)
            elif rows == rows_d:
                grads[0][at // rows_d] = value.astype(BF)
            else:
                grads[1][...] = value.astype(BF)

        for i in range(3):
            put(over_rows(normed[...], change[:, i * thin : (i + 1) * thin]), i * rows_d, rows_d)
        put(over_rows(mix[...], grad_mid[...].astype(BF)), 3 * rows_d, rows_d)
        put(over_rows(seen_rows[...], few[...]), 4 * rows_d, rows_p)

    def db3():
        shape = (devices // 2, rows_four, thin)
        natural = [((4, thin, thin), BF), ((wide, thin), BF)]
        out = call(
            db3_kernel,
            "db3",
            (
                core,
                plan.hold(plan["db2"][0]),
                plan["dattn"][2],
                plan["db1"][0],
                plan["dattn"][4],
                plan["db2"][3],
                plan["dattn"][0],
            ),
            *([(shape, BF)] * 2 if aligned else natural),
            bits=1,
        )
        if not aligned:
            blocks = out[0].reshape(4, devices, rows_d, thin).transpose(1, 0, 2, 3)
            whole = jnp.concatenate(
                [blocks.reshape(devices, -1, thin), out[1].reshape(devices, rows_p, thin)], axis=1
            )
            out = split(whole.reshape(devices // 2, 2, rows_four, thin), core, 1)
        return [value.reshape(lead_d + (rows_four, thin)) for value in out]

    plan.kernel("db3", ["db2"], db3)

    def four_kernel(here, got, qkv_out, out_out, proj_out):
        total = here[...].astype(F32) + got[...].astype(F32)
        for i in range(3):
            qkv_out[:, i * thin : (i + 1) * thin] = total[i * rows_d : (i + 1) * rows_d]
        out_out[...] = total[3 * rows_d : 4 * rows_d]
        proj_out[...] = total[4 * rows_d :]

    def four_sum(here, got):
        if aligned:
            return call(
                four_kernel,
                "four_sum",
                (here, got),
                ((rows_d, 3 * thin), F32),
                ((rows_d, thin), F32),
                ((rows_p, thin), F32),
            )
        total = here.astype(F32) + got.astype(F32)
        cuts = [total[i * rows_d : (i + 1) * rows_d] for i in range(4)]
        return [jnp.concatenate(cuts[:3], axis=1), cuts[3], total[4 * rows_d :]]

    sum_four = scatter(
        plan, cube, "gD1", ["c"] + GD1_ORDER(z), ["db3"], lambda: plan["db3"], 0, aligned, four_sum
    )

    def emlp_kernel(near, far, w_d, slo, w_u, change_out, part_out, away_out):
        grad = jnp.concatenate([near[...], far[...]], axis=0)
        total = 0.0
        for b in range(ups):
            cols = slice(b * half, (b + 1) * half)
            change = sum(
                against_rows(grad[:, i * half : (i + 1) * half], w_d[i, cols]) for i in range(2)
            )
            change = (slo[:, cols] * change).astype(BF)
            change_out[:, cols] = change
            total = total + against_rows(change, w_u[b])
        part_out[...] = total[:own]
        away_out[...] = total[own:].astype(BF)

    plan.kernel(
        "emlp",
        ["Y1"],
        lambda: call(
            emlp_kernel,
            "emlp",
            (plan["db2"][4], plan.hold(plan["Y1"]), w_three(), plan["up"][1], w_two()),
            ((every, mlp), BF),
            ((own, wide), F32),
            ((own, wide), BF),
        ),
    )
    plan.send("Y2", ["emlp"], cube, "y", lambda: plan["emlp"][2])

    def emlpg_kernel(bit, near, far, hid, norm_near, norm_far, change, *grads):
        grad = jnp.concatenate([near[...], far[...]], axis=0)
        rows = jnp.concatenate([norm_near[...], norm_far[...]], axis=0)
        for i in range(2):
            value = over_rows(hid[...], grad[:, i * half : (i + 1) * half])
            if aligned:
                for ref, cut in zip(grads[:2], halves_of(value, bit, rows_m)):
                    ref[i] = cut.astype(BF)
            else:
                grads[0][i] = value.astype(BF)
        for b in range(ups):
            value = over_rows(rows, change[:, b * half : (b + 1) * half])
            if aligned:
                for ref, cut in zip(grads[2:], halves_of(value, bit, rows_e)):
                    ref[b] = cut.astype(BF)
            else:
                grads[1][b] = value.astype(BF)

    def emlpg():
        three, two = (2, group // 2, rows_m, half), (ups, group, rows_e, half)
        out = call(
            emlpg_kernel,
            "emlpg",
            (
                core,
                plan["db2"][4],
                plan["Y1"],
                plan["up"][0],
                plan["norm"][1],
                plan["X2"],
                plan.hold(plan["emlp"][0]),
            ),
            *(
                [(three, BF)] * 2 + [(two, BF)] * 2
                if aligned
                else [((2, mlp, half), BF), ((ups, wide, half), BF)]
            ),
            bits=1,
        )
        if not aligned:
            out = split(out[0].reshape(2, group // 2, 2, rows_m, half), core, 2) + split(
                out[1].reshape(ups, group, 2, rows_e, half), core, 2
            )
        shapes = [(2,) + lead_e + (rows_m, half)] * 2 + [(ups, 2) + lead_e + (rows_e, half)] * 2
        return [value.reshape(shape) for value, shape in zip(out, shapes)]

    plan.kernel("emlpg", ["emlp"], emlpg)

    def three_kernel(here, got, out):
        for i in range(2):
            out[:, i * half : (i + 1) * half] = here[i].astype(F32) + got[i].astype(F32)

    def three_sum(here, got):
        if aligned:
            return call(three_kernel, "three_sum", (here, got), ((rows_m, wide), F32))
        total = here.astype(F32) + got.astype(F32)
        return [jnp.concatenate([total[i] for i in range(2)], axis=1)]

    def two_kernel(bit, here, got, here_out, away_out):
        for b in range(ups):
            for ref, which in ((here_out, bit[0]), (away_out, 1 - bit[0])):
                total = here[b, which].astype(F32) + got[b, which].astype(F32)
                ref[b] = total.astype(ref.dtype)

    def two_sum(here, got):
        if aligned:
            shape = (ups, rows_e, half)
            out = call(
                two_kernel, "two_sum", (side, here, got), (shape, F32), (shape, BF), bits=1
            )
            return [None] + out
        far, near = split(here.astype(F32) + got.astype(F32), side, 1)
        return [None, near, far.astype(BF)]

    sum_three = scatter(
        plan, cube, "gE3", ["c"] + GE3_ORDER(z), ["emlpg"], lambda: plan["emlpg"][:2], 1, aligned, three_sum
    )
    sum_two = scatter(
        plan, cube, "gE2", ["c"] + GE2_ORDER(z), ["emlpg"], lambda: plan["emlpg"][2:], 2, aligned, two_sum
    )

    def enb_kernel(mid, gain, own_part, got, near, middle_out, gain_out, branch_out):
        change, gain_grad = norm_back(mid[...], gain[...], own_part[...] + got[...].astype(F32))
        total = near[...].astype(F32) + change
        middle_out[...] = total
        gain_out[...] = gain_grad
        branch_out[...] = total.astype(BF)

    plan.kernel(
        "enb",
        ["Y2"],
        lambda: call(
            enb_kernel,
            "enb",
            (plan["norm"][0], gains[1], plan["emlp"][1], plan.hold(plan["Y2"]), plan["db2"][4]),
            ((own, wide), F32),
            ((1, wide), F32),
            ((own, wide), BF),
        ),
    )
    plan.send("Y3", ["enb"], cube, "y", lambda: plan["enb"][2])

    def eab_kernel(bit, near, far, mix, triple_ref, normed, w, part_out, away_out, *grads):
        def put(value, at):
            if aligned:
                for ref, side_value in zip(grads, halves_of(value, bit, rows_e)):
                    ref[at] = side_value.astype(BF)
            else:
                grads[0][at] = value.astype(BF)

        grad = jnp.concatenate([near[...], far[...]], axis=0)
        put(
            jnp.concatenate(
                [over_rows(mix[...], grad[:, i * half : (i + 1) * half]) for i in range(2)], axis=0
            ),
            3,
        )
        grad_mixed = sum(
            against_rows(grad[:, i * half : (i + 1) * half], w[3, i * half : (i + 1) * half])
            for i in range(2)
        ).astype(BF)
        bias = bias_of(own, length, seq_in + 1)
        pieces = [
            attend_back(triple_ref[i : i + own, :], grad_mixed[i : i + own], half, bias)
            for i in range(0, every, own)
        ]
        total = 0.0
        for i in range(3):
            change = jnp.concatenate([piece[i] for piece in pieces], axis=0)
            put(over_rows(normed[...], change), i)
            total = total + against_rows(change, w[i])
        part_out[...] = total[:own]
        away_out[...] = total[own:].astype(BF)

    def eab():
        shape = (4, group, rows_e, half)
        out = call(
            eab_kernel,
            "eab",
            (
                core,
                plan["enb"][2],
                plan.hold(plan["Y3"]),
                plan["attn"][2],
                plan["attn"][1],
                plan["attn"][0],
                w_one(),
            ),
            ((own, wide), F32),
            ((own, wide), BF),
            *([(shape, BF)] * 2 if aligned else [((4, wide, half), BF)]),
            bits=1,
        )
        if not aligned:
            out = out[:2] + split(out[2].reshape(4, group, 2, rows_e, half), core, 2)
        lead = (4, 2) + lead_e + (rows_e, half)
        return out[:2] + [value.reshape(lead) for value in out[2:]]

    plan.kernel("eab", ["Y3"], eab)

    def one_kernel(bit, here, got, out_out, here_out, away_out):
        for i in range(2):
            out_out[:, i * half : (i + 1) * half] = here[3, i].astype(F32) + got[3, i].astype(F32)
        for i in range(3):
            for ref, which in ((here_out, bit[0]), (away_out, 1 - bit[0])):
                total = here[i, which].astype(F32) + got[i, which].astype(F32)
                ref[i] = total.astype(ref.dtype)

    def one_sum(here, got):
        if aligned:
            return call(
                one_kernel,
                "one_sum",
                (side, here, got),
                ((rows_e, wide), F32),
                ((3, rows_e, half), F32),
                ((3, rows_e, half), BF),
                bits=1,
            )
        total = here.astype(F32) + got.astype(F32)
        far, near = split(total[:3], side, 1)
        return [jnp.concatenate([total[3, i] for i in range(2)], axis=1), near, far.astype(BF)]

    sum_one = scatter(
        plan, cube, "gE1", ["c"] + GE1_ORDER(z), ["eab"], lambda: plan["eab"][2:], 2, aligned, one_sum
    )
    plan.send("Y4", ["eab"], cube, "y", lambda: plan["eab"][1])

    def elast_kernel(
        bit, seq, gain, own_part, got, grad_mid, hot, gain_two, mask_part, gain_three, gain_four,
        near_out, far_out, small, rows_ref,
    ):
        change, gain_grad = norm_back(seq[:own], gain[...], own_part[...] + got[...].astype(F32))
        total = grad_mid[...] + change
        for chip in range(chips):
            at = chip * length
            rows_ref[chip * seq_in : chip * seq_in + 1, :] = total[
                at + visible_count : at + visible_count + 1
            ]
            rows_ref[chip * seq_in + 1 : (chip + 1) * seq_in, :] = total[at : at + visible_count]
        near, far = rows_ref[:, :half], rows_ref[:, half:]
        near_out[...] = jnp.where(bit[0] == 1, far, near)
        far_out[...] = jnp.where(bit[0] == 1, near, far).astype(BF)
        small[...] = jnp.zeros_like(small)
        class_row = jnp.zeros((1, wide), F32)
        sensor_rows = jnp.zeros((sensor_count, wide), F32)
        for chip in range(chips):
            at = chip * length
            class_row = class_row + total[at + seq_in : at + seq_in + 1]
            rows = jnp.sum(total[at : at + length], axis=0, keepdims=True)
            sensor_rows = sensor_rows + hot[:, chip : chip + 1] * rows
        small[:sensor_count, :] = sensor_rows
        at = sensor_count
        for row in (class_row, gain_grad, gain_two[...]):
            small[at : at + 1, :] = row
            at += 1
        for row in (mask_part, gain_three, gain_four):
            small[at : at + 1, :thin] = row[...]
            at += 1

    plan.kernel(
        "elast",
        ["Y4"],
        lambda: call(
            elast_kernel,
            "elast",
            (
                side,
                plan["seq"][0],
                gains[0],
                plan["eab"][0],
                plan.hold(plan["Y4"]),
                plan["enb"][0],
                onehot[:chips].astype(F32).T,
                plan["enb"][1],
                plan["db2"][2],
                plan["db2"][1],
                plan["db1"][1],
            ),
            ((chips * seq_in, half), F32),
            ((chips * seq_in, half), BF),
            ((-(-(sensor_count + 6) // 8) * 8, wide), F32),
            bits=1,
            scratch=[pltpu.VMEM((chips * seq_in, wide), F32)],
        ),
    )

    def small_kernel(own_part, got, class_out, sensor_out, *outs):
        total = own_part[...] + got[...]
        sensor_out[...] = total[:sensor_count]
        class_out[...] = total[sensor_count : sensor_count + 1]
        for i, ref in enumerate(outs):
            at = sensor_count + 1 + i
            ref[...] = total[at : at + 1, : ref.shape[1]]

    before = lambda: plan["elast"][2]
    needs = ["elast"]
    steps = ["y", *z[::-1], "x", "c"]
    for i, step in enumerate(steps):
        plan.send(f"s{i}", needs, cube, step, before)

        def finish(i=i, before=before):
            got = plan.hold(plan[f"s{i}"])
            if i < len(steps) - 1:
                return [before() + got]
            return call(
                small_kernel,
                "small_sum",
                (before(), got),
                ((1, wide), F32),
                ((sensor_count, wide), F32),
                ((1, wide), F32),
                ((1, wide), F32),
                ((1, thin), F32),
                ((1, thin), F32),
                ((1, thin), F32),
            )

        plan.kernel(f"sm{i}", [f"s{i}"], finish)
        before, needs = (lambda i=i: plan[f"sm{i}"][0]), [f"sm{i}"]
    small = needs[0]

    def beside_kernel(bit, here, got, out):
        count, _, size = here.shape
        first = bit[0] == 0
        for i in range(count):
            near, far = here[i], got[i].astype(F32)
            for j, value in enumerate((jnp.where(first, near, far), jnp.where(first, far, near))):
                at = place_of(i, j, count)
                out[:, at * size : (at + 1) * size] = value

    def place_of(i, j, count):
        return 2 * i + j if count == 3 else j * count + i

    def crossed(name, start):
        plan.send(f"{name}.w", [start], cube, "y", lambda: plan[start][2])

        def finish():
            here, got = plan[start][1], plan.hold(plan[f"{name}.w"])
            shape = (rows_e, 2 * here.shape[0] * half)
            return call(beside_kernel, "beside", (side, here, got), (shape, F32), bits=1)

        plan.kernel(f"{name}.mw", [f"{name}.w"], finish)

    crossed("gE1", sum_one)
    crossed("gE2", sum_two)

    def stacked_kernel(bit, here, got, out):
        rows = here.shape[0]
        near, far = here[...], got[...].astype(here.dtype)
        out[:rows] = jnp.where(bit[0] == 0, near, far)
        out[rows:] = jnp.where(bit[0] == 0, far, near)

    def halves(name, start):
        plan.send(name, [start], cube, "y", lambda: plan[start][1])

        def finish():
            here = plan[start][0]
            shape = (2 * here.shape[0], here.shape[1])
            got = plan.hold(plan[name])
            return call(stacked_kernel, "stacked", (side, here, got), (shape, here.dtype), bits=1)

        plan.kernel(f"{name}m", [name], finish)

    halves("blk", "dmlp")
    halves("tok", "elast")
    plan.run(ORDER)

    rest = [value[0] if value.shape[0] == 1 else value for value in plan[small]]
    return (
        plan["blkm"][0],
        plan["tokm"][0],
        plan["gE1.mw"][0],
        plan[sum_one][0],
        plan["gE2.mw"][0],
        plan[sum_three][0],
        plan[sum_four][2],
        plan[sum_four][0],
        plan[sum_four][1],
        plan[sum_five][0],
        plan[sum_five][1],
    ) + tuple(rest)


def solution(mesh):
    every = P(("section", "dp"), None)
    rows = P("dp", None)
    in_specs = (
        rows,
        rows,
        P("dp"),
        P(),
        P(),
        P(),
        every,
        every,
        P(),
        every,
        every,
        every,
        P(),
        P(),
        every,
        every,
        P(),
        every,
        every,
        rows,
    )
    out_specs = (P("dp", "section"),) * 2 + (every,) * 9 + (P(),) * 7
    return jax.shard_map(local, mesh=mesh, in_specs=in_specs, out_specs=out_specs, check_vma=False)
```

```python
import math

import jax
import jax.numpy as jnp
from jax import lax
from jax.experimental import pallas as pl
from jax.experimental.pallas import tpu as pltpu
from jax.sharding import PartitionSpec as P

HEAD_DIM = 64
PAIR = 2 * HEAD_DIM
BF = jnp.bfloat16
F32 = jnp.float32
SCALE = HEAD_DIM ** (-0.5)


def matmul(left, right):
    return jnp.dot(left, right, preferred_element_type=F32)


def against_rows(left, right):
    return lax.dot_general(left, right, (((1,), (1,)), ((), ())), preferred_element_type=F32)


def over_rows(left, right):
    return lax.dot_general(left, right, (((0,), (0,)), ((), ())), preferred_element_type=F32)


def normal_parts(rows):
    mean = jnp.mean(rows, axis=-1, keepdims=True)
    centred = rows - mean
    spread = jnp.mean(centred * centred, axis=-1, keepdims=True)
    inverse = lax.rsqrt(spread + 1e-05)
    return centred * inverse, inverse


def layer_norm(rows, gain):
    return (normal_parts(rows)[0] * gain).astype(BF)


def norm_back(rows, gain, grad):
    hat, inverse = normal_parts(rows)
    scaled = grad * gain
    out = inverse * (
        scaled
        - jnp.mean(scaled, axis=-1, keepdims=True)
        - hat * jnp.mean(scaled * hat, axis=-1, keepdims=True)
    )
    return out, jnp.sum(grad * hat, axis=0, keepdims=True)


def gelu_parts(value):
    square = value * value
    flat = jnp.tanh(0.7978845608028654 * (value + 0.044715 * value * square))
    side = 0.5 * (1.0 + flat)
    slope = side + 0.5 * value * (1.0 - flat * flat) * (
        0.7978845608028654 + 3.0 * 0.044715 * 0.7978845608028654 * square
    )
    return value * side, slope


def position_table(count, width):
    half = width // 2
    place = jnp.arange(count, dtype=F32)[:, None]
    rate = jnp.exp(jnp.arange(half, dtype=F32) * (-math.log(10000.0) / half))
    angle = place * rate[None, :]
    return jnp.concatenate([jnp.sin(angle), jnp.cos(angle)], axis=1)


def shares_of(key, query, bias):
    scores = against_rows(key, query)
    if bias is not None:
        scores = scores + jnp.concatenate([bias, bias], axis=1)
    raised = jnp.exp(scores - jnp.max(scores, axis=0, keepdims=True))
    return raised * (1.0 / jnp.sum(raised, axis=0, keepdims=True))


def apart(value):
    first = lax.broadcasted_iota(jnp.int32, value.shape, 1) < HEAD_DIM
    none = jnp.zeros_like(value)
    return jnp.concatenate([jnp.where(first, value, none), jnp.where(first, none, value)], axis=0)


def together(value):
    rows = value.shape[0] // 2
    first = lax.broadcasted_iota(jnp.int32, (rows, value.shape[1]), 1) < HEAD_DIM
    return jnp.where(first, value[:rows], value[rows:])


def bias_of(length, seq, valid):
    if length == valid:
        return None
    key = lax.broadcasted_iota(jnp.int32, (length, length), 0)
    query = lax.broadcasted_iota(jnp.int32, (length, length), 1)
    kept = jnp.zeros((length, length), jnp.bool_)
    for start in range(0, length, seq):
        kept = kept | (
            (key >= start) & (key < start + valid) & (query >= start) & (query < start + seq)
        )
    return jnp.where(kept, 0.0, -1e30)


def attend(triple, width, bias):
    out = []
    for at in range(0, width, PAIR):
        query, key, value = (triple[:, i * width + at : i * width + at + PAIR] for i in range(3))
        shares = shares_of(key, apart(query) * SCALE, bias).astype(BF)
        out.append(together(over_rows(shares, value)).astype(BF))
    return jnp.concatenate(out, axis=1)


def attend_back(triple, grad_mixed, width, bias):
    out = ([], [], [])
    for at in range(0, width, PAIR):
        query, key, value = (triple[:, i * width + at : i * width + at + PAIR] for i in range(3))
        queries, grads = apart(query) * SCALE, apart(grad_mixed[:, at : at + PAIR])
        exact = shares_of(key, queries, bias)
        grad_shares = against_rows(value, grads)
        mean = jnp.sum(grad_shares * exact, axis=0, keepdims=True)
        grad_scores = (exact * (grad_shares - mean)).astype(BF)
        out[0].append((together(over_rows(grad_scores, key)) * SCALE).astype(BF))
        out[1].append(matmul(grad_scores, queries).astype(BF))
        out[2].append(matmul(exact.astype(BF), grads).astype(BF))
    return [jnp.concatenate(piece, axis=1) for piece in out]


def call(body, args, *outs, bits=0, scratch=(), space=pltpu.VMEM):
    size = sum(math.prod(shape) * jnp.dtype(dtype).itemsize for shape, dtype in outs)
    size += sum(value.size * value.dtype.itemsize for value in args[bits:])
    count = len(args)
    earlier = [] if Plan.earlier is None else [Plan.earlier]

    def ordered(*refs):
        body(*refs[:count], *refs[count + len(earlier) :])

    run = pl.pallas_call(
        ordered,
        out_shape=[jax.ShapeDtypeStruct(shape, dtype) for shape, dtype in outs],
        in_specs=[pl.BlockSpec(memory_space=pltpu.SMEM)] * bits
        + [pl.BlockSpec(memory_space=space)] * (count - bits)
        + [pl.BlockSpec(memory_space=pl.ANY)] * len(earlier),
        cost_estimate=pl.CostEstimate(
            flops=COSTS.get(Plan.now, 10**10), bytes_accessed=1000, transcendentals=0
        ),
        compiler_params=pltpu.CompilerParams(
            vmem_limit_bytes=size + size // 4 + ((10 << 20) if size > (6 << 20) else (2 << 20))
        ),
        scratch_shapes=list(scratch),
    )
    return list(run(*args, *earlier))


def after(value, *others):
    return lax.optimization_barrier((value,) + others)[0]


def flat(value, place, split):
    rest = value.shape[place + split : -1]
    head = (math.prod(value.shape[:place]),) + (2,) * split
    return value.reshape(head + (math.prod(rest), value.shape[-1]))


def merge_kernel(bit, own, got, out):
    def step(i, _):
        out[i, bit[0]] = own[i]
        out[i, 1 - bit[0]] = got[i]
        return 0

    lax.fori_loop(0, own.shape[0], step, 0)


def merged(own, got, bit, place, aligned):
    if not aligned:
        mine = bit[0] == 0
        return jnp.where(mine, jnp.stack([own, got], place), jnp.stack([got, own], place))
    left, right = flat(own, place, False), flat(got, place, False)
    shape = left.shape[:1] + (2,) + left.shape[1:]
    (out,) = call(merge_kernel, (bit, left, right), (shape, own.dtype), bits=1)
    return out.reshape(own.shape[:place] + (2,) + own.shape[place:])


def copy_kernel(got, out):
    out[...] = got[...]


def far_kernel(bit, low, own, near_got, far_got, out):
    middle = bit[0] != low[0]

    def step(i, _):
        out[i, bit[0]] = own[i]
        out[i, 1 - bit[0]] = jnp.where(middle, near_got[i], far_got[i])
        return 0

    lax.fori_loop(0, own.shape[0], step, 0)


def add_kernel(here, got, out):
    def step(i, _):
        out[i] = here[i] + got[i]
        return 0

    lax.fori_loop(0, here.shape[0], step, 0)


def split_kernel(bit, here, got, away_out, here_out):
    def step(i, _):
        for out, side in ((away_out, 1 - bit[0]), (here_out, bit[0])):
            out[i] = here[i, side] + got[i, side]
        return 0

    lax.fori_loop(0, here.shape[0], step, 0)


def split_sum(here, got, bit, place, aligned):
    rest = here.shape[:place] + here.shape[place + 1 :]
    if not aligned:
        return split(here + got, bit, place)
    left, right = flat(here, place, True), flat(got, place, True)
    shape = left.shape[:1] + left.shape[2:]
    parts = call(
        split_kernel, (bit, left, right), (shape, BF), (shape, BF), bits=1
    )
    return [value.reshape(rest) for value in parts]


def split(total, bit, place):
    return [
        lax.dynamic_index_in_dim(total, which, place, keepdims=False)
        for which in (1 - bit[0], bit[0])
    ]


class Cube:
    def __init__(self):
        self.names = [
            (axis, bit)
            for axis in ("section", "dp")
            for bit in reversed(range((lax.axis_size(axis) - 1).bit_length()))
        ]
        self.bits = {
            (axis, bit): ((lax.axis_index(axis) >> bit) & 1).reshape(1)
            for axis, bit in self.names
        }
        depth = len(self.names) - 3
        self.of = {"c": ("dp", 0), "x": ("dp", 1), "y": ("section", 0)}
        self.of.update({f"z{i}": ("dp", 2 + i) for i in range(depth)})
        self.z = [f"z{i}" for i in range(depth)]
        self.line = {"zB": {1: 2, 2: 1}, "zC": {1: 0, 2: 3}, "zD": {0: 1, 3: 2}}

    def swap(self, value, step):
        if step in self.line:
            hops = self.line[step]
            places = [(i, i >> 2) for i in range(lax.axis_size("dp"))]
            route = [(i, i + 4 * (hops[z] - z)) for i, z in places if z in hops]
            return lax.ppermute(value, "dp", route)
        axis, bit = self.of[step]
        route = [(i, i ^ (1 << bit)) for i in range(lax.axis_size(axis))]
        return lax.ppermute(value, axis, route)

    def bit(self, step):
        return self.bits[self.of[step]]

    def place(self, held, step):
        at = self.names.index(self.of[step])
        return sum(1 for other in held if self.names.index(self.of[other]) < at)


class Plan:
    now = earlier = None

    def __init__(self):
        self.steps, self.value, self.token = {}, {}, None

    def add(self, name, needs, body):
        self.steps[name] = (needs, body)

    def hold(self, value):
        return value if self.token is None else after(value, self.token)

    def run(self, order):
        left, names = dict(self.steps), list(self.steps)
        wanted = [names[i] for i in order] if len(order) == len(names) else names
        while left:
            name = next(
                n for n in wanted if n in left and all(d in self.value for d in left[n][0])
            )
            Plan.now = names.index(name)
            with jax.named_scope(name):
                self.value[name] = left.pop(name)[1]()

    def __getattr__(self, name):
        return self.value[name]

    def kernel(self, name, needs, body):
        def step():
            Plan.earlier = self.token
            out = body()
            Plan.earlier = None
            self.token = min((v for v in out if v is not None), key=lambda value: value.size)
            return out

        self.add(name, needs, step)

    def send(self, name, needs, cube, step, value):
        self.add(name, needs, lambda: cube.swap(self.hold(value()), step))


def gather(plan, cube, name, order, needs, piece, lead, aligned):
    held = []
    before = piece
    for step in order:
        source = (lambda at: lambda: plan.value[at][0])(needs[0]) if step == "zC" else before
        plan.send(f"{name}.{step}", needs, cube, step, source)

        def finish(step=step, before=before, held=tuple(held)):
            got = plan.value[f"{name}.{step}"]
            if step == "zB":
                block = flat(got, got.ndim - 2, False)
                (out,) = call(copy_kernel, (block,), (block.shape, got.dtype))
                return [out.reshape(got.shape)]
            if step == "zC":
                own = before()
                place = lead + cube.place(held, "z1")
                cut = [
                    flat(value, place, False)
                    for value in (own, plan.value[f"{name}.mzB"][0], got)
                ]
                shape = cut[0].shape[:1] + (2,) + cut[0].shape[1:]
                bits = (cube.bit("z1"), cube.bit("z0"))
                (out,) = call(far_kernel, bits + tuple(cut), (shape, own.dtype), bits=2)
                return [out.reshape(own.shape[:place] + (2,) + own.shape[place:])]
            place = lead + cube.place(held, step)
            return [merged(before(), got, cube.bit(step), place, aligned)]

        needs = [f"{name}.m{step}"]
        plan.kernel(needs[0], [f"{name}.{step}"], finish)
        if step != "zB":
            before = (lambda at: lambda: plan.value[at][0])(needs[0])
            held.append("z1" if step == "zC" else step)
    return needs[0]


def scatter(plan, cube, name, order, needs, cut, lead, aligned, last):
    bit_of = {"zC": "z1"}
    held = [bit_of.get(step, step) for step in order if step != "zB"]
    held = sorted(held, key=lambda step: cube.names.index(cube.of[step]))
    before = cut
    for index, step in enumerate(order):
        hop = "zD" if step == "zC" else step
        plan.send(f"{name}.{step}", needs, cube, hop, lambda before=before: before()[0])
        held = [other for other in held if other != bit_of.get(step, step)]
        follow = order[index + 1] if held else None

        def finish(step=step, before=before, follow=follow, held=tuple(held)):
            got = plan.value[f"{name}.{step}"]
            if step == "zC":
                far, near = before()
                left, right = flat(far, lead, False), flat(got, lead, False)
                (out,) = call(add_kernel, (left, right), (left.shape, BF))
                return [out.reshape(far.shape), near]
            if follow is None:
                return last(before()[1], got)
            dim = bit_of.get(follow, follow)
            place = lead + cube.place(held, dim)
            return split_sum(before()[1], got, cube.bit(dim), place, aligned)

        needs = [f"{name}.a{step}"]
        plan.kernel(needs[0], [f"{name}.{step}"], finish)
        before = (lambda at: lambda: plan.value[at])(needs[0])
    return needs[0]


def blocks_of(shard, width):
    return [shard[..., i : i + width] for i in range(0, shard.shape[-1], width)]

def along(z, letters):
    ways = {"z": z, "r": z[::-1], "Z": z, "R": z[::-1]}
    if len(z) == 2:
        ways["Z"], ways["R"] = ["z0", "zB", "zC"], ["zC", "zB", "z0"]
    return [step for letter in letters for step in ways.get(letter, [letter])]


WAYS = ("Zxc", "Zxc", "xZc", "Zxyc", "Zxyc")
BACK = ("cxR", "cRx", "cxr", "cyxR", "cyxR")
ORDER = (
    0, 33, 1, 23, 45, 34, 35, 2, 3, 13, 24, 46, 47, 36, 25, 37, 4, 5, 14, 48, 49, 15, 38, 39, 6, 26, 7,
    27, 50, 51, 16, 17, 40, 41, 8, 9, 18, 28, 29, 52, 19, 53, 42, 43, 30, 31, 57, 10, 11, 44, 32, 20,
    21, 12, 58, 59, 22, 54, 55, 60, 61, 62, 63, 56, 64, 65, 79, 80, 81, 82, 83, 66, 67, 144, 95, 96, 97,
    106, 84, 98, 68, 69, 107, 145, 108, 99, 100, 116, 85, 117, 118, 109, 110, 119, 120, 101, 102, 111,
    112, 70, 71, 121, 128, 122, 103, 104, 86, 87, 129, 130, 72, 146, 113, 73, 105, 131, 132, 123, 124,
    147, 114, 88, 89, 133, 134, 74, 75, 115, 142, 125, 126, 135, 136, 143, 90, 91, 137, 138, 127, 76,
    77, 140, 92, 93, 139, 141, 78, 94,
)
COSTS = {
    0: 1000000000, 4: 3000000000, 6: 3000000000, 16: 1000, 48: 1000000000, 66: 1000000000, 68:
    3000000000, 70: 3000000000, 78: 1000000000, 80: 3000000000, 86: 1000000000, 94: 3000000000, 99:
    1000, 105: 3000000000, 111: 1000, 115: 1000000000, 116: 1000000000, 117: 1000000000, 121:
    1000000000, 139: 1000,
}


def local(
    tokens,
    patch_order,
    sensor_tag,
    class_token,
    sensor_table,
    enc_gain_one,
    enc_qkv,
    enc_out,
    enc_gain_two,
    enc_up,
    enc_down,
    dec_proj,
    mask_token,
    dec_gain_one,
    dec_qkv,
    dec_out,
    dec_gain_two,
    dec_up,
    dec_down,
    out_grad,
):
    cube, plan = Cube(), Plan()
    section = lax.axis_index("section")
    sections = lax.axis_size("section")
    group = lax.axis_size("dp")
    devices = sections * group
    wide = tokens.shape[1]
    thin = out_grad.shape[1]
    half = wide // sections
    mlp = enc_up.shape[1] // sections
    ups = mlp // half
    rows_e, rows_m = enc_qkv.shape[0], enc_down.shape[0]
    rows_p, rows_d, rows_n = dec_proj.shape[0], dec_qkv.shape[0], dec_down.shape[0]
    rows_four = 4 * rows_d + rows_p
    v_ups = dec_up.shape[1] // thin
    quarters = rows_n // rows_d
    chips_all = patch_order.shape[0]
    chips = chips_all // sections
    seq_in = tokens.shape[0] // chips_all
    seq_out = patch_order.shape[1]
    visible_count = seq_in - 1
    sensor_count = sensor_table.shape[0]
    length = -(-(seq_in + 1) // 8) * 8
    own = chips * length
    every = sections * own
    rows_all = chips * seq_out
    aligned = rows_d % 16 == 0 and rows_e % 8 == 0
    side, core = cube.bit("y"), cube.bit("c")
    lead_d, lead_e = (2,) * (len(cube.names) - 1), (2,) * (len(cube.names) - 2)

    def part(value, which, axis):
        size = value.shape[axis] // sections
        return lax.dynamic_slice_in_dim(value, which * size, size, axis=axis)

    def mine_first(value):
        return jnp.concatenate([part(value, section, 0), part(value, 1 - section, 0)], axis=0)

    gains = [
        gain.astype(F32)[None, :]
        for gain in (enc_gain_one, enc_gain_two, dec_gain_one, dec_gain_two)
    ]
    order = part(patch_order, section, 0)[:, :visible_count]
    grad_rows = part(out_grad, section, 0)
    mask_row = mask_token.astype(F32)[None, :]
    tags = mine_first(sensor_tag)
    onehot = tags[:, None] == jnp.arange(sensor_count, dtype=jnp.int32)[None, :]

    def pack_kernel(bit, *refs):
        far_refs, outs, near_refs, sems = refs[:9], refs[9:15], refs[15:24], refs[24]
        copies = [
            pltpu.make_async_copy(far, near, sems.at[i])
            for i, (far, near) in enumerate(zip(far_refs, near_refs))
        ]
        for copy in copies:
            copy.start()
        for copy in copies:
            copy.wait()
        qkv, out, up, down, proj, qkv_d, out_d, up_d, down_d = near_refs
        away, mine, outs_out, three, four, five = outs
        other = bit[0] == 1
        for i in range(3 + ups):
            from_ref, at = (qkv, i * wide) if i < 3 else (up, (i - 3) * half)
            step = half if i < 3 else mlp
            near, far = (from_ref[:, at + j * step : at + j * step + half] for j in range(2))
            mine[i] = jnp.where(other, far, near)
            away[i] = jnp.where(other, near, far)
        for i in range(2):
            outs_out[0, i] = out[:, i * half : (i + 1) * half]
            three[i] = down[:, i * half : (i + 1) * half]
        for i in range(3):
            four[i * rows_d : (i + 1) * rows_d, :] = qkv_d[:, i * thin : (i + 1) * thin]
        four[3 * rows_d : 4 * rows_d, :] = out_d[...]
        four[4 * rows_d :, :] = proj[...]
        for i in range(v_ups):
            five[i] = up_d[:, i * thin : (i + 1) * thin]
        for i in range(quarters):
            five[v_ups + i] = down_d[i * rows_d : (i + 1) * rows_d, :]

    table = position_table(seq_out, thin)

    def pack():
        if aligned:
            return call(
                pack_kernel,
                (after(side, table), enc_qkv, enc_out, enc_up, enc_down, dec_proj, dec_qkv, dec_out, dec_up, dec_down),
                ((3 + ups, rows_e, half), BF),
                ((3 + ups, rows_e, half), BF),
                ((1, 2, rows_e, half), BF),
                ((2, rows_m, half), BF),
                ((rows_four, thin), BF),
                ((v_ups + quarters, rows_d, thin), BF),
                bits=1,
                space=pltpu.HBM,
                scratch=[
                    pltpu.VMEM(shard.shape, BF)
                    for shard in (
                        enc_qkv, enc_out, enc_up, enc_down, dec_proj, dec_qkv, dec_out, dec_up, dec_down,
                    )
                ]
                + [pltpu.SemaphoreType.DMA((9,))],
            )
        cut = enc_qkv.reshape(rows_e, 3, sections, half)
        sides = [
            jnp.stack(
                [cut[:, i, which] for i in range(3)]
                + blocks_of(part(enc_up, which, 1), half)
            )
            for which in range(2)
        ]
        return [
            jnp.where(side[0] == 1, sides[0], sides[1]),
            jnp.where(side[0] == 1, sides[1], sides[0]),
            jnp.stack(blocks_of(enc_out, half))[None],
            jnp.stack(blocks_of(enc_down, half)),
            jnp.concatenate(blocks_of(dec_qkv, thin) + [dec_out, dec_proj], axis=0),
            jnp.stack(
                blocks_of(dec_up, thin)
                + [dec_down[i : i + rows_d] for i in range(0, rows_n, rows_d)]
            ),
        ]

    plan.kernel("pack", [], pack)
    plan.send("sw", ["pack"], cube, "y", lambda: plan.pack[0])

    def columns_kernel(bit, mine, got, outs, one, two):
        for i in range(3 + ups):
            to, at = (one, i) if i < 3 else (two, i - 3)
            to[at, bit[0]] = mine[i]
            to[at, 1 - bit[0]] = got[i]
        one[3] = outs[0]

    def columns():
        mine, got, outs = plan.pack[1], plan.sw, plan.pack[2]
        if aligned:
            return call(
                columns_kernel,
                (side, mine, got, outs),
                ((4, 2, rows_e, half), BF),
                ((ups, 2, rows_e, half), BF),
                bits=1,
            )
        both = merged(mine, got, side, 1, False)
        return [jnp.concatenate([both[:3], outs], axis=0), both[3:]]

    plan.kernel("msw", ["sw"], columns)
    ways = [along(cube.z, letters) for letters in WAYS]
    backs = [along(cube.z, letters) for letters in BACK]
    parts_one = ("E1", ways[0], ["msw"], lambda: plan.msw[0], 2)
    parts_two = ("E2", ways[1], ["msw"], lambda: plan.msw[1], 2)
    parts_three = ("E3", ways[2], ["pack"], lambda: plan.pack[3], 1)
    e_one, e_two, e_three = (
        gather(plan, cube, *parts, aligned) for parts in (parts_one, parts_two, parts_three)
    )

    def w_one():
        return plan.value[e_one][0].reshape(4, wide, half)

    def w_two():
        return plan.value[e_two][0].reshape(ups, wide, half)

    def w_three():
        return plan.value[e_three][0].reshape(2, mlp, half)

    def read_whole(bit, near, far):
        if near.shape[1] % 16 != 0:
            near, far = near.astype(F32), far.astype(F32)
        first = bit[0] == 0
        both = jnp.stack([jnp.where(first, near, far), jnp.where(first, far, near)], axis=1)
        return both.reshape(-1, both.shape[-1]).astype(BF)

    def four_kernel(bit, near, far, w_p, w):
        for i in range(4):
            rows = slice(i * rows_d, (i + 1) * rows_d)
            w[i] = read_whole(bit, near[:, rows, :], far[:, rows, :])
        w_p[...] = read_whole(bit, near[:, 4 * rows_d :, :], far[:, 4 * rows_d :, :])

    def five_kernel(bit, near, far, w_u, w_d):
        count = thin // rows_n // 2
        for b in range(v_ups):
            w_u[b] = read_whole(bit, near[b], far[b])
            some = slice(b * count, (b + 1) * count)
            halves_of_b = [
                jnp.concatenate([ref[v_ups + q, some] for q in range(quarters)], axis=1)
                for ref in (near, far)
            ]
            w_d[b] = read_whole(bit, *halves_of_b)

    def joined(name, way, kernel, lead, natural, *outs):
        *_, before, step = way

        def finish():
            near = plan.value[f"{name}.m{before}"][0]
            far = plan.value[f"{name}.{step}"]
            if not aligned:
                whole = merged(near, far, core, near.ndim - 2, False)
                return natural(whole.reshape(lead + (devices,) + whole.shape[-2:]))
            shape = lead + (devices // 2,) + near.shape[-2:]
            args = (core, near.reshape(shape), far.reshape(shape))
            return call(kernel, args, *outs, bits=1)

        gather(plan, cube, name, way[:-1], ["pack"], PIECES[name], len(lead), aligned)
        plan.send(f"{name}.{step}", [f"{name}.m{before}"], cube, step, lambda: plan.value[f"{name}.m{before}"][0])
        plan.kernel(f"{name}.m{step}", [f"{name}.{step}"], finish)
        return f"{name}.m{step}"

    def four_natural(whole):
        blocks = whole[:, : 4 * rows_d].reshape(devices, 4, rows_d, thin)
        return [
            whole[:, 4 * rows_d :].reshape(wide, thin),
            blocks.transpose(1, 0, 2, 3).reshape(4, thin, thin),
        ]

    def five_natural(whole):
        return [
            whole[:v_ups].reshape(v_ups, thin, thin),
            whole[v_ups:].transpose(1, 0, 2, 3).reshape(v_ups, thin, thin),
        ]

    PIECES = {"D1": lambda: plan.pack[4], "D2": lambda: plan.pack[5]}
    square = ((v_ups, thin, thin), BF)
    d_one = joined("D1", ways[3], four_kernel, (), four_natural, ((wide, thin), BF), ((4, thin, thin), BF))
    d_two = joined("D2", ways[4], five_kernel, (v_ups + quarters,), five_natural, square, square)

    def seq_kernel(bit, rows, lead, hot, sensors, out, wide_rows):
        wide_rows[...] = rows[...].astype(F32)
        table_rows = sensors[...].astype(F32)
        class_row = lead[...].astype(F32)
        for chip in range(chips_all):
            own_at, far_at = (chip * seq_in, (chip + chips) % chips_all * seq_in)
            added = jnp.sum(hot[:, chip : chip + 1] * table_rows, axis=0, keepdims=True)
            to = chip * length

            def chosen(start, count):
                near = wide_rows[own_at + start : own_at + start + count, :]
                far = wide_rows[far_at + start : far_at + start + count, :]
                return jnp.where(bit[0] == 0, near, far) + added

            out[to : to + visible_count, :] = chosen(1, visible_count)
            out[to + visible_count : to + seq_in, :] = chosen(0, 1)
            out[to + seq_in : to + seq_in + 1, :] = class_row + added
            out[to + seq_in + 1 : to + length, :] = jnp.zeros((length - seq_in - 1, wide), F32)

    def sequence():
        hot = onehot.astype(F32).T
        args = (side, tokens, class_token[None, :], hot, sensor_table)
        scratch = [pltpu.VMEM((chips_all * seq_in, wide), F32)]
        return call(seq_kernel, args, ((every, wide), F32), bits=1, scratch=scratch)

    plan.kernel("seq", ["pack"], sequence)

    def attn_kernel(seq, gain, w, normed_out, triple_out, mixed_out, part_out, away_out):
        normed = layer_norm(seq[...], gain[...])
        normed_out[...] = normed
        for i in range(3):
            triple_out[:, i * half : (i + 1) * half] = matmul(normed, w[i]).astype(BF)
        bias = bias_of(own, length, seq_in + 1)
        triple = triple_out[...]
        mixed = jnp.concatenate(
            [attend(triple[i : i + own], half, bias) for i in range(0, every, own)], axis=0
        )
        mixed_out[...] = mixed
        for i in range(2):
            cols = slice(i * half, (i + 1) * half)
            total = matmul(mixed, w[3, i * half : (i + 1) * half])
            part_out[:, cols] = total
            away_out[:, cols] = total.astype(BF)

    plan.kernel(
        "attn",
        ["seq", e_one],
        lambda: call(
            attn_kernel,
            (plan.seq[0], gains[0], w_one()),
            ((every, wide), BF),
            ((every, 3 * half), BF),
            ((every, half), BF),
            ((every, wide), F32),
            ((every, wide), BF),
        ),
    )
    plan.send("X1", ["attn"], cube, "y", lambda: plan.attn[4])

    def whole_sum(mine, got):
        far = jnp.concatenate([got[own:], got[:own]], axis=0)
        return mine[...] + far.astype(F32)

    def norm_kernel(seq, mine, got, gain, middle_out, normed_out):
        middle = seq[...] + whole_sum(mine, got)
        middle_out[...] = middle
        normed_out[...] = layer_norm(middle, gain[...])

    plan.kernel(
        "norm",
        ["X1"],
        lambda: call(
            norm_kernel,
            (plan.seq[0], plan.attn[3], plan.X1, gains[1]),
            ((every, wide), F32),
            ((every, wide), BF),
        ),
    )

    def up_kernel(rows, w, hidden_out, slope_out):
        for i in range(ups):
            cols = slice(i * half, (i + 1) * half)
            value, slope = gelu_parts(matmul(rows[...], w[i]))
            hidden_out[:, cols] = value.astype(BF)
            slope_out[:, cols] = slope

    plan.kernel(
        "up",
        ["norm", e_two],
        lambda: call(
            up_kernel,
            (plan.norm[1], w_two()),
            ((every, mlp), BF),
            ((every, mlp), F32),
        ),
    )

    def down_kernel(rows, w, part_out, away_out):
        for i in range(2):
            cols = slice(i * half, (i + 1) * half)
            total = matmul(rows[...], w[i])
            part_out[:, cols] = total[:own]
            away_out[:, cols] = total[own:].astype(BF)

    plan.kernel(
        "down",
        ["up", e_three],
        lambda: call(
            down_kernel,
            (plan.up[0], w_three()),
            ((own, wide), F32),
            ((own, wide), BF),
        ),
    )
    plan.send("X3", ["down"], cube, "y", lambda: plan.down[1])

    def chosen_of(order_ref, chip):
        place = lax.broadcasted_iota(jnp.int32, (seq_out, visible_count), 0)
        return (place == order_ref[chip : chip + 1, :]).astype(F32)

    def dattn_kernel(
        mid, own_part, got, w_p, order_ref, mask, tab, gain, w, gain_two,
        visible_out, input_out, normed_out, triple_out, mixed_out, middle_out, normed_two_out,
    ):
        encoded = mid[:own] + own_part[...] + got[...].astype(F32)
        for chip in range(chips):
            visible = encoded[chip * length : chip * length + visible_count].astype(BF)
            visible_out[chip * visible_count : (chip + 1) * visible_count, :] = visible
        projected = matmul(visible_out[...], w_p[...])
        high = projected.astype(BF)
        low = (projected - high.astype(F32)).astype(BF)
        for chip in range(chips):
            rows = slice(chip * seq_out, (chip + 1) * seq_out)
            few = slice(chip * visible_count, (chip + 1) * visible_count)
            chosen = chosen_of(order_ref, chip)
            seen = jnp.sum(chosen, axis=1, keepdims=True)
            chosen = chosen.astype(BF)
            value = matmul(chosen, high[few]) + matmul(chosen, low[few])
            value = value + (1.0 - seen) * mask[...] + tab[...]
            input_out[rows, :] = value
            normed = layer_norm(value, gain[...])
            normed_out[rows, :] = normed
            triple_d = jnp.concatenate([matmul(normed, w[i]).astype(BF) for i in range(3)], axis=1)
            triple_out[rows, :] = triple_d
            mixed_d = attend(triple_d, thin, None)
            mixed_out[rows, :] = mixed_d
            middle_d = value + matmul(mixed_d, w[3])
            middle_out[rows, :] = middle_d
            normed_two_out[rows, :] = layer_norm(middle_d, gain_two[...])

    plan.kernel(
        "dattn",
        ["X3", d_one],
        lambda: call(
            dattn_kernel,
            (
                plan.norm[0],
                plan.down[0],
                plan.X3,
                plan.value[d_one][0],
                order,
                mask_row,
                table,
                gains[2],
                plan.value[d_one][1],
                gains[3],
            ),
            ((chips * visible_count, wide), BF),
            ((rows_all, thin), F32),
            ((rows_all, thin), BF),
            ((rows_all, 3 * thin), BF),
            ((rows_all, thin), BF),
            ((rows_all, thin), F32),
            ((rows_all, thin), BF),
        ),
    )

    def halves_of(value, bit, rows):
        cut = value.reshape(-1, 2, rows, value.shape[-1])
        other = bit[0] == 1
        near, far = cut[:, 0], cut[:, 1]
        return jnp.where(other, near, far), jnp.where(other, far, near)

    def dmlp_kernel(
        section_bit, mid, normed, w_u, w_d, grad_ref, out, away_out, back_out, hidden_out, change_out
    ):
        rows, grad = normed[...], grad_ref[...]
        total = mid[...]
        back = jnp.zeros((rows_all, thin), F32)
        for b in range(v_ups):
            value, slope_d = gelu_parts(matmul(rows, w_u[b]))
            value = value.astype(BF)
            hidden_out[b] = value
            total = total + matmul(value, w_d[b])
            change = (slope_d * against_rows(grad, w_d[b])).astype(BF)
            change_out[b] = change
            back = back + against_rows(change, w_u[b])
        other = section_bit[0] == 1
        near, far = total[:, : thin // 2].astype(BF), total[:, thin // 2 :].astype(BF)
        out[...] = jnp.where(other, far, near)
        away_out[...] = jnp.where(other, near, far)
        back_out[...] = back

    plan.kernel(
        "dmlp",
        ["dattn", d_two],
        lambda: call(
            dmlp_kernel,
            (side, plan.dattn[5], plan.dattn[6], *plan.value[d_two], grad_rows),
            ((rows_all, thin // 2), BF),
            ((rows_all, thin // 2), BF),
            ((rows_all, thin), F32),
            ((v_ups, rows_all, thin), BF),
            ((v_ups, rows_all, thin), BF),
            bits=1,
        ),
    )

    def dmlpb_kernel(bit, hidden, change, normed, grad_ref, *grads):
        rows, grad = normed[...], grad_ref[...]
        for b in range(v_ups):
            down, up = over_rows(hidden[b], grad), over_rows(rows, change[b])
            if aligned:
                for ref, value in zip(grads, halves_of(up, bit, rows_d)):
                    ref[b] = value.astype(BF)
                count = thin // rows_n // 2
                for ref, value in zip(grads, halves_of(down, bit, rows_n)):
                    for q in range(quarters):
                        ref[v_ups + q, b * count : (b + 1) * count] = value[
                            :, q * rows_d : (q + 1) * rows_d
                        ].astype(BF)
            else:
                grads[0][b], grads[0][v_ups + b] = up.astype(BF), down.astype(BF)

    def dmlpb():
        shape = (v_ups + quarters, devices // 2, rows_d, thin)
        natural = (v_ups + quarters, thin, thin)
        out = call(
            dmlpb_kernel,
            (core, plan.dmlp[3], plan.dmlp[4], plan.dattn[6], grad_rows),
            *([(shape, BF)] * 2 if aligned else [(natural, BF)]),
            bits=1,
        )
        if not aligned:
            turned = out[0][v_ups:].reshape(devices, quarters, rows_d, thin).transpose(1, 0, 2, 3)
            whole = jnp.concatenate([out[0][:v_ups].reshape(turned.shape), turned], axis=0)
            whole = whole.reshape((v_ups + quarters, devices // 2, 2, rows_d, thin))
            out = split(whole, core, 2)
        return [value.reshape((v_ups + quarters,) + lead_d + (rows_d, thin)) for value in out]

    plan.kernel("dmlpb", ["dmlp"], dmlpb)

    def five_sum_kernel(here, got, up_out, down_out):
        for i in range(v_ups):
            up_out[:, i * thin : (i + 1) * thin] = here[i].astype(F32) + got[i].astype(F32)
        for i in range(quarters):
            down_out[i * rows_d : (i + 1) * rows_d, :] = here[v_ups + i].astype(F32) + got[
                v_ups + i
            ].astype(F32)

    def five_sum(here, got):
        if aligned:
            return call(
                five_sum_kernel,
                (here, got),
                ((rows_d, v_ups * thin), F32),
                ((rows_n, thin), F32),
            )
        total = here.astype(F32) + got.astype(F32)
        return [
            jnp.concatenate([total[i] for i in range(v_ups)], axis=1),
            total[v_ups:].reshape(rows_n, thin),
        ]

    sum_five = scatter(
        plan, cube, "gD2", backs[4], ["dmlpb"], lambda: plan.dmlpb, 1, aligned, five_sum
    )

    def db1_kernel(mid, gain, back, grad_ref, w, middle_out, gain_out, mixed_out):
        change, gain_grad = norm_back(mid[...], gain[...], back[...])
        total = grad_ref[...].astype(F32) + change
        middle_out[...] = total
        gain_out[...] = gain_grad
        mixed_out[...] = against_rows(total.astype(BF), w[3]).astype(BF)

    plan.kernel(
        "db1",
        ["dmlp"],
        lambda: call(
            db1_kernel,
            (plan.dattn[5], gains[3], plan.dmlp[2], grad_rows, plan.value[d_one][1]),
            ((rows_all, thin), F32),
            ((1, thin), F32),
            ((rows_all, thin), BF),
        ),
    )

    def db2_kernel(
        triple_ref, grad_ref, w, start, gain, grad_mid, order_ref, w_p,
        triple_out, gain_out, mask_out, few_out, branch_out,
    ):
        gain_grad = jnp.zeros((1, thin), F32)
        mask_grad = jnp.zeros((1, thin), F32)
        for chip in range(chips):
            rows = slice(chip * seq_out, (chip + 1) * seq_out)
            parts = attend_back(triple_ref[rows, :], grad_ref[rows, :], thin, None)
            change = 0.0
            for i in range(3):
                triple_out[rows, i * thin : (i + 1) * thin] = parts[i]
                change = change + against_rows(parts[i], w[i])
            change, gain_part = norm_back(start[rows, :], gain[...], change)
            gain_grad = gain_grad + gain_part
            total = grad_mid[rows, :] + change
            chosen = chosen_of(order_ref, chip)
            seen = jnp.sum(chosen, axis=1, keepdims=True)
            mask_grad = mask_grad + jnp.sum((1.0 - seen) * total, axis=0, keepdims=True)
            few = over_rows(chosen.astype(BF), total.astype(BF)).astype(BF)
            few_out[chip * visible_count : (chip + 1) * visible_count, :] = few
        gain_out[...] = gain_grad
        mask_out[...] = mask_grad
        branch = against_rows(few_out[...], w_p[...])
        gap = jnp.zeros((length - visible_count, wide), F32)
        branch_out[...] = jnp.concatenate(
            [
                piece
                for chip in range(chips)
                for piece in (branch[chip * visible_count : (chip + 1) * visible_count], gap)
            ],
            axis=0,
        ).astype(BF)

    plan.kernel(
        "db2",
        ["db1"],
        lambda: call(
            db2_kernel,
            (
                plan.dattn[3],
                plan.db1[2],
                plan.value[d_one][1],
                plan.dattn[1],
                gains[2],
                plan.db1[0],
                order,
                plan.value[d_one][0],
            ),
            ((rows_all, 3 * thin), BF),
            ((1, thin), F32),
            ((1, thin), F32),
            ((chips * visible_count, thin), BF),
            ((own, wide), BF),
        ),
    )
    plan.send("Y1", ["db2"], cube, "y", lambda: plan.db2[4])

    def db3_kernel(bit, change, normed, grad_mid, mix, few, seen_rows, *grads):
        def put(value, at, rows):
            if aligned:
                for ref, side_value in zip(grads, halves_of(value, bit, rows)):
                    ref[:, at : at + rows, :] = side_value.astype(BF)
            elif rows == rows_d:
                grads[0][at // rows_d] = value.astype(BF)
            else:
                grads[1][...] = value.astype(BF)

        for i in range(3):
            put(over_rows(normed[...], change[:, i * thin : (i + 1) * thin]), i * rows_d, rows_d)
        put(over_rows(mix[...], grad_mid[...].astype(BF)), 3 * rows_d, rows_d)
        put(over_rows(seen_rows[...], few[...]), 4 * rows_d, rows_p)

    def db3():
        shape = (devices // 2, rows_four, thin)
        natural = [((4, thin, thin), BF), ((wide, thin), BF)]
        out = call(
            db3_kernel,
            (
                core,
                plan.db2[0],
                plan.dattn[2],
                plan.db1[0],
                plan.dattn[4],
                plan.db2[3],
                plan.dattn[0],
            ),
            *([(shape, BF)] * 2 if aligned else natural),
            bits=1,
        )
        if not aligned:
            blocks = out[0].reshape(4, devices, rows_d, thin).transpose(1, 0, 2, 3)
            whole = jnp.concatenate(
                [blocks.reshape(devices, -1, thin), out[1].reshape(devices, rows_p, thin)], axis=1
            )
            out = split(whole.reshape(devices // 2, 2, rows_four, thin), core, 1)
        return [value.reshape(lead_d + (rows_four, thin)) for value in out]

    plan.kernel("db3", ["db2"], db3)

    def four_sum_kernel(here, got, qkv_out, out_out, proj_out):
        total = here[...].astype(F32) + got[...].astype(F32)
        for i in range(3):
            qkv_out[:, i * thin : (i + 1) * thin] = total[i * rows_d : (i + 1) * rows_d]
        out_out[...] = total[3 * rows_d : 4 * rows_d]
        proj_out[...] = total[4 * rows_d :]

    def four_sum(here, got):
        if aligned:
            return call(
                four_sum_kernel,
                (here, got),
                ((rows_d, 3 * thin), F32),
                ((rows_d, thin), F32),
                ((rows_p, thin), F32),
            )
        total = here.astype(F32) + got.astype(F32)
        cuts = [total[i * rows_d : (i + 1) * rows_d] for i in range(4)]
        return [jnp.concatenate(cuts[:3], axis=1), cuts[3], total[4 * rows_d :]]

    sum_four = scatter(
        plan, cube, "gD1", backs[3], ["db3"], lambda: plan.db3, 0, aligned, four_sum
    )

    def emlp_kernel(near, far, w_d, slo, w_u, change_out, part_out, away_out):
        grad = jnp.concatenate([near[...], far[...]], axis=0)
        total = 0.0
        for b in range(ups):
            cols = slice(b * half, (b + 1) * half)
            change = sum(
                against_rows(grad[:, i * half : (i + 1) * half], w_d[i, cols]) for i in range(2)
            )
            change = (slo[:, cols] * change).astype(BF)
            change_out[:, cols] = change
            total = total + against_rows(change, w_u[b])
        part_out[...] = total
        away_out[...] = total.astype(BF)

    plan.kernel(
        "emlp",
        ["Y1"],
        lambda: call(
            emlp_kernel,
            (plan.db2[4], plan.Y1, w_three(), plan.up[1], w_two()),
            ((every, mlp), BF),
            ((every, wide), F32),
            ((every, wide), BF),
        ),
    )
    plan.send("Y2", ["emlp"], cube, "y", lambda: plan.emlp[2])

    def emlpg_kernel(bit, near, far, hid, rows, change, *grads):
        grad = jnp.concatenate([near[...], far[...]], axis=0)
        for i in range(2):
            value = over_rows(hid[...], grad[:, i * half : (i + 1) * half])
            if aligned:
                for ref, cut in zip(grads[:2], halves_of(value, bit, rows_m)):
                    ref[i] = cut.astype(BF)
            else:
                grads[0][i] = value.astype(BF)
        for b in range(ups):
            value = over_rows(rows[...], change[:, b * half : (b + 1) * half])
            if aligned:
                for ref, cut in zip(grads[2:], halves_of(value, bit, rows_e)):
                    ref[b] = cut.astype(BF)
            else:
                grads[1][b] = value.astype(BF)

    def emlpg():
        three, two = (2, group // 2, rows_m, half), (ups, group, rows_e, half)
        out = call(
            emlpg_kernel,
            (
                core,
                plan.db2[4],
                plan.Y1,
                plan.up[0],
                plan.norm[1],
                plan.emlp[0],
            ),
            *(
                [(three, BF)] * 2 + [(two, BF)] * 2
                if aligned
                else [((2, mlp, half), BF), ((ups, wide, half), BF)]
            ),
            bits=1,
        )
        if not aligned:
            out = split(out[0].reshape(2, group // 2, 2, rows_m, half), core, 2) + split(
                out[1].reshape(ups, group, 2, rows_e, half), core, 2
            )
        shapes = [(2,) + lead_e + (rows_m, half)] * 2 + [(ups, 2) + lead_e + (rows_e, half)] * 2
        return [value.reshape(shape) for value, shape in zip(out, shapes)]

    plan.kernel("emlpg", ["emlp"], emlpg)

    def three_kernel(here, got, out):
        for i in range(2):
            out[:, i * half : (i + 1) * half] = here[i].astype(F32) + got[i].astype(F32)

    def three_sum(here, got):
        if aligned:
            return call(three_kernel, (here, got), ((rows_m, wide), F32))
        total = here.astype(F32) + got.astype(F32)
        return [jnp.concatenate([total[i] for i in range(2)], axis=1)]

    def two_kernel(bit, here, got, here_out, away_out):
        for b in range(ups):
            for ref, which in ((here_out, bit[0]), (away_out, 1 - bit[0])):
                total = here[b, which].astype(F32) + got[b, which].astype(F32)
                ref[b] = total.astype(ref.dtype)

    def two_sum(here, got):
        if aligned:
            shape = (ups, rows_e, half)
            out = call(
                two_kernel, (side, here, got), (shape, F32), (shape, BF), bits=1
            )
            return [None] + out
        far, near = split(here.astype(F32) + got.astype(F32), side, 1)
        return [None, near, far.astype(BF)]

    sum_three = scatter(
        plan, cube, "gE3", backs[2], ["emlpg"], lambda: plan.emlpg[:2], 1, aligned, three_sum
    )
    sum_two = scatter(
        plan, cube, "gE2", backs[1], ["emlpg"], lambda: plan.emlpg[2:], 2, aligned, two_sum
    )

    def enb_kernel(mid, gain, mine, got, near, far, middle_out, gain_out, branch_out):
        hat, inverse = normal_parts(mid[...])
        grad = whole_sum(mine, got)
        scaled = grad * gain[...]
        change = inverse * (
            scaled
            - jnp.mean(scaled, axis=-1, keepdims=True)
            - hat * jnp.mean(scaled * hat, axis=-1, keepdims=True)
        )
        total = jnp.concatenate([near[...], far[...]], axis=0).astype(F32) + change
        middle_out[...] = total[:own]
        gain_out[...] = jnp.sum((grad * hat)[:own], axis=0, keepdims=True)
        branch_out[...] = total.astype(BF)

    plan.kernel(
        "enb",
        ["Y2"],
        lambda: call(
            enb_kernel,
            (plan.norm[0], gains[1], plan.emlp[1], plan.Y2, plan.db2[4], plan.Y1),
            ((own, wide), F32),
            ((1, wide), F32),
            ((every, wide), BF),
        ),
    )

    def eab_kernel(bit, grad_ref, mix, triple_ref, normed, w, part_out, away_out, *grads):
        def put(value, at):
            if aligned:
                for ref, side_value in zip(grads, halves_of(value, bit, rows_e)):
                    ref[at] = side_value.astype(BF)
            else:
                grads[0][at] = value.astype(BF)

        grad = grad_ref[...]
        put(
            jnp.concatenate(
                [over_rows(mix[...], grad[:, i * half : (i + 1) * half]) for i in range(2)], axis=0
            ),
            3,
        )
        grad_mixed = sum(
            against_rows(grad[:, i * half : (i + 1) * half], w[3, i * half : (i + 1) * half])
            for i in range(2)
        ).astype(BF)
        bias = bias_of(own, length, seq_in + 1)
        pieces = [
            attend_back(triple_ref[i : i + own, :], grad_mixed[i : i + own], half, bias)
            for i in range(0, every, own)
        ]
        total = 0.0
        for i in range(3):
            change = jnp.concatenate([piece[i] for piece in pieces], axis=0)
            put(over_rows(normed[...], change), i)
            total = total + against_rows(change, w[i])
        part_out[...] = total[:own]
        away_out[...] = total[own:].astype(BF)

    def eab():
        shape = (4, group, rows_e, half)
        out = call(
            eab_kernel,
            (
                core,
                plan.enb[2],
                plan.attn[2],
                plan.attn[1],
                plan.attn[0],
                w_one(),
            ),
            ((own, wide), F32),
            ((own, wide), BF),
            *([(shape, BF)] * 2 if aligned else [((4, wide, half), BF)]),
            bits=1,
        )
        if not aligned:
            out = out[:2] + split(out[2].reshape(4, group, 2, rows_e, half), core, 2)
        lead = (4, 2) + lead_e + (rows_e, half)
        return out[:2] + [value.reshape(lead) for value in out[2:]]

    plan.kernel("eab", ["enb"], eab)

    def one_kernel(bit, here, got, out_out, here_out, away_out):
        for i in range(2):
            out_out[:, i * half : (i + 1) * half] = here[3, i].astype(F32) + got[3, i].astype(F32)
        for i in range(3):
            for ref, which in ((here_out, bit[0]), (away_out, 1 - bit[0])):
                total = here[i, which].astype(F32) + got[i, which].astype(F32)
                ref[i] = total.astype(ref.dtype)

    def one_sum(here, got):
        if aligned:
            return call(
                one_kernel,
                (side, here, got),
                ((rows_e, wide), F32),
                ((3, rows_e, half), F32),
                ((3, rows_e, half), BF),
                bits=1,
            )
        total = here.astype(F32) + got.astype(F32)
        far, near = split(total[:3], side, 1)
        return [jnp.concatenate([total[3, i] for i in range(2)], axis=1), near, far.astype(BF)]

    sum_one = scatter(
        plan, cube, "gE1", backs[0], ["eab"], lambda: plan.eab[2:], 2, aligned, one_sum
    )
    plan.send("Y4", ["eab"], cube, "y", lambda: plan.eab[1])

    def elast_kernel(
        bit, seq, gain, own_part, got, grad_mid, hot, gain_two, mask_part, gain_three, gain_four,
        near_out, far_out, small, rows_ref,
    ):
        change, gain_grad = norm_back(seq[:own], gain[...], own_part[...] + got[...].astype(F32))
        total = grad_mid[...] + change
        for chip in range(chips):
            at = chip * length
            rows_ref[chip * seq_in : chip * seq_in + 1, :] = total[
                at + visible_count : at + visible_count + 1
            ]
            rows_ref[chip * seq_in + 1 : (chip + 1) * seq_in, :] = total[at : at + visible_count]
        near, far = rows_ref[:, :half], rows_ref[:, half:]
        near_out[...] = jnp.where(bit[0] == 1, far, near)
        far_out[...] = jnp.where(bit[0] == 1, near, far).astype(BF)
        small[...] = jnp.zeros_like(small)
        class_row = jnp.zeros((1, wide), F32)
        sensor_rows = jnp.zeros((sensor_count, wide), F32)
        for chip in range(chips):
            at = chip * length
            class_row = class_row + total[at + seq_in : at + seq_in + 1]
            rows = jnp.sum(total[at : at + length], axis=0, keepdims=True)
            sensor_rows = sensor_rows + hot[:, chip : chip + 1] * rows
        small[:sensor_count, :] = sensor_rows
        at = sensor_count
        for row in (class_row, gain_grad, gain_two[...]):
            small[at : at + 1, :] = row
            at += 1
        for row in (mask_part, gain_three, gain_four):
            small[at : at + 1, :thin] = row[...]
            at += 1

    plan.kernel(
        "elast",
        ["Y4"],
        lambda: call(
            elast_kernel,
            (
                side,
                plan.seq[0],
                gains[0],
                plan.eab[0],
                plan.Y4,
                plan.enb[0],
                onehot[:chips].astype(F32).T,
                plan.enb[1],
                plan.db2[2],
                plan.db2[1],
                plan.db1[1],
            ),
            ((chips * seq_in, half), F32),
            ((chips * seq_in, half), BF),
            ((-(-(sensor_count + 6) // 8) * 8, wide), F32),
            bits=1,
            scratch=[pltpu.VMEM((chips * seq_in, wide), F32)],
        ),
    )

    def small_kernel(own_part, got, class_out, sensor_out, *outs):
        total = own_part[...] + got[...]
        sensor_out[...] = total[:sensor_count]
        class_out[...] = total[sensor_count : sensor_count + 1]
        for i, ref in enumerate(outs):
            at = sensor_count + 1 + i
            ref[...] = total[at : at + 1, : ref.shape[1]]

    def plus_kernel(mine, got, out):
        out[...] = mine[...] + got[...]

    before = lambda: plan.elast[2]
    needs = ["elast"]
    steps = ["y", *cube.z[::-1], "x", "c"]
    for i, step in enumerate(steps):
        plan.send(f"s{i}", needs, cube, step, before)

        def finish(i=i, before=before):
            got = plan.value[f"s{i}"]
            if i < len(steps) - 1:
                return call(plus_kernel, (before(), got), (got.shape, F32))
            return call(
                small_kernel,
                (before(), got),
                ((1, wide), F32),
                ((sensor_count, wide), F32),
                ((1, wide), F32),
                ((1, wide), F32),
                ((1, thin), F32),
                ((1, thin), F32),
                ((1, thin), F32),
            )

        plan.kernel(f"sm{i}", [f"s{i}"], finish)
        before, needs = (lambda i=i: plan.value[f"sm{i}"][0]), [f"sm{i}"]
    small = needs[0]

    def beside_kernel(bit, here, got, out):
        count, _, size = here.shape
        first = bit[0] == 0
        for i in range(count):
            near, far = here[i], got[i].astype(F32)
            for j, value in enumerate((jnp.where(first, near, far), jnp.where(first, far, near))):
                at = place_of(i, j, count)
                out[:, at * size : (at + 1) * size] = value

    def place_of(i, j, count):
        return 2 * i + j if count == 3 else j * count + i

    def crossed(name, start):
        plan.send(f"{name}.w", [start], cube, "y", lambda: plan.value[start][2])

        def finish():
            here, got = plan.value[start][1], plan.value[f"{name}.w"]
            shape = (rows_e, 2 * here.shape[0] * half)
            return call(beside_kernel, (side, here, got), (shape, F32), bits=1)

        plan.kernel(f"{name}.mw", [f"{name}.w"], finish)

    crossed("gE1", sum_one)
    crossed("gE2", sum_two)

    def stacked_kernel(bit, here, got, out):
        rows = here.shape[0]
        near, far = here[...], got[...].astype(here.dtype)
        out[:rows] = jnp.where(bit[0] == 0, near, far)
        out[rows:] = jnp.where(bit[0] == 0, far, near)

    def halves(name, start):
        plan.send(name, [start], cube, "y", lambda: plan.value[start][1])

        def finish():
            here = plan.value[start][0]
            shape = (2 * here.shape[0], here.shape[1])
            got = plan.value[name]
            return call(stacked_kernel, (side, here, got), (shape, here.dtype), bits=1)

        plan.kernel(f"{name}m", [name], finish)

    halves("blk", "dmlp")
    halves("tok", "elast")
    plan.run(ORDER)

    rest = [value[0] if value.shape[0] == 1 else value for value in plan.value[small]]
    return (
        plan.blkm[0],
        plan.tokm[0],
        plan.value["gE1.mw"][0],
        plan.value[sum_one][0],
        plan.value["gE2.mw"][0],
        plan.value[sum_three][0],
        plan.value[sum_four][2],
        plan.value[sum_four][0],
        plan.value[sum_four][1],
        plan.value[sum_five][0],
        plan.value[sum_five][1],
    ) + tuple(rest)


def solution(mesh):
    every = P(("section", "dp"), None)
    rows = P("dp", None)
    in_specs = (
        rows,
        rows,
        P("dp"),
        P(),
        P(),
        P(),
        every,
        every,
        P(),
        every,
        every,
        every,
        P(),
        P(),
        every,
        every,
        P(),
        every,
        every,
        rows,
    )
    out_specs = (P("dp", "section"),) * 2 + (every,) * 9 + (P(),) * 7
    return jax.shard_map(local, mesh=mesh, in_specs=in_specs, out_specs=out_specs, check_vma=False)
```

```python
import math

import jax
import jax.numpy as jnp
from jax import lax
from jax.experimental import pallas as pl
from jax.experimental.pallas import tpu as pltpu
from jax.sharding import PartitionSpec as P

HEAD_DIM = 64
PAIR = 2 * HEAD_DIM
BF = jnp.bfloat16
F32 = jnp.float32
SCALE = HEAD_DIM ** (-0.5)


def matmul(left, right):
    return jnp.dot(left, right, preferred_element_type=F32)


def against_rows(left, right):
    return lax.dot_general(left, right, (((1,), (1,)), ((), ())), preferred_element_type=F32)


def over_rows(left, right):
    return lax.dot_general(left, right, (((0,), (0,)), ((), ())), preferred_element_type=F32)


def normal_parts(rows):
    mean = jnp.mean(rows, axis=-1, keepdims=True)
    centred = rows - mean
    spread = jnp.mean(centred * centred, axis=-1, keepdims=True)
    inverse = lax.rsqrt(spread + 1e-05)
    return centred * inverse, inverse


def layer_norm(rows, gain):
    return (normal_parts(rows)[0] * gain).astype(BF)


def norm_back(rows, gain, grad):
    hat, inverse = normal_parts(rows)
    scaled = grad * gain
    out = inverse * (
        scaled
        - jnp.mean(scaled, axis=-1, keepdims=True)
        - hat * jnp.mean(scaled * hat, axis=-1, keepdims=True)
    )
    return out, jnp.sum(grad * hat, axis=0, keepdims=True)


def gelu_parts(value):
    square = value * value
    flat = jnp.tanh(0.7978845608028654 * (value + 0.044715 * value * square))
    side = 0.5 * (1.0 + flat)
    slope = side + 0.5 * value * (1.0 - flat * flat) * (
        0.7978845608028654 + 3.0 * 0.044715 * 0.7978845608028654 * square
    )
    return value * side, slope


def position_table(count, width):
    half = width // 2
    place = jnp.arange(count, dtype=F32)[:, None]
    rate = jnp.exp(jnp.arange(half, dtype=F32) * (-math.log(10000.0) / half))
    angle = place * rate[None, :]
    return jnp.concatenate([jnp.sin(angle), jnp.cos(angle)], axis=1)


def apart(value):
    first = lax.broadcasted_iota(jnp.int32, value.shape, 1) < HEAD_DIM
    none = jnp.zeros_like(value)
    return jnp.concatenate([jnp.where(first, value, none), jnp.where(first, none, value)], axis=0)


def together(value):
    rows = value.shape[0] // 2
    first = lax.broadcasted_iota(jnp.int32, (rows, value.shape[1]), 1) < HEAD_DIM
    return jnp.where(first, value[:rows], value[rows:])


def bias_of(length, seq, valid):
    if length == valid:
        return None
    key = lax.broadcasted_iota(jnp.int32, (length, length), 0)
    query = lax.broadcasted_iota(jnp.int32, (length, length), 1)
    kept = jnp.zeros((length, length), jnp.bool_)
    for start in range(0, length, seq):
        kept = kept | (
            (key >= start) & (key < start + valid) & (query >= start) & (query < start + seq)
        )
    return jnp.where(kept, 0.0, -1e30)


def ahead(items, first, rest):
    out, now = [], first(items[0])
    for i, item in enumerate(items):
        later = first(items[i + 1]) if i + 1 < len(items) else None
        out.append(rest(item, now))
        now = later
    return out


def pairs_of(blocks, width):
    return [(block, at) for block in range(len(blocks)) for at in range(0, width, PAIR)]


def softmax_of(scores, bias):
    if bias is not None:
        scores = scores + jnp.concatenate([bias, bias], axis=1)
    raised = jnp.exp(scores - jnp.max(scores, axis=0, keepdims=True))
    return raised * (1.0 / jnp.sum(raised, axis=0, keepdims=True))


def attend(triples, width, bias):
    def part(item, i):
        block, at = item
        return triples[block][:, i * width + at : i * width + at + PAIR]

    def scores(item):
        return against_rows(part(item, 1), apart(part(item, 0)) * SCALE)

    def mixed(item, value):
        shares = softmax_of(value, bias).astype(BF)
        return together(over_rows(shares, part(item, 2))).astype(BF)

    out = ahead(pairs_of(triples, width), scores, mixed)
    count = width // PAIR
    return [
        jnp.concatenate(out[i * count : (i + 1) * count], axis=1) for i in range(len(triples))
    ]


def attend_back(triples, grads_mixed, width, bias):
    def part(item, i):
        block, at = item
        return triples[block][:, i * width + at : i * width + at + PAIR]

    def scores(item):
        queries = apart(part(item, 0)) * SCALE
        grads = apart(grads_mixed[item[0]][:, item[1] : item[1] + PAIR])
        return (
            queries,
            grads,
            against_rows(part(item, 1), queries),
            against_rows(part(item, 2), grads),
        )

    def back(item, given):
        queries, grads, value, grad_shares = given
        exact = softmax_of(value, bias)
        mean = jnp.sum(grad_shares * exact, axis=0, keepdims=True)
        grad_scores = (exact * (grad_shares - mean)).astype(BF)
        return (
            (together(over_rows(grad_scores, part(item, 1))) * SCALE).astype(BF),
            matmul(grad_scores, queries).astype(BF),
            matmul(exact.astype(BF), grads).astype(BF),
        )

    if bias is None:
        out = ahead(pairs_of(triples, width), scores, back)
    else:
        out = [back(item, scores(item)) for item in pairs_of(triples, width)]
    count = width // PAIR
    return [
        [
            jnp.concatenate([one[j] for one in out[i * count : (i + 1) * count]], axis=1)
            for j in range(3)
        ]
        for i in range(len(triples))
    ]


def call(body, args, *outs, bits=0, scratch=(), space=pltpu.VMEM):
    size = sum(math.prod(shape) * jnp.dtype(dtype).itemsize for shape, dtype in outs)
    size += sum(value.size * value.dtype.itemsize for value in args[bits:])
    count = len(args)
    earlier = [] if Plan.earlier is None else [Plan.earlier]

    def ordered(*refs):
        body(*refs[:count], *refs[count + len(earlier) :])

    run = pl.pallas_call(
        ordered,
        out_shape=[jax.ShapeDtypeStruct(shape, dtype) for shape, dtype in outs],
        in_specs=[pl.BlockSpec(memory_space=pltpu.SMEM)] * bits
        + [pl.BlockSpec(memory_space=space)] * (count - bits)
        + [pl.BlockSpec(memory_space=pl.ANY)] * len(earlier),
        cost_estimate=pl.CostEstimate(
            flops=COSTS.get(Plan.now, 10**10), bytes_accessed=1000, transcendentals=0
        ),
        compiler_params=pltpu.CompilerParams(
            vmem_limit_bytes=size + size // 4 + ((10 << 20) if size > (6 << 20) else (2 << 20))
        ),
        scratch_shapes=list(scratch),
    )
    return list(run(*args, *earlier))


def after(value, *others):
    return lax.optimization_barrier((value,) + others)[0]


def flat(value, place, split):
    rest = value.shape[place + split : -1]
    head = (math.prod(value.shape[:place]),) + (2,) * split
    return value.reshape(head + (math.prod(rest), value.shape[-1]))


def merge_kernel(bit, own, got, out):
    def step(i, _):
        out[i, bit[0]] = own[i]
        out[i, 1 - bit[0]] = got[i]
        return 0

    lax.fori_loop(0, own.shape[0], step, 0)


def merged(own, got, bit, place, aligned):
    if not aligned:
        mine = bit[0] == 0
        return jnp.where(mine, jnp.stack([own, got], place), jnp.stack([got, own], place))
    left, right = flat(own, place, False), flat(got, place, False)
    shape = left.shape[:1] + (2,) + left.shape[1:]
    (out,) = call(merge_kernel, (bit, left, right), (shape, own.dtype), bits=1)
    return out.reshape(own.shape[:place] + (2,) + own.shape[place:])


def copy_kernel(got, out):
    out[...] = got[...]


def far_kernel(bit, low, own, near_got, far_got, out):
    middle = bit[0] != low[0]

    def step(i, _):
        out[i, bit[0]] = own[i]
        out[i, 1 - bit[0]] = jnp.where(middle, near_got[i], far_got[i])
        return 0

    lax.fori_loop(0, own.shape[0], step, 0)


def add_kernel(here, got, out):
    def step(i, _):
        out[i] = here[i] + got[i]
        return 0

    lax.fori_loop(0, here.shape[0], step, 0)


def split_kernel(bit, here, got, away_out, here_out):
    def step(i, _):
        for out, side in ((away_out, 1 - bit[0]), (here_out, bit[0])):
            out[i] = here[i, side] + got[i, side]
        return 0

    lax.fori_loop(0, here.shape[0], step, 0)


def split_sum(here, got, bit, place, aligned):
    rest = here.shape[:place] + here.shape[place + 1 :]
    if not aligned:
        return split(here + got, bit, place)
    left, right = flat(here, place, True), flat(got, place, True)
    shape = left.shape[:1] + left.shape[2:]
    parts = call(
        split_kernel, (bit, left, right), (shape, BF), (shape, BF), bits=1
    )
    return [value.reshape(rest) for value in parts]


def split(total, bit, place):
    return [
        lax.dynamic_index_in_dim(total, which, place, keepdims=False)
        for which in (1 - bit[0], bit[0])
    ]


class Cube:
    def __init__(self):
        self.names = [
            (axis, bit)
            for axis in ("section", "dp")
            for bit in reversed(range((lax.axis_size(axis) - 1).bit_length()))
        ]
        self.bits = {
            (axis, bit): ((lax.axis_index(axis) >> bit) & 1).reshape(1)
            for axis, bit in self.names
        }
        depth = len(self.names) - 3
        self.of = {"c": ("dp", 0), "x": ("dp", 1), "y": ("section", 0)}
        self.of.update({f"z{i}": ("dp", 2 + i) for i in range(depth)})
        self.z = [f"z{i}" for i in range(depth)]
        self.line = {"zB": {1: 2, 2: 1}, "zC": {1: 0, 2: 3}, "zD": {0: 1, 3: 2}}

    def swap(self, value, step):
        if step in self.line:
            hops = self.line[step]
            places = [(i, i >> 2) for i in range(lax.axis_size("dp"))]
            route = [(i, i + 4 * (hops[z] - z)) for i, z in places if z in hops]
            return lax.ppermute(value, "dp", route)
        axis, bit = self.of[step]
        route = [(i, i ^ (1 << bit)) for i in range(lax.axis_size(axis))]
        return lax.ppermute(value, axis, route)

    def bit(self, step):
        return self.bits[self.of[step]]

    def place(self, held, step):
        at = self.names.index(self.of[step])
        return sum(1 for other in held if self.names.index(self.of[other]) < at)


class Plan:
    now = earlier = None

    def __init__(self):
        self.steps, self.value, self.token = {}, {}, None

    def add(self, name, needs, body):
        self.steps[name] = (needs, body)

    def hold(self, value):
        return value if self.token is None else after(value, self.token)

    def run(self, order):
        left, names = dict(self.steps), list(self.steps)
        wanted = [names[i] for i in order] if len(order) == len(names) else names
        while left:
            name = next(
                n for n in wanted if n in left and all(d in self.value for d in left[n][0])
            )
            Plan.now = names.index(name)
            with jax.named_scope(name):
                self.value[name] = left.pop(name)[1]()

    def __getattr__(self, name):
        return self.value[name]

    def kernel(self, name, needs, body):
        def step():
            Plan.earlier = self.token
            out = body()
            Plan.earlier = None
            self.token = min((v for v in out if v is not None), key=lambda value: value.size)
            return out

        self.add(name, needs, step)

    def send(self, name, needs, cube, step, value):
        self.add(name, needs, lambda: cube.swap(self.hold(value()), step))


def gather(plan, cube, name, order, needs, piece, lead, aligned):
    held = []
    before = piece
    for step in order:
        source = (lambda at: lambda: plan.value[at][0])(needs[0]) if step == "zC" else before
        plan.send(f"{name}.{step}", needs, cube, step, source)

        def finish(step=step, before=before, held=tuple(held)):
            got = plan.value[f"{name}.{step}"]
            if step == "zB":
                block = flat(got, got.ndim - 2, False)
                (out,) = call(copy_kernel, (block,), (block.shape, got.dtype))
                return [out.reshape(got.shape)]
            if step == "zC":
                own = before()
                place = lead + cube.place(held, "z1")
                cut = [
                    flat(value, place, False)
                    for value in (own, plan.value[f"{name}.mzB"][0], got)
                ]
                shape = cut[0].shape[:1] + (2,) + cut[0].shape[1:]
                bits = (cube.bit("z1"), cube.bit("z0"))
                (out,) = call(far_kernel, bits + tuple(cut), (shape, own.dtype), bits=2)
                return [out.reshape(own.shape[:place] + (2,) + own.shape[place:])]
            place = lead + cube.place(held, step)
            return [merged(before(), got, cube.bit(step), place, aligned)]

        needs = [f"{name}.m{step}"]
        plan.kernel(needs[0], [f"{name}.{step}"], finish)
        if step != "zB":
            before = (lambda at: lambda: plan.value[at][0])(needs[0])
            held.append("z1" if step == "zC" else step)
    return needs[0]


def scatter(plan, cube, name, order, needs, cut, lead, aligned, last):
    bit_of = {"zC": "z1"}
    held = [bit_of.get(step, step) for step in order if step != "zB"]
    held = sorted(held, key=lambda step: cube.names.index(cube.of[step]))
    before = cut
    for index, step in enumerate(order):
        hop = "zD" if step == "zC" else step
        plan.send(f"{name}.{step}", needs, cube, hop, lambda before=before: before()[0])
        held = [other for other in held if other != bit_of.get(step, step)]
        follow = order[index + 1] if held else None

        def finish(step=step, before=before, follow=follow, held=tuple(held)):
            got = plan.value[f"{name}.{step}"]
            if step == "zC":
                far, near = before()
                left, right = flat(far, lead, False), flat(got, lead, False)
                (out,) = call(add_kernel, (left, right), (left.shape, BF))
                return [out.reshape(far.shape), near]
            if follow is None:
                return last(before()[1], got)
            dim = bit_of.get(follow, follow)
            place = lead + cube.place(held, dim)
            return split_sum(before()[1], got, cube.bit(dim), place, aligned)

        needs = [f"{name}.a{step}"]
        plan.kernel(needs[0], [f"{name}.{step}"], finish)
        before = (lambda at: lambda: plan.value[at])(needs[0])
    return needs[0]


def blocks_of(shard, width):
    return [shard[..., i : i + width] for i in range(0, shard.shape[-1], width)]

def along(z, letters):
    ways = {"z": z, "r": z[::-1], "Z": z, "R": z[::-1]}
    if len(z) == 2:
        ways["Z"], ways["R"] = ["z0", "zB", "zC"], ["zC", "zB", "z0"]
    return [step for letter in letters for step in ways.get(letter, [letter])]


WAYS = ("Zxc", "Zxc", "xZc", "Zxyc", "Zxyc")
BACK = ("cxR", "cRx", "cxr", "cyxR", "cyxR")
ORDER = (
    0, 33, 1, 23, 45, 34, 35, 2, 3, 24, 46, 47, 13, 36, 37, 4, 25, 5, 14, 48, 49, 15, 38, 39, 6, 26, 27,
    7, 50, 51, 16, 17, 40, 41, 8, 9, 28, 29, 52, 53, 18, 19, 42, 43, 30, 31, 57, 10, 11, 44, 32, 20, 21,
    12, 58, 59, 22, 54, 55, 60, 61, 62, 63, 56, 64, 65, 79, 80, 81, 82, 66, 83, 144, 95, 67, 96, 97,
    106, 84, 98, 145, 68, 69, 107, 108, 99, 116, 117, 100, 118, 109, 110, 85, 119, 120, 101, 102, 111,
    112, 70, 71, 121, 128, 122, 86, 87, 113, 129, 130, 103, 104, 72, 146, 73, 131, 132, 123, 124, 105,
    147, 114, 88, 89, 133, 134, 74, 75, 115, 142, 125, 126, 135, 136, 90, 91, 137, 138, 76, 143, 77,
    127, 140, 92, 93, 139, 141, 78, 94,
)
COSTS = {
    0: 1000000000, 2: 22000000000, 6: 3000000000, 12: 3000000000, 14: 15000000000, 16: 1000, 24: 1000,
    32: 1000, 34: 22000000000, 36: 1000, 38: 22000000000, 48: 1000000000, 50: 15000000000, 56:
    3000000000, 60: 15000000000, 61: 1000, 62: 15000000000, 64: 1000, 65: 3000000000, 66: 1000000000,
    68: 3000000000, 76: 15000000000, 78: 1000000000, 79: 15000000000, 82: 1000000000, 84: 15000000000,
    86: 1000000000, 94: 3000000000, 101: 3000000000, 103: 3000000000, 105: 3000000000, 107: 15000000000,
    109: 22000000000, 111: 1000, 115: 1000000000, 117: 22000000000, 119: 1000000000, 121: 1000000000,
    129: 22000000000, 139: 1000, 141: 22000000000, 145: 1000,
}


def local(
    tokens,
    patch_order,
    sensor_tag,
    class_token,
    sensor_table,
    enc_gain_one,
    enc_qkv,
    enc_out,
    enc_gain_two,
    enc_up,
    enc_down,
    dec_proj,
    mask_token,
    dec_gain_one,
    dec_qkv,
    dec_out,
    dec_gain_two,
    dec_up,
    dec_down,
    out_grad,
):
    cube, plan = Cube(), Plan()
    section = lax.axis_index("section")
    sections = lax.axis_size("section")
    group = lax.axis_size("dp")
    devices = sections * group
    wide = tokens.shape[1]
    thin = out_grad.shape[1]
    half = wide // sections
    mlp = enc_up.shape[1] // sections
    ups = mlp // half
    rows_e, rows_m = enc_qkv.shape[0], enc_down.shape[0]
    rows_p, rows_d, rows_n = dec_proj.shape[0], dec_qkv.shape[0], dec_down.shape[0]
    rows_four = 4 * rows_d + rows_p
    v_ups = dec_up.shape[1] // thin
    quarters = rows_n // rows_d
    chips_all = patch_order.shape[0]
    chips = chips_all // sections
    seq_in = tokens.shape[0] // chips_all
    seq_out = patch_order.shape[1]
    visible_count = seq_in - 1
    sensor_count = sensor_table.shape[0]
    length = -(-(seq_in + 1) // 8) * 8
    own = chips * length
    every = sections * own
    rows_all = chips * seq_out
    aligned = rows_d % 16 == 0 and rows_e % 8 == 0
    side, core = cube.bit("y"), cube.bit("c")
    lead_d, lead_e = (2,) * (len(cube.names) - 1), (2,) * (len(cube.names) - 2)

    def part(value, which, axis):
        size = value.shape[axis] // sections
        return lax.dynamic_slice_in_dim(value, which * size, size, axis=axis)

    def mine_first(value):
        return jnp.concatenate([part(value, section, 0), part(value, 1 - section, 0)], axis=0)

    gains = [
        gain.astype(F32)[None, :]
        for gain in (enc_gain_one, enc_gain_two, dec_gain_one, dec_gain_two)
    ]
    order = part(patch_order, section, 0)[:, :visible_count]
    grad_rows = part(out_grad, section, 0)
    mask_row = mask_token.astype(F32)[None, :]
    tags = mine_first(sensor_tag)
    onehot = tags[:, None] == jnp.arange(sensor_count, dtype=jnp.int32)[None, :]

    def pack_kernel(bit, *refs):
        far_refs, outs, near_refs, sems = refs[:9], refs[9:15], refs[15:24], refs[24]
        copies = [
            pltpu.make_async_copy(far, near, sems.at[i])
            for i, (far, near) in enumerate(zip(far_refs, near_refs))
        ]
        for copy in copies:
            copy.start()
        for copy in copies:
            copy.wait()
        qkv, out, up, down, proj, qkv_d, out_d, up_d, down_d = near_refs
        away, mine, outs_out, three, four, five = outs
        other = bit[0] == 1
        for i in range(3 + ups):
            from_ref, at = (qkv, i * wide) if i < 3 else (up, (i - 3) * half)
            step = half if i < 3 else mlp
            near, far = (from_ref[:, at + j * step : at + j * step + half] for j in range(2))
            mine[i] = jnp.where(other, far, near)
            away[i] = jnp.where(other, near, far)
        for i in range(2):
            outs_out[0, i] = out[:, i * half : (i + 1) * half]
            three[i] = down[:, i * half : (i + 1) * half]
        for i in range(3):
            four[i * rows_d : (i + 1) * rows_d, :] = qkv_d[:, i * thin : (i + 1) * thin]
        four[3 * rows_d : 4 * rows_d, :] = out_d[...]
        four[4 * rows_d :, :] = proj[...]
        for i in range(v_ups):
            five[i] = up_d[:, i * thin : (i + 1) * thin]
        for i in range(quarters):
            five[v_ups + i] = down_d[i * rows_d : (i + 1) * rows_d, :]

    table = position_table(seq_out, thin)

    def pack():
        if aligned:
            return call(
                pack_kernel,
                (after(side, table), enc_qkv, enc_out, enc_up, enc_down, dec_proj, dec_qkv, dec_out, dec_up, dec_down),
                ((3 + ups, rows_e, half), BF),
                ((3 + ups, rows_e, half), BF),
                ((1, 2, rows_e, half), BF),
                ((2, rows_m, half), BF),
                ((rows_four, thin), BF),
                ((v_ups + quarters, rows_d, thin), BF),
                bits=1,
                space=pltpu.HBM,
                scratch=[
                    pltpu.VMEM(shard.shape, BF)
                    for shard in (
                        enc_qkv, enc_out, enc_up, enc_down, dec_proj, dec_qkv, dec_out, dec_up, dec_down,
                    )
                ]
                + [pltpu.SemaphoreType.DMA((9,))],
            )
        cut = enc_qkv.reshape(rows_e, 3, sections, half)
        sides = [
            jnp.stack(
                [cut[:, i, which] for i in range(3)]
                + blocks_of(part(enc_up, which, 1), half)
            )
            for which in range(2)
        ]
        return [
            jnp.where(side[0] == 1, sides[0], sides[1]),
            jnp.where(side[0] == 1, sides[1], sides[0]),
            jnp.stack(blocks_of(enc_out, half))[None],
            jnp.stack(blocks_of(enc_down, half)),
            jnp.concatenate(blocks_of(dec_qkv, thin) + [dec_out, dec_proj], axis=0),
            jnp.stack(
                blocks_of(dec_up, thin)
                + [dec_down[i : i + rows_d] for i in range(0, rows_n, rows_d)]
            ),
        ]

    plan.kernel("pack", [], pack)
    plan.send("sw", ["pack"], cube, "y", lambda: plan.pack[0])

    def columns_kernel(bit, mine, got, outs, one, two):
        for i in range(3 + ups):
            to, at = (one, i) if i < 3 else (two, i - 3)
            to[at, bit[0]] = mine[i]
            to[at, 1 - bit[0]] = got[i]
        one[3] = outs[0]

    def columns():
        mine, got, outs = plan.pack[1], plan.sw, plan.pack[2]
        if aligned:
            return call(
                columns_kernel,
                (side, mine, got, outs),
                ((4, 2, rows_e, half), BF),
                ((ups, 2, rows_e, half), BF),
                bits=1,
            )
        both = merged(mine, got, side, 1, False)
        return [jnp.concatenate([both[:3], outs], axis=0), both[3:]]

    plan.kernel("msw", ["sw"], columns)
    ways = [along(cube.z, letters) for letters in WAYS]
    backs = [along(cube.z, letters) for letters in BACK]
    parts_one = ("E1", ways[0], ["msw"], lambda: plan.msw[0], 2)
    parts_two = ("E2", ways[1], ["msw"], lambda: plan.msw[1], 2)
    parts_three = ("E3", ways[2], ["pack"], lambda: plan.pack[3], 1)
    e_one, e_two, e_three = (
        gather(plan, cube, *parts, aligned) for parts in (parts_one, parts_two, parts_three)
    )

    def w_one():
        return plan.value[e_one][0].reshape(4, wide, half)

    def w_two():
        return plan.value[e_two][0].reshape(ups, wide, half)

    def w_three():
        return plan.value[e_three][0].reshape(2, mlp, half)

    def read_whole(bit, near, far):
        if near.shape[1] % 16 != 0:
            near, far = near.astype(F32), far.astype(F32)
        first = bit[0] == 0
        both = jnp.stack([jnp.where(first, near, far), jnp.where(first, far, near)], axis=1)
        return both.reshape(-1, both.shape[-1]).astype(BF)

    def four_kernel(bit, near, far, w_p, w):
        for i in range(4):
            rows = slice(i * rows_d, (i + 1) * rows_d)
            w[i] = read_whole(bit, near[:, rows, :], far[:, rows, :])
        w_p[...] = read_whole(bit, near[:, 4 * rows_d :, :], far[:, 4 * rows_d :, :])

    def five_kernel(bit, near, far, w_u, w_d):
        count = thin // rows_n // 2
        for b in range(v_ups):
            w_u[b] = read_whole(bit, near[b], far[b])
            some = slice(b * count, (b + 1) * count)
            halves_of_b = [
                jnp.concatenate([ref[v_ups + q, some] for q in range(quarters)], axis=1)
                for ref in (near, far)
            ]
            w_d[b] = read_whole(bit, *halves_of_b)

    def joined(name, way, kernel, lead, natural, *outs):
        *_, before, step = way

        def finish():
            near = plan.value[f"{name}.m{before}"][0]
            far = plan.value[f"{name}.{step}"]
            if not aligned:
                whole = merged(near, far, core, near.ndim - 2, False)
                return natural(whole.reshape(lead + (devices,) + whole.shape[-2:]))
            shape = lead + (devices // 2,) + near.shape[-2:]
            args = (core, near.reshape(shape), far.reshape(shape))
            return call(kernel, args, *outs, bits=1)

        gather(plan, cube, name, way[:-1], ["pack"], PIECES[name], len(lead), aligned)
        plan.send(f"{name}.{step}", [f"{name}.m{before}"], cube, step, lambda: plan.value[f"{name}.m{before}"][0])
        plan.kernel(f"{name}.m{step}", [f"{name}.{step}"], finish)
        return f"{name}.m{step}"

    def four_natural(whole):
        blocks = whole[:, : 4 * rows_d].reshape(devices, 4, rows_d, thin)
        return [
            whole[:, 4 * rows_d :].reshape(wide, thin),
            blocks.transpose(1, 0, 2, 3).reshape(4, thin, thin),
        ]

    def five_natural(whole):
        return [
            whole[:v_ups].reshape(v_ups, thin, thin),
            whole[v_ups:].transpose(1, 0, 2, 3).reshape(v_ups, thin, thin),
        ]

    PIECES = {"D1": lambda: plan.pack[4], "D2": lambda: plan.pack[5]}
    square = ((v_ups, thin, thin), BF)
    d_one = joined("D1", ways[3], four_kernel, (), four_natural, ((wide, thin), BF), ((4, thin, thin), BF))
    d_two = joined("D2", ways[4], five_kernel, (v_ups + quarters,), five_natural, square, square)

    def seq_kernel(bit, rows, lead, hot, sensors, out, wide_rows):
        wide_rows[...] = rows[...].astype(F32)
        table_rows = sensors[...].astype(F32)
        class_row = lead[...].astype(F32)
        for chip in range(chips_all):
            own_at, far_at = (chip * seq_in, (chip + chips) % chips_all * seq_in)
            added = jnp.sum(hot[:, chip : chip + 1] * table_rows, axis=0, keepdims=True)
            to = chip * length

            def chosen(start, count):
                near = wide_rows[own_at + start : own_at + start + count, :]
                far = wide_rows[far_at + start : far_at + start + count, :]
                return jnp.where(bit[0] == 0, near, far) + added

            out[to : to + visible_count, :] = chosen(1, visible_count)
            out[to + visible_count : to + seq_in, :] = chosen(0, 1)
            out[to + seq_in : to + seq_in + 1, :] = class_row + added
            out[to + seq_in + 1 : to + length, :] = jnp.zeros((length - seq_in - 1, wide), F32)

    def sequence():
        hot = onehot.astype(F32).T
        args = (side, tokens, class_token[None, :], hot, sensor_table)
        scratch = [pltpu.VMEM((chips_all * seq_in, wide), F32)]
        return call(seq_kernel, args, ((every, wide), F32), bits=1, scratch=scratch)

    plan.kernel("seq", ["pack"], sequence)

    def attn_kernel(seq, gain, w, normed_out, triple_out, mixed_out, part_out, away_out):
        normed = layer_norm(seq[...], gain[...])
        normed_out[...] = normed
        for i in range(3):
            triple_out[:, i * half : (i + 1) * half] = matmul(normed, w[i]).astype(BF)
        bias = bias_of(own, length, seq_in + 1)
        triple = triple_out[...]
        blocks = [triple[i : i + own] for i in range(0, every, own)]
        mixed = jnp.concatenate(attend(blocks, half, bias), axis=0)
        mixed_out[...] = mixed
        for i in range(2):
            cols = slice(i * half, (i + 1) * half)
            total = matmul(mixed, w[3, i * half : (i + 1) * half])
            part_out[:, cols] = total
            away_out[:, cols] = total.astype(BF)

    plan.kernel(
        "attn",
        ["seq", e_one],
        lambda: call(
            attn_kernel,
            (plan.seq[0], gains[0], w_one()),
            ((every, wide), BF),
            ((every, 3 * half), BF),
            ((every, half), BF),
            ((every, wide), F32),
            ((every, wide), BF),
        ),
    )
    plan.send("X1", ["attn"], cube, "y", lambda: plan.attn[4])

    def whole_sum(mine, got):
        far = jnp.concatenate([got[own:], got[:own]], axis=0)
        return mine[...] + far.astype(F32)

    def norm_kernel(seq, mine, got, gain, middle_out, normed_out):
        middle = seq[...] + whole_sum(mine, got)
        middle_out[...] = middle
        normed_out[...] = layer_norm(middle, gain[...])

    plan.kernel(
        "norm",
        ["X1"],
        lambda: call(
            norm_kernel,
            (plan.seq[0], plan.attn[3], plan.X1, gains[1]),
            ((every, wide), F32),
            ((every, wide), BF),
        ),
    )

    def up_kernel(rows, w, hidden_out, slope_out):
        def rest(i, expanded):
            cols = slice(i * half, (i + 1) * half)
            value, slope = gelu_parts(expanded)
            hidden_out[:, cols] = value.astype(BF)
            slope_out[:, cols] = slope

        ahead(range(ups), lambda i: matmul(rows[...], w[i]), rest)

    plan.kernel(
        "up",
        ["norm", e_two],
        lambda: call(
            up_kernel,
            (plan.norm[1], w_two()),
            ((every, mlp), BF),
            ((every, mlp), F32),
        ),
    )

    def down_kernel(rows, w, part_out, away_out):
        for i in range(2):
            cols = slice(i * half, (i + 1) * half)
            total = matmul(rows[...], w[i])
            part_out[:, cols] = total[:own]
            away_out[:, cols] = total[own:].astype(BF)

    plan.kernel(
        "down",
        ["up", e_three],
        lambda: call(
            down_kernel,
            (plan.up[0], w_three()),
            ((own, wide), F32),
            ((own, wide), BF),
        ),
    )
    plan.send("X3", ["down"], cube, "y", lambda: plan.down[1])

    def chosen_of(order_ref, chip):
        place = lax.broadcasted_iota(jnp.int32, (seq_out, visible_count), 0)
        return (place == order_ref[chip : chip + 1, :]).astype(F32)

    def dattn_kernel(
        mid, own_part, got, w_p, order_ref, mask, tab, gain, w, gain_two,
        visible_out, input_out, normed_out, triple_out, mixed_out, middle_out, normed_two_out,
    ):
        encoded = mid[:own] + own_part[...] + got[...].astype(F32)
        for chip in range(chips):
            visible = encoded[chip * length : chip * length + visible_count].astype(BF)
            visible_out[chip * visible_count : (chip + 1) * visible_count, :] = visible
        projected = matmul(visible_out[...], w_p[...])
        high = projected.astype(BF)
        low = (projected - high.astype(F32)).astype(BF)
        for chip in range(chips):
            rows = slice(chip * seq_out, (chip + 1) * seq_out)
            few = slice(chip * visible_count, (chip + 1) * visible_count)
            chosen = chosen_of(order_ref, chip)
            seen = jnp.sum(chosen, axis=1, keepdims=True)
            chosen = chosen.astype(BF)
            value = matmul(chosen, high[few]) + matmul(chosen, low[few])
            value = value + (1.0 - seen) * mask[...] + tab[...]
            input_out[rows, :] = value
            normed = layer_norm(value, gain[...])
            normed_out[rows, :] = normed
            for i in range(3):
                triple_out[rows, i * thin : (i + 1) * thin] = matmul(normed, w[i]).astype(BF)
        every_row = [slice(chip * seq_out, (chip + 1) * seq_out) for chip in range(chips)]
        mixed_all = attend([triple_out[rows, :] for rows in every_row], thin, None)
        for rows, mixed_d in zip(every_row, mixed_all):
            mixed_out[rows, :] = mixed_d
            middle_d = input_out[rows, :] + matmul(mixed_d, w[3])
            middle_out[rows, :] = middle_d
            normed_two_out[rows, :] = layer_norm(middle_d, gain_two[...])

    plan.kernel(
        "dattn",
        ["X3", d_one],
        lambda: call(
            dattn_kernel,
            (
                plan.norm[0],
                plan.down[0],
                plan.X3,
                plan.value[d_one][0],
                order,
                mask_row,
                table,
                gains[2],
                plan.value[d_one][1],
                gains[3],
            ),
            ((chips * visible_count, wide), BF),
            ((rows_all, thin), F32),
            ((rows_all, thin), BF),
            ((rows_all, 3 * thin), BF),
            ((rows_all, thin), BF),
            ((rows_all, thin), F32),
            ((rows_all, thin), BF),
        ),
    )

    def halves_of(value, bit, rows):
        cut = value.reshape(-1, 2, rows, value.shape[-1])
        other = bit[0] == 1
        near, far = cut[:, 0], cut[:, 1]
        return jnp.where(other, near, far), jnp.where(other, far, near)

    def dmlp_kernel(
        section_bit, mid, normed, w_u, w_d, grad_ref, out, away_out, back_out, hidden_out, change_out
    ):
        rows, grad = normed[...], grad_ref[...]

        def first(b):
            return matmul(rows, w_u[b]), against_rows(grad, w_d[b])

        def rest(b, given):
            value, slope_d = gelu_parts(given[0])
            hidden_out[b] = value.astype(BF)
            change = (slope_d * given[1]).astype(BF)
            change_out[b] = change
            return matmul(hidden_out[b], w_d[b]), against_rows(change, w_u[b])

        terms = ahead(range(v_ups), first, rest)
        total = sum((term[0] for term in terms), mid[...])
        back = sum(term[1] for term in terms)
        other = section_bit[0] == 1
        near, far = total[:, : thin // 2].astype(BF), total[:, thin // 2 :].astype(BF)
        out[...] = jnp.where(other, far, near)
        away_out[...] = jnp.where(other, near, far)
        back_out[...] = back

    plan.kernel(
        "dmlp",
        ["dattn", d_two],
        lambda: call(
            dmlp_kernel,
            (side, plan.dattn[5], plan.dattn[6], *plan.value[d_two], grad_rows),
            ((rows_all, thin // 2), BF),
            ((rows_all, thin // 2), BF),
            ((rows_all, thin), F32),
            ((v_ups, rows_all, thin), BF),
            ((v_ups, rows_all, thin), BF),
            bits=1,
        ),
    )

    def dmlpb_kernel(bit, hidden, change, normed, grad_ref, *grads):
        rows, grad = normed[...], grad_ref[...]
        for b in range(v_ups):
            down, up = over_rows(hidden[b], grad), over_rows(rows, change[b])
            if aligned:
                for ref, value in zip(grads, halves_of(up, bit, rows_d)):
                    ref[b] = value.astype(BF)
                count = thin // rows_n // 2
                for ref, value in zip(grads, halves_of(down, bit, rows_n)):
                    for q in range(quarters):
                        ref[v_ups + q, b * count : (b + 1) * count] = value[
                            :, q * rows_d : (q + 1) * rows_d
                        ].astype(BF)
            else:
                grads[0][b], grads[0][v_ups + b] = up.astype(BF), down.astype(BF)

    def dmlpb():
        shape = (v_ups + quarters, devices // 2, rows_d, thin)
        natural = (v_ups + quarters, thin, thin)
        out = call(
            dmlpb_kernel,
            (core, plan.dmlp[3], plan.dmlp[4], plan.dattn[6], grad_rows),
            *([(shape, BF)] * 2 if aligned else [(natural, BF)]),
            bits=1,
        )
        if not aligned:
            turned = out[0][v_ups:].reshape(devices, quarters, rows_d, thin).transpose(1, 0, 2, 3)
            whole = jnp.concatenate([out[0][:v_ups].reshape(turned.shape), turned], axis=0)
            whole = whole.reshape((v_ups + quarters, devices // 2, 2, rows_d, thin))
            out = split(whole, core, 2)
        return [value.reshape((v_ups + quarters,) + lead_d + (rows_d, thin)) for value in out]

    plan.kernel("dmlpb", ["dmlp"], dmlpb)

    def five_sum_kernel(here, got, up_out, down_out):
        for i in range(v_ups):
            up_out[:, i * thin : (i + 1) * thin] = here[i].astype(F32) + got[i].astype(F32)
        for i in range(quarters):
            down_out[i * rows_d : (i + 1) * rows_d, :] = here[v_ups + i].astype(F32) + got[
                v_ups + i
            ].astype(F32)

    def five_sum(here, got):
        if aligned:
            return call(
                five_sum_kernel,
                (here, got),
                ((rows_d, v_ups * thin), F32),
                ((rows_n, thin), F32),
            )
        total = here.astype(F32) + got.astype(F32)
        return [
            jnp.concatenate([total[i] for i in range(v_ups)], axis=1),
            total[v_ups:].reshape(rows_n, thin),
        ]

    sum_five = scatter(
        plan, cube, "gD2", backs[4], ["dmlpb"], lambda: plan.dmlpb, 1, aligned, five_sum
    )

    def db1_kernel(mid, gain, back, grad_ref, w, middle_out, gain_out, mixed_out):
        change, gain_grad = norm_back(mid[...], gain[...], back[...])
        total = grad_ref[...].astype(F32) + change
        middle_out[...] = total
        gain_out[...] = gain_grad
        mixed_out[...] = against_rows(total.astype(BF), w[3]).astype(BF)

    plan.kernel(
        "db1",
        ["dmlp"],
        lambda: call(
            db1_kernel,
            (plan.dattn[5], gains[3], plan.dmlp[2], grad_rows, plan.value[d_one][1]),
            ((rows_all, thin), F32),
            ((1, thin), F32),
            ((rows_all, thin), BF),
        ),
    )

    def db2_kernel(
        triple_ref, grad_ref, w, start, gain, grad_mid, order_ref, w_p,
        triple_out, gain_out, mask_out, few_out, branch_out,
    ):
        gain_grad = jnp.zeros((1, thin), F32)
        mask_grad = jnp.zeros((1, thin), F32)
        every_row = [slice(chip * seq_out, (chip + 1) * seq_out) for chip in range(chips)]
        parts_all = attend_back(
            [triple_ref[rows, :] for rows in every_row],
            [grad_ref[rows, :] for rows in every_row],
            thin,
            None,
        )
        for chip, (rows, parts) in enumerate(zip(every_row, parts_all)):
            change = 0.0
            for i in range(3):
                triple_out[rows, i * thin : (i + 1) * thin] = parts[i]
                change = change + against_rows(parts[i], w[i])
            change, gain_part = norm_back(start[rows, :], gain[...], change)
            gain_grad = gain_grad + gain_part
            total = grad_mid[rows, :] + change
            chosen = chosen_of(order_ref, chip)
            seen = jnp.sum(chosen, axis=1, keepdims=True)
            mask_grad = mask_grad + jnp.sum((1.0 - seen) * total, axis=0, keepdims=True)
            few = over_rows(chosen.astype(BF), total.astype(BF)).astype(BF)
            few_out[chip * visible_count : (chip + 1) * visible_count, :] = few
        gain_out[...] = gain_grad
        mask_out[...] = mask_grad
        branch = against_rows(few_out[...], w_p[...])
        gap = jnp.zeros((length - visible_count, wide), F32)
        branch_out[...] = jnp.concatenate(
            [
                piece
                for chip in range(chips)
                for piece in (branch[chip * visible_count : (chip + 1) * visible_count], gap)
            ],
            axis=0,
        ).astype(BF)

    plan.kernel(
        "db2",
        ["db1"],
        lambda: call(
            db2_kernel,
            (
                plan.dattn[3],
                plan.db1[2],
                plan.value[d_one][1],
                plan.dattn[1],
                gains[2],
                plan.db1[0],
                order,
                plan.value[d_one][0],
            ),
            ((rows_all, 3 * thin), BF),
            ((1, thin), F32),
            ((1, thin), F32),
            ((chips * visible_count, thin), BF),
            ((own, wide), BF),
        ),
    )
    plan.send("Y1", ["db2"], cube, "y", lambda: plan.db2[4])

    def db3_kernel(bit, change, normed, grad_mid, mix, few, seen_rows, *grads):
        def put(value, at, rows):
            if aligned:
                for ref, side_value in zip(grads, halves_of(value, bit, rows)):
                    ref[:, at : at + rows, :] = side_value.astype(BF)
            elif rows == rows_d:
                grads[0][at // rows_d] = value.astype(BF)
            else:
                grads[1][...] = value.astype(BF)

        for i in range(3):
            put(over_rows(normed[...], change[:, i * thin : (i + 1) * thin]), i * rows_d, rows_d)
        put(over_rows(mix[...], grad_mid[...].astype(BF)), 3 * rows_d, rows_d)
        put(over_rows(seen_rows[...], few[...]), 4 * rows_d, rows_p)

    def db3():
        shape = (devices // 2, rows_four, thin)
        natural = [((4, thin, thin), BF), ((wide, thin), BF)]
        out = call(
            db3_kernel,
            (
                core,
                plan.db2[0],
                plan.dattn[2],
                plan.db1[0],
                plan.dattn[4],
                plan.db2[3],
                plan.dattn[0],
            ),
            *([(shape, BF)] * 2 if aligned else natural),
            bits=1,
        )
        if not aligned:
            blocks = out[0].reshape(4, devices, rows_d, thin).transpose(1, 0, 2, 3)
            whole = jnp.concatenate(
                [blocks.reshape(devices, -1, thin), out[1].reshape(devices, rows_p, thin)], axis=1
            )
            out = split(whole.reshape(devices // 2, 2, rows_four, thin), core, 1)
        return [value.reshape(lead_d + (rows_four, thin)) for value in out]

    plan.kernel("db3", ["db2"], db3)

    def four_sum_kernel(here, got, qkv_out, out_out, proj_out):
        total = here[...].astype(F32) + got[...].astype(F32)
        for i in range(3):
            qkv_out[:, i * thin : (i + 1) * thin] = total[i * rows_d : (i + 1) * rows_d]
        out_out[...] = total[3 * rows_d : 4 * rows_d]
        proj_out[...] = total[4 * rows_d :]

    def four_sum(here, got):
        if aligned:
            return call(
                four_sum_kernel,
                (here, got),
                ((rows_d, 3 * thin), F32),
                ((rows_d, thin), F32),
                ((rows_p, thin), F32),
            )
        total = here.astype(F32) + got.astype(F32)
        cuts = [total[i * rows_d : (i + 1) * rows_d] for i in range(4)]
        return [jnp.concatenate(cuts[:3], axis=1), cuts[3], total[4 * rows_d :]]

    sum_four = scatter(
        plan, cube, "gD1", backs[3], ["db3"], lambda: plan.db3, 0, aligned, four_sum
    )

    def emlp_kernel(near, far, w_d, slo, w_u, change_out, part_out, away_out):
        grad = jnp.concatenate([near[...], far[...]], axis=0)

        def first(b):
            cols = slice(b * half, (b + 1) * half)
            return sum(
                against_rows(grad[:, i * half : (i + 1) * half], w_d[i, cols]) for i in range(2)
            )

        def rest(b, given):
            cols = slice(b * half, (b + 1) * half)
            change = (slo[:, cols] * given).astype(BF)
            change_out[:, cols] = change
            return against_rows(change, w_u[b])

        total = sum(ahead(range(ups), first, rest))
        part_out[...] = total
        away_out[...] = total.astype(BF)

    plan.kernel(
        "emlp",
        ["Y1"],
        lambda: call(
            emlp_kernel,
            (plan.db2[4], plan.Y1, w_three(), plan.up[1], w_two()),
            ((every, mlp), BF),
            ((every, wide), F32),
            ((every, wide), BF),
        ),
    )
    plan.send("Y2", ["emlp"], cube, "y", lambda: plan.emlp[2])

    def emlpg_kernel(bit, near, far, hid, rows, change, *grads):
        grad = jnp.concatenate([near[...], far[...]], axis=0)
        for i in range(2):
            value = over_rows(hid[...], grad[:, i * half : (i + 1) * half])
            if aligned:
                for ref, cut in zip(grads[:2], halves_of(value, bit, rows_m)):
                    ref[i] = cut.astype(BF)
            else:
                grads[0][i] = value.astype(BF)
        for b in range(ups):
            value = over_rows(rows[...], change[:, b * half : (b + 1) * half])
            if aligned:
                for ref, cut in zip(grads[2:], halves_of(value, bit, rows_e)):
                    ref[b] = cut.astype(BF)
            else:
                grads[1][b] = value.astype(BF)

    def emlpg():
        three, two = (2, group // 2, rows_m, half), (ups, group, rows_e, half)
        out = call(
            emlpg_kernel,
            (
                core,
                plan.db2[4],
                plan.Y1,
                plan.up[0],
                plan.norm[1],
                plan.emlp[0],
            ),
            *(
                [(three, BF)] * 2 + [(two, BF)] * 2
                if aligned
                else [((2, mlp, half), BF), ((ups, wide, half), BF)]
            ),
            bits=1,
        )
        if not aligned:
            out = split(out[0].reshape(2, group // 2, 2, rows_m, half), core, 2) + split(
                out[1].reshape(ups, group, 2, rows_e, half), core, 2
            )
        shapes = [(2,) + lead_e + (rows_m, half)] * 2 + [(ups, 2) + lead_e + (rows_e, half)] * 2
        return [value.reshape(shape) for value, shape in zip(out, shapes)]

    plan.kernel("emlpg", ["emlp"], emlpg)

    def three_kernel(here, got, out):
        for i in range(2):
            out[:, i * half : (i + 1) * half] = here[i].astype(F32) + got[i].astype(F32)

    def three_sum(here, got):
        if aligned:
            return call(three_kernel, (here, got), ((rows_m, wide), F32))
        total = here.astype(F32) + got.astype(F32)
        return [jnp.concatenate([total[i] for i in range(2)], axis=1)]

    def two_kernel(bit, here, got, here_out, away_out):
        for b in range(ups):
            for ref, which in ((here_out, bit[0]), (away_out, 1 - bit[0])):
                total = here[b, which].astype(F32) + got[b, which].astype(F32)
                ref[b] = total.astype(ref.dtype)

    def two_sum(here, got):
        if aligned:
            shape = (ups, rows_e, half)
            out = call(
                two_kernel, (side, here, got), (shape, F32), (shape, BF), bits=1
            )
            return [None] + out
        far, near = split(here.astype(F32) + got.astype(F32), side, 1)
        return [None, near, far.astype(BF)]

    sum_three = scatter(
        plan, cube, "gE3", backs[2], ["emlpg"], lambda: plan.emlpg[:2], 1, aligned, three_sum
    )
    sum_two = scatter(
        plan, cube, "gE2", backs[1], ["emlpg"], lambda: plan.emlpg[2:], 2, aligned, two_sum
    )

    def enb_kernel(mid, gain, mine, got, near, far, middle_out, gain_out, branch_out):
        hat, inverse = normal_parts(mid[...])
        grad = whole_sum(mine, got)
        scaled = grad * gain[...]
        change = inverse * (
            scaled
            - jnp.mean(scaled, axis=-1, keepdims=True)
            - hat * jnp.mean(scaled * hat, axis=-1, keepdims=True)
        )
        total = jnp.concatenate([near[...], far[...]], axis=0).astype(F32) + change
        middle_out[...] = total[:own]
        gain_out[...] = jnp.sum((grad * hat)[:own], axis=0, keepdims=True)
        branch_out[...] = total.astype(BF)

    plan.kernel(
        "enb",
        ["Y2"],
        lambda: call(
            enb_kernel,
            (plan.norm[0], gains[1], plan.emlp[1], plan.Y2, plan.db2[4], plan.Y1),
            ((own, wide), F32),
            ((1, wide), F32),
            ((every, wide), BF),
        ),
    )

    def eab_kernel(bit, grad_ref, mix, triple_ref, normed, w, part_out, away_out, *grads):
        def put(value, at):
            if aligned:
                for ref, side_value in zip(grads, halves_of(value, bit, rows_e)):
                    ref[at] = side_value.astype(BF)
            else:
                grads[0][at] = value.astype(BF)

        grad = grad_ref[...]
        put(
            jnp.concatenate(
                [over_rows(mix[...], grad[:, i * half : (i + 1) * half]) for i in range(2)], axis=0
            ),
            3,
        )
        grad_mixed = sum(
            against_rows(grad[:, i * half : (i + 1) * half], w[3, i * half : (i + 1) * half])
            for i in range(2)
        ).astype(BF)
        bias = bias_of(own, length, seq_in + 1)
        starts = range(0, every, own)
        pieces = attend_back(
            [triple_ref[i : i + own, :] for i in starts],
            [grad_mixed[i : i + own] for i in starts],
            half,
            bias,
        )
        total = 0.0
        for i in range(3):
            change = jnp.concatenate([piece[i] for piece in pieces], axis=0)
            put(over_rows(normed[...], change), i)
            total = total + against_rows(change, w[i])
        part_out[...] = total[:own]
        away_out[...] = total[own:].astype(BF)

    def eab():
        shape = (4, group, rows_e, half)
        out = call(
            eab_kernel,
            (
                core,
                plan.enb[2],
                plan.attn[2],
                plan.attn[1],
                plan.attn[0],
                w_one(),
            ),
            ((own, wide), F32),
            ((own, wide), BF),
            *([(shape, BF)] * 2 if aligned else [((4, wide, half), BF)]),
            bits=1,
        )
        if not aligned:
            out = out[:2] + split(out[2].reshape(4, group, 2, rows_e, half), core, 2)
        lead = (4, 2) + lead_e + (rows_e, half)
        return out[:2] + [value.reshape(lead) for value in out[2:]]

    plan.kernel("eab", ["enb"], eab)

    def one_kernel(bit, here, got, out_out, here_out, away_out):
        for i in range(2):
            out_out[:, i * half : (i + 1) * half] = here[3, i].astype(F32) + got[3, i].astype(F32)
        for i in range(3):
            for ref, which in ((here_out, bit[0]), (away_out, 1 - bit[0])):
                total = here[i, which].astype(F32) + got[i, which].astype(F32)
                ref[i] = total.astype(ref.dtype)

    def one_sum(here, got):
        if aligned:
            return call(
                one_kernel,
                (side, here, got),
                ((rows_e, wide), F32),
                ((3, rows_e, half), F32),
                ((3, rows_e, half), BF),
                bits=1,
            )
        total = here.astype(F32) + got.astype(F32)
        far, near = split(total[:3], side, 1)
        return [jnp.concatenate([total[3, i] for i in range(2)], axis=1), near, far.astype(BF)]

    sum_one = scatter(
        plan, cube, "gE1", backs[0], ["eab"], lambda: plan.eab[2:], 2, aligned, one_sum
    )
    plan.send("Y4", ["eab"], cube, "y", lambda: plan.eab[1])

    def elast_kernel(
        bit, seq, gain, own_part, got, grad_mid, hot, gain_two, mask_part, gain_three, gain_four,
        near_out, far_out, small, rows_ref,
    ):
        change, gain_grad = norm_back(seq[:own], gain[...], own_part[...] + got[...].astype(F32))
        total = grad_mid[...] + change
        for chip in range(chips):
            at = chip * length
            rows_ref[chip * seq_in : chip * seq_in + 1, :] = total[
                at + visible_count : at + visible_count + 1
            ]
            rows_ref[chip * seq_in + 1 : (chip + 1) * seq_in, :] = total[at : at + visible_count]
        near, far = rows_ref[:, :half], rows_ref[:, half:]
        near_out[...] = jnp.where(bit[0] == 1, far, near)
        far_out[...] = jnp.where(bit[0] == 1, near, far).astype(BF)
        small[...] = jnp.zeros_like(small)
        class_row = jnp.zeros((1, wide), F32)
        sensor_rows = jnp.zeros((sensor_count, wide), F32)
        for chip in range(chips):
            at = chip * length
            class_row = class_row + total[at + seq_in : at + seq_in + 1]
            rows = jnp.sum(total[at : at + length], axis=0, keepdims=True)
            sensor_rows = sensor_rows + hot[:, chip : chip + 1] * rows
        small[:sensor_count, :] = sensor_rows
        at = sensor_count
        for row in (class_row, gain_grad, gain_two[...]):
            small[at : at + 1, :] = row
            at += 1
        for row in (mask_part, gain_three, gain_four):
            small[at : at + 1, :thin] = row[...]
            at += 1

    plan.kernel(
        "elast",
        ["Y4"],
        lambda: call(
            elast_kernel,
            (
                side,
                plan.seq[0],
                gains[0],
                plan.eab[0],
                plan.Y4,
                plan.enb[0],
                onehot[:chips].astype(F32).T,
                plan.enb[1],
                plan.db2[2],
                plan.db2[1],
                plan.db1[1],
            ),
            ((chips * seq_in, half), F32),
            ((chips * seq_in, half), BF),
            ((-(-(sensor_count + 6) // 8) * 8, wide), F32),
            bits=1,
            scratch=[pltpu.VMEM((chips * seq_in, wide), F32)],
        ),
    )

    def small_kernel(own_part, got, class_out, sensor_out, *outs):
        total = own_part[...] + got[...]
        sensor_out[...] = total[:sensor_count]
        class_out[...] = total[sensor_count]
        for i, ref in enumerate(outs):
            at = sensor_count + 1 + i
            ref[...] = total[at, : ref.shape[0]]

    def plus_kernel(mine, got, out):
        out[...] = mine[...] + got[...]

    before = lambda: plan.elast[2]
    needs = ["elast"]
    steps = ["y", *cube.z[::-1], "x", "c"]
    for i, step in enumerate(steps):
        plan.send(f"s{i}", needs, cube, step, before)

        def finish(i=i, before=before):
            got = plan.value[f"s{i}"]
            if i < len(steps) - 1:
                return call(plus_kernel, (before(), got), (got.shape, F32))
            return call(
                small_kernel,
                (before(), got),
                ((wide,), F32),
                ((sensor_count, wide), F32),
                *[((size,), F32) for size in (wide, wide, thin, thin, thin)],
            )

        plan.kernel(f"sm{i}", [f"s{i}"], finish)
        before, needs = (lambda i=i: plan.value[f"sm{i}"][0]), [f"sm{i}"]
    small = needs[0]

    def beside_kernel(bit, here, got, out):
        count, _, size = here.shape
        first = bit[0] == 0
        for i in range(count):
            near, far = here[i], got[i].astype(F32)
            for j, value in enumerate((jnp.where(first, near, far), jnp.where(first, far, near))):
                at = place_of(i, j, count)
                out[:, at * size : (at + 1) * size] = value

    def place_of(i, j, count):
        return 2 * i + j if count == 3 else j * count + i

    def crossed(name, start):
        plan.send(f"{name}.w", [start], cube, "y", lambda: plan.value[start][2])

        def finish():
            here, got = plan.value[start][1], plan.value[f"{name}.w"]
            shape = (rows_e, 2 * here.shape[0] * half)
            return call(beside_kernel, (side, here, got), (shape, F32), bits=1)

        plan.kernel(f"{name}.mw", [f"{name}.w"], finish)

    crossed("gE1", sum_one)
    crossed("gE2", sum_two)

    def stacked_kernel(bit, here, got, out):
        rows = here.shape[0]
        near, far = here[...], got[...].astype(here.dtype)
        out[:rows] = jnp.where(bit[0] == 0, near, far)
        out[rows:] = jnp.where(bit[0] == 0, far, near)

    def halves(name, start):
        plan.send(name, [start], cube, "y", lambda: plan.value[start][1])

        def finish():
            here = plan.value[start][0]
            shape = (2 * here.shape[0], here.shape[1])
            got = plan.value[name]
            return call(stacked_kernel, (side, here, got), (shape, here.dtype), bits=1)

        plan.kernel(f"{name}m", [name], finish)

    halves("blk", "dmlp")
    halves("tok", "elast")
    plan.run(ORDER)

    rest = plan.value[small]
    return (
        plan.blkm[0],
        plan.tokm[0],
        plan.value["gE1.mw"][0],
        plan.value[sum_one][0],
        plan.value["gE2.mw"][0],
        plan.value[sum_three][0],
        plan.value[sum_four][2],
        plan.value[sum_four][0],
        plan.value[sum_four][1],
        plan.value[sum_five][0],
        plan.value[sum_five][1],
    ) + tuple(rest)


def solution(mesh):
    every = P(("section", "dp"), None)
    rows = P("dp", None)
    in_specs = (
        rows,
        rows,
        P("dp"),
        P(),
        P(),
        P(),
        every,
        every,
        P(),
        every,
        every,
        every,
        P(),
        P(),
        every,
        every,
        P(),
        every,
        every,
        rows,
    )
    out_specs = (P("dp", "section"),) * 2 + (every,) * 9 + (P(),) * 7
    return jax.shard_map(local, mesh=mesh, in_specs=in_specs, out_specs=out_specs, check_vma=False)
```
